32 devices in a mesh: dp: 8 (over z, y), blk: 4 (over x, core).
Axes of the slice: x: 2, y: 2, z: 4, core: 2. Of those that a mesh axis runs over, the one named last changes fastest.
Arguments:
- tokens: float32 [16, 512, 768], P('dp', 'blk'), may hold values from -6 to 6
- segment_ids: int32 [16, 512], P('dp', 'blk'), may hold values from 0 to 7, as said below
- pad_mask: int32 [16, 512], P('dp', 'blk'), may hold values from 0 to 1, as said below
- joint_weight: bfloat16 [768, 2304], P(('dp', 'blk')), may hold values from -0.21875 to 0.21875
- joint_bias: bfloat16 [1536], P(('dp', 'blk')), may hold values from -1 to 1
- output_weight: bfloat16 [768, 768], P(('dp', 'blk')), may hold values from -3.5 to 3.5
- output_bias: bfloat16 [768], P(('dp', 'blk')), may hold values from -1.5 to 1.5
- first_gain: bfloat16 [768], P(('dp', 'blk')), may hold values from 0.099609375 to 1.8984375
- first_shift: bfloat16 [768], P(('dp', 'blk')), may hold values from -1.5 to 1.5
- up_weight: bfloat16 [768, 3072], P(('dp', 'blk')), may hold values from -0.21875 to 0.21875
- up_bias: bfloat16 [3072], P(('dp', 'blk')), may hold values from -2.5 to 2.5
- down_weight: bfloat16 [3072, 768], P(('dp', 'blk')), may hold values from -0.109375 to 0.109375
- down_bias: bfloat16 [768], P(('dp', 'blk')), may hold values from -1.5 to 1.5
- second_gain: bfloat16 [768], P(('dp', 'blk')), may hold values from 0.099609375 to 1.8984375
- second_shift: bfloat16 [768], P(('dp', 'blk')), may hold values from -1.5 to 1.5
- cotangent: float32 [16, 512, 768], P('dp', 'blk'), may hold values from -6 to 6
Outputs:
- result: float32 [16, 512, 768], P('dp', 'blk')
- grad_tokens: float32 [16, 512, 768], P('dp', 'blk')
- grad_joint_weight: float32 [768, 2304], P(('dp', 'blk'))
- grad_joint_bias: float32 [1536], P(('dp', 'blk'))
- grad_output_weight: float32 [768, 768], P(('dp', 'blk'))
- grad_output_bias: float32 [768], P(('dp', 'blk'))
- grad_first_gain: float32 [768], P(('dp', 'blk'))
- grad_first_shift: float32 [768], P(('dp', 'blk'))
- grad_up_weight: float32 [768, 3072], P(('dp', 'blk'))
- grad_up_bias: float32 [3072], P(('dp', 'blk'))
- grad_down_weight: float32 [3072, 768], P(('dp', 'blk'))
- grad_down_bias: float32 [768], P(('dp', 'blk'))
- grad_second_gain: float32 [768], P(('dp', 'blk'))
- grad_second_shift: float32 [768], P(('dp', 'blk'))
The draws below stay inside these ranges and needn't reach their ends.
Inputs may be any that keep to these rules, and one draw needn't show every extreme that they name: `segment_ids`: along each row the numbers start at 0 and never fall; every number that occurs has a slot with pad_mask 1; in each aligned group of 2 rows one row has the single number 0. `pad_mask`: in each row the zeros form one run at its end, of fewer than max(1, 51) slots, and these slots carry the number of the row's last filled slot in segment_ids.
All inputs are finite; a program needn't handle non-finite values.
Results may differ from the reference program's by a relative error of at most 0.014.
Values may be sent and summed in bfloat16 or wider, within the bound.
A program may use at most 192 MiB of HBM per device.

```python
import jax
import jax.numpy as jnp
from jax import lax

D = 768
HEADS = 12
HEAD_DIM = 64
FF = 3072
ROWS_DEV = 2
SEQ = 512
ROWS = 16


def layout(key):
    length = SEQ
    row_count = ROWS
    spacing = max(2, length // 4)
    dense_spacing = max(2, length // 16)
    starts_drawn = jax.random.randint(jax.random.fold_in(key, 11), (row_count, length), 0, spacing) == 0
    padding = jax.random.randint(jax.random.fold_in(key, 12), (row_count, 1), 0, max(1, length // 10))
    chosen = jax.random.randint(jax.random.fold_in(key, 13), (row_count // ROWS_DEV, 1), 0, ROWS_DEV)
    position = jnp.arange(length, dtype=jnp.int32)[None, :]
    row_index = jnp.arange(row_count, dtype=jnp.int32)[:, None]
    group_chosen = jnp.repeat(chosen, ROWS_DEV, axis=0)
    spanning = row_index % ROWS_DEV == group_chosen
    crowded = row_index % ROWS_DEV == (group_chosen + 1) % ROWS_DEV
    dense_starts = position % dense_spacing == 0
    filled = position < length - padding
    starts = (starts_drawn | crowded & dense_starts) & filled & (position > 0) & jnp.logical_not(spanning)
    segment = jnp.minimum(jnp.cumsum(starts.astype(jnp.int32), axis=1), 7)
    return (segment.astype(jnp.int32), filled.astype(jnp.int32))


def draw_segment_ids(key, part):
    segment, filled = layout(key)
    return segment


def draw_pad_mask(key, part):
    segment, filled = layout(key)
    return filled


def steps_of(own_key, shape, cuts, low, top_value):
    loudness = 1.0
    for axis_at, shards_of in cuts:
        heights = jax.random.uniform(jax.random.fold_in(jax.random.fold_in(own_key, 6), axis_at), (shards_of,), jnp.float32, low / len(cuts), top_value / len(cuts))
        loudness = loudness * jnp.repeat(jnp.exp(heights), shape[axis_at] // shards_of).reshape((-1,) + (1,) * (len(shape) - 1 - axis_at))
    return loudness


def centred(key, extent, deviation, limit, split=(), kind=jnp.bfloat16):
    loudness = steps_of(key, extent, split, -0.22, 0.18) if split else 1.0
    array = jax.random.normal(key, extent, jnp.float32) * deviation * loudness
    return jnp.minimum(jnp.maximum(array, -limit), limit).astype(kind)


def setup_inputs(seed: int = 0) -> dict:
    seeds = jax.random.split(jax.random.key(seed), 17)
    return {
        "tokens": centred(seeds[0], (ROWS, SEQ, D), 1.0, 6.0, ((0, 8), (1, 4)), jnp.float32),
        "segment_ids": draw_segment_ids(jax.random.fold_in(seeds[16], 71), 0),
        "pad_mask": draw_pad_mask(jax.random.fold_in(seeds[16], 71), 0),
        "joint_weight": centred(seeds[3], (D, 3 * D), D ** -0.5, 0.21875, ((0, 32),)),
        "joint_bias": centred(seeds[4], (2 * D,), 0.2, 1.0, ((0, 32),)),
        "output_weight": centred(seeds[5], (D, D), (max(1, D // 256)) ** -0.5, 3.5, ((0, 32),)),
        "output_bias": centred(seeds[6], (D,), 0.3, 1.5, ((0, 32),)),
        "first_gain": jnp.clip(1.0 + 0.18 * jax.random.normal(seeds[7], (D,), jnp.float32), 0.099609375, 1.8984375).astype(jnp.bfloat16),
        "first_shift": centred(seeds[8], (D,), 0.3, 1.5, ((0, 32),)),
        "up_weight": centred(seeds[9], (D, FF), D ** -0.5, 0.21875, ((0, 32),)),
        "up_bias": centred(seeds[10], (FF,), 0.5, 2.5, ((0, 32),)),
        "down_weight": centred(seeds[11], (FF, D), FF ** -0.5, 0.109375, ((0, 32),)),
        "down_bias": centred(seeds[12], (D,), 0.3, 1.5, ((0, 32),)),
        "second_gain": jnp.clip(1.0 + 0.18 * jax.random.normal(seeds[13], (D,), jnp.float32), 0.099609375, 1.8984375).astype(jnp.bfloat16),
        "second_shift": centred(seeds[14], (D,), 0.3, 1.5, ((0, 32),)),
        "cotangent": centred(seeds[15], (ROWS, SEQ, D), 1.0, 6.0, ((0, 8), (1, 4)), jnp.float32),
    }


@jax.custom_vjp
def low(v):
    return lax.optimization_barrier(v.astype(jnp.bfloat16)).astype(jnp.float32)

@jax.custom_vjp
def low_back(v):
    return v

def low_keep(v):
    return (low(v), None)

def low_pass(kept, grad):
    return (grad,)

def back_keep(v):
    return (v, None)

def back_low(kept, grad):
    return (low(grad),)
low.defvjp(low_keep, low_pass)
low_back.defvjp(back_keep, back_low)
epsilon = 1e-05
masked_score = -1e+30
highest = lax.Precision.HIGHEST

def norm_rows(values_in, gain, shift):
    centered = values_in - lax.optimization_barrier(jnp.mean(values_in, axis=-1, keepdims=True))
    variance = lax.optimization_barrier(jnp.mean(centered * centered, axis=-1, keepdims=True))
    return centered * lax.rsqrt(variance + epsilon) * gain + shift

def layer_row(row_tokens, segment, present, weights):
    joint_weight, joint_bias, output_weight, output_bias, first_gain, first_shift, up_weight, up_bias, down_weight, down_bias, second_gain, second_shift = weights
    length = row_tokens.shape[0]
    features = row_tokens.shape[1]
    normed_one = low(norm_rows(row_tokens, first_gain, first_shift))
    joint = jnp.dot(normed_one, joint_weight, precision=highest)
    query = low(low_back(joint[:, :features] + joint_bias[:features]))
    keys = low(low_back(joint[:, features:2 * features]))
    values = low(low_back(joint[:, 2 * features:] + joint_bias[features:]))
    query_heads = query.reshape(length, HEADS, HEAD_DIM)
    key_heads = keys.reshape(length, HEADS, HEAD_DIM)
    value_heads = values.reshape(length, HEADS, HEAD_DIM)
    scores = low_back(jnp.einsum('qhd,khd->hqk', query_heads, key_heads, precision=highest) * HEAD_DIM ** (-0.5))
    allowed = (segment[:, None] == segment[None, :]) & (present[None, :] == 1)
    scores = jnp.where(allowed[None], scores, masked_score)
    largest = lax.optimization_barrier(jnp.max(scores, axis=-1, keepdims=True))
    expos = jnp.exp(scores - largest)
    probs = low(expos / lax.optimization_barrier(jnp.sum(expos, axis=-1, keepdims=True)))
    attended = jnp.einsum('hqk,khd->qhd', probs, value_heads, precision=highest).reshape(length, features)
    attended = low(low_back(attended))
    middle = row_tokens + low_back(jnp.dot(attended, output_weight, precision=highest) + output_bias)
    normed_two = low(norm_rows(middle, second_gain, second_shift))
    hidden = low_back(jnp.dot(normed_two, up_weight, precision=highest) + up_bias)
    activated = low(jax.nn.gelu(hidden, approximate=True))
    return middle + low_back(jnp.dot(activated, down_weight, precision=highest) + down_bias)

def reference(tokens, segment_ids, pad_mask, joint_weight, joint_bias, output_weight, output_bias, first_gain, first_shift, up_weight, up_bias, down_weight, down_bias, second_gain, second_shift, cotangent):
    params = tuple((entry.astype(jnp.float32) for entry in (joint_weight, joint_bias, output_weight, output_bias, first_gain, first_shift, up_weight, up_bias, down_weight, down_bias, second_gain, second_shift)))

    def forward(layer_input, weights):
        per_row = jax.checkpoint(lambda row_tokens, segment, present: layer_row(row_tokens, segment, present, weights))
        return lax.map(lambda entries: per_row(entries[0], entries[1], entries[2]), (layer_input, segment_ids, pad_mask))
    result, pullback = jax.vjp(forward, tokens, params)
    grad_tokens, grads = pullback(cotangent)
    grad_joint_weight, grad_joint_bias, grad_output_weight, grad_output_bias, grad_first_gain, grad_first_shift, grad_up_weight, grad_up_bias, grad_down_weight, grad_down_bias, grad_second_gain, grad_second_shift = grads
    return (result, grad_tokens, grad_joint_weight, grad_joint_bias, grad_output_weight, grad_output_bias, grad_first_gain, grad_first_shift, grad_up_weight, grad_up_bias, grad_down_weight, grad_down_bias, grad_second_gain, grad_second_shift)
```

```python
import jax
import jax.numpy as jnp
from jax import lax
from jax.sharding import PartitionSpec as P

HEADS = 12


epsilon = 1e-05
masked_score = -1e30


def normalize(values_in, gain, shift):
    centered = values_in - jnp.mean(values_in, axis=-1, keepdims=True)
    inverse = lax.rsqrt(jnp.mean(centered * centered, axis=-1, keepdims=True) + epsilon)
    unit_rows = centered * inverse
    return (unit_rows * gain + shift, unit_rows, inverse)


def normalize_back(grad_normed, unit_rows, inverse, gain):
    scaled = grad_normed * gain
    grad_input = inverse * (
        scaled
        - jnp.mean(scaled, axis=-1, keepdims=True)
        - unit_rows * jnp.mean(scaled * unit_rows, axis=-1, keepdims=True)
    )
    return (
        grad_input,
        jnp.sum(grad_normed * unit_rows, axis=(0, 1)),
        jnp.sum(grad_normed, axis=(0, 1)),
    )


def project(activation, weight):
    return jnp.einsum("rcd,dn->rcn", activation, weight, preferred_element_type=jnp.float32)


def project_back(gradient, weight):
    return jnp.einsum("rcn,dn->rcd", gradient, weight, preferred_element_type=jnp.float32)


def outer_sum(activation, gradient):
    return jnp.einsum("rcd,rcn->dn", activation, gradient, preferred_element_type=jnp.float32)


def split_heads(matrix, head_count):
    return matrix.reshape(
        matrix.shape[0], matrix.shape[1], head_count, matrix.shape[2] // head_count
    )


def masked_scores(query_heads, key_heads, query_segment, key_segment, scaling):
    raw_scores = (
        jnp.einsum("rqhd,rkhd->rhqk", query_heads, key_heads, preferred_element_type=jnp.float32)
        * scaling
    )
    allowed = (query_segment[:, :, None] == key_segment[:, None, :])[:, None]
    return (jnp.where(allowed, raw_scores, masked_score), allowed)


def column_sums(gradient):
    return jnp.sum(gradient.astype(jnp.float32), axis=(0, 1))


def scatter_sum(gradient):
    summed = lax.psum_scatter(
        gradient.astype(jnp.bfloat16), ("dp", "blk"), scatter_dimension=0, tiled=True
    )
    return summed.astype(jnp.float32)


def per_device(
    tokens,
    segment_ids,
    pad_mask,
    joint_weight,
    joint_bias,
    output_weight,
    output_bias,
    first_gain,
    first_shift,
    up_weight,
    up_bias,
    down_weight,
    down_bias,
    second_gain,
    second_shift,
    cotangent,
):
    batch_rows, local_len, features = tokens.shape
    head_count = HEADS
    head_size = features // head_count
    scaling = head_size ** (-0.5)
    device_count = lax.axis_size("dp") * lax.axis_size("blk")
    small_parts = (
        joint_bias, output_bias, first_gain, first_shift, up_bias, down_bias, second_gain, second_shift
    )
    small_all = lax.all_gather(jnp.concatenate(small_parts), ("dp", "blk"), axis=0, tiled=True)
    small_all = small_all.reshape(device_count, -1)
    small_full = []
    small_at = 0
    for part in small_parts:
        small_full.append(small_all[:, small_at : small_at + part.shape[0]].reshape(-1))
        small_at += part.shape[0]
    full_joint_bias, full_output_bias, gain_one, shift_one = small_full[:4]
    full_up_bias, full_down_bias, gain_two, shift_two = small_full[4:]
    full_joint = lax.all_gather(joint_weight, ("dp", "blk"), axis=0, tiled=True)
    full_output = lax.all_gather(output_weight, ("dp", "blk"), axis=0, tiled=True)
    normed_one, unit_one, inverse_one = normalize(
        tokens, gain_one.astype(jnp.float32), shift_one.astype(jnp.float32)
    )
    normed_one_low = normed_one.astype(jnp.bfloat16)
    joint = project(normed_one_low, full_joint)
    bias_values = full_joint_bias.astype(jnp.float32)
    query = (joint[..., :features] + bias_values[:features]).astype(jnp.bfloat16)
    keys = joint[..., features : 2 * features].astype(jnp.bfloat16)
    values = (joint[..., 2 * features :] + bias_values[features:]).astype(jnp.bfloat16)
    key_segment = jnp.where(pad_mask == 1, segment_ids, -1)
    query_heads = split_heads(query, head_count)
    top_score = jnp.full((batch_rows, head_count, local_len), masked_score, jnp.float32)
    key_portion = lax.all_gather(keys, "blk", axis=1, tiled=True)
    value_portion = lax.all_gather(values, "blk", axis=1, tiled=True)
    segment_portion = lax.all_gather(key_segment, "blk", axis=1, tiled=True)
    scores, allowed = masked_scores(
        query_heads, split_heads(key_portion, head_count), segment_ids, segment_portion, scaling
    )
    new_top = jnp.maximum(top_score, jnp.max(scores, axis=-1))
    weights = jnp.where(allowed, jnp.exp(scores - new_top[..., None]), 0.0)
    total_weight = jnp.sum(weights, axis=-1)
    weighted = jnp.einsum(
        "rhqk,rkhd->rhqd",
        weights.astype(jnp.bfloat16),
        split_heads(value_portion, head_count),
        preferred_element_type=jnp.float32,
    )
    top_score, total_weight, weighted = (new_top, total_weight, weighted)
    log_total = top_score + jnp.log(total_weight)
    attended_heads = weighted / total_weight[..., None]
    attended = jnp.transpose(attended_heads, (0, 2, 1, 3)).reshape(batch_rows, local_len, features)
    attended_low = attended.astype(jnp.bfloat16)
    middle = tokens + project(attended_low, full_output) + full_output_bias.astype(jnp.float32)
    full_up = lax.all_gather(up_weight, ("dp", "blk"), axis=0, tiled=True)
    full_down = lax.all_gather(down_weight, ("dp", "blk"), axis=0, tiled=True)
    normed_two, unit_two, inverse_two = normalize(
        middle, gain_two.astype(jnp.float32), shift_two.astype(jnp.float32)
    )
    normed_two_low = normed_two.astype(jnp.bfloat16)
    hidden = project(normed_two_low, full_up) + full_up_bias.astype(jnp.float32)
    activated, gelu_pullback = jax.vjp(jax.nn.gelu, hidden)
    activated_low = activated.astype(jnp.bfloat16)
    result = middle + project(activated_low, full_down) + full_down_bias.astype(jnp.float32)
    later_up, later_down, later_gain_two = full_up, full_down, gain_two
    grad_result = cotangent.astype(jnp.bfloat16)
    grad_down_weight = outer_sum(activated_low, grad_result)
    grad_down_bias = column_sums(grad_result)
    grad_activated = project_back(grad_result, later_down)
    grad_hidden = gelu_pullback(grad_activated)[0].astype(jnp.bfloat16)
    grad_up_bias = column_sums(grad_hidden)
    grad_up_weight = outer_sum(normed_two_low, grad_hidden)
    grad_normed_two = project_back(grad_hidden, later_up)
    grad_from_second, grad_gain_two, grad_shift_two = normalize_back(
        grad_normed_two, unit_two, inverse_two, later_gain_two.astype(jnp.float32)
    )
    grad_middle = cotangent + grad_from_second
    grad_up_shard = scatter_sum(grad_up_weight)
    grad_down_shard = scatter_sum(grad_down_weight)
    later_joint, later_output, later_gain_one = full_joint, full_output, gain_one
    grad_branch = grad_middle.astype(jnp.bfloat16)
    grad_output_weight = outer_sum(attended_low, grad_branch)
    grad_output_bias = column_sums(grad_branch)
    grad_attended = project_back(grad_branch, later_output).astype(jnp.bfloat16)
    grad_heads = split_heads(grad_attended, head_count)
    delta = jnp.einsum("rqhd,rhqd->rhq", grad_heads.astype(jnp.float32), attended_heads)
    key_heads = split_heads(key_portion, head_count)
    scores, allowed = masked_scores(query_heads, key_heads, segment_ids, segment_portion, scaling)
    probs = jnp.where(allowed, jnp.exp(scores - log_total[..., None]), 0.0)
    grad_probs = jnp.einsum(
        "rqhd,rkhd->rhqk",
        grad_heads,
        split_heads(value_portion, head_count),
        preferred_element_type=jnp.float32,
    )
    grad_scores = (probs * (grad_probs - delta[..., None])).astype(jnp.bfloat16)
    grad_query = scaling * jnp.einsum(
        "rhqk,rkhd->rqhd", grad_scores, key_heads, preferred_element_type=jnp.float32
    )
    every_total, every_delta = (
        lax.all_gather(log_total, "blk", axis=2, tiled=True),
        lax.all_gather(delta, "blk", axis=2, tiled=True),
    )
    own_keys = split_heads(keys, head_count)
    own_values = split_heads(values, head_count)
    query_portion = lax.all_gather(query, "blk", axis=1, tiled=True)
    grad_portion = lax.all_gather(grad_attended, "blk", axis=1, tiled=True)
    segment_portion = lax.all_gather(segment_ids, "blk", axis=1, tiled=True)
    portion_queries = split_heads(query_portion, head_count)
    portion_grads = split_heads(grad_portion, head_count)
    scores, allowed = masked_scores(
        portion_queries, own_keys, segment_portion, key_segment, scaling
    )
    probs = jnp.where(allowed, jnp.exp(scores - every_total[..., None]), 0.0)
    grad_values = jnp.einsum(
        "rhqk,rqhd->rkhd",
        probs.astype(jnp.bfloat16),
        portion_grads,
        preferred_element_type=jnp.float32,
    )
    grad_probs = jnp.einsum(
        "rqhd,rkhd->rhqk", portion_grads, own_values, preferred_element_type=jnp.float32
    )
    grad_scores = (probs * (grad_probs - every_delta[..., None])).astype(jnp.bfloat16)
    grad_keys = scaling * jnp.einsum(
        "rhqk,rqhd->rkhd", grad_scores, portion_queries, preferred_element_type=jnp.float32
    )
    grad_keys, grad_values = (grad_keys, grad_values)
    grad_joint = jnp.concatenate(
        [
            grad_query.reshape(batch_rows, local_len, features),
            grad_keys.reshape(batch_rows, local_len, features),
            grad_values.reshape(batch_rows, local_len, features),
        ],
        axis=-1,
    ).astype(jnp.bfloat16)
    grad_joint_weight = outer_sum(normed_one_low, grad_joint)
    grad_joint_bias = jnp.concatenate(
        [column_sums(grad_joint[..., :features]), column_sums(grad_joint[..., 2 * features :])]
    )
    grad_normed_one = project_back(grad_joint, later_joint)
    grad_from_first, grad_gain_one, grad_shift_one = normalize_back(
        grad_normed_one, unit_one, inverse_one, later_gain_one.astype(jnp.float32)
    )
    grad_tokens = grad_middle + grad_from_first
    small_grads = (
        grad_joint_bias, grad_output_bias, grad_gain_one, grad_shift_one,
        grad_up_bias, grad_down_bias, grad_gain_two, grad_shift_two,
    )
    packed = jnp.concatenate([part.reshape(device_count, -1) for part in small_grads], axis=1)
    own = lax.psum_scatter(packed, ("dp", "blk"), scatter_dimension=0, tiled=True)[0]
    small_shards = []
    small_at = 0
    for part in small_parts:
        small_shards.append(own[small_at : small_at + part.shape[0]])
        small_at += part.shape[0]
    return (
        result,
        grad_tokens,
        scatter_sum(grad_joint_weight),
        small_shards[0],
        scatter_sum(grad_output_weight),
        small_shards[1],
        small_shards[2],
        small_shards[3],
        grad_up_shard,
        small_shards[4],
        grad_down_shard,
        small_shards[5],
        small_shards[6],
        small_shards[7],
    )


def solution(mesh):
    placed = (
        P("dp", "blk", None),
        P("dp", "blk"),
        P("dp", "blk"),
        P(("dp", "blk"), None),
        P(("dp", "blk")),
        P(("dp", "blk"), None),
        P(("dp", "blk")),
        P(("dp", "blk")),
        P(("dp", "blk")),
        P(("dp", "blk"), None),
        P(("dp", "blk")),
        P(("dp", "blk"), None),
        P(("dp", "blk")),
        P(("dp", "blk")),
        P(("dp", "blk")),
        P("dp", "blk", None),
    )
    return jax.shard_map(
        per_device,
        mesh=mesh,
        in_specs=placed,
        out_specs=(
            P("dp", "blk", None),
            P("dp", "blk", None),
            P(("dp", "blk"), None),
            P(("dp", "blk")),
            P(("dp", "blk"), None),
            P(("dp", "blk")),
            P(("dp", "blk")),
            P(("dp", "blk")),
            P(("dp", "blk"), None),
            P(("dp", "blk")),
            P(("dp", "blk"), None),
            P(("dp", "blk")),
            P(("dp", "blk")),
            P(("dp", "blk")),
        ),
        check_vma=False,
    )
```

```python
import jax
import jax.numpy as jnp
from jax import lax
from jax.experimental import pallas as pl
from jax.experimental.pallas import tpu as pltpu
from jax.sharding import PartitionSpec as P

HEADS = 12
COPIES = 256


epsilon = 1e-05
masked_score = -1e30


def normalize(values_in, gain, shift):
    centered = values_in - jnp.mean(values_in, axis=-1, keepdims=True)
    inverse = lax.rsqrt(jnp.mean(centered * centered, axis=-1, keepdims=True) + epsilon)
    unit_rows = centered * inverse
    return (unit_rows * gain + shift, unit_rows, inverse)


def normalize_back(grad_normed, unit_rows, inverse, gain):
    scaled = grad_normed * gain
    grad_input = inverse * (
        scaled
        - jnp.mean(scaled, axis=-1, keepdims=True)
        - unit_rows * jnp.mean(scaled * unit_rows, axis=-1, keepdims=True)
    )
    return (
        grad_input,
        jnp.sum(grad_normed * unit_rows, axis=(0, 1)),
        jnp.sum(grad_normed, axis=(0, 1)),
    )


def project(activation, weight):
    return jnp.einsum("rcd,dn->rcn", activation, weight, preferred_element_type=jnp.float32)


def project_back(gradient, weight):
    return jnp.einsum("rcn,dn->rcd", gradient, weight, preferred_element_type=jnp.float32)


def outer_sum(activation, gradient):
    return jnp.einsum("rcd,rcn->dn", activation, gradient, preferred_element_type=jnp.float32)


def split_heads(matrix, head_count):
    return matrix.reshape(
        matrix.shape[0], matrix.shape[1], head_count, matrix.shape[2] // head_count
    )


def masked_scores(query_heads, key_heads, query_segment, key_segment, scaling):
    raw_scores = (
        jnp.einsum("rqhd,rkhd->rhqk", query_heads, key_heads, preferred_element_type=jnp.float32)
        * scaling
    )
    allowed = (query_segment[:, :, None] == key_segment[:, None, :])[:, None]
    return (jnp.where(allowed, raw_scores, masked_score), allowed)


def column_sums(gradient):
    return jnp.sum(gradient.astype(jnp.float32), axis=(0, 1))


def scatter_sum(gradient):
    summed = lax.psum_scatter(
        gradient.astype(jnp.bfloat16), ("dp", "blk"), scatter_dimension=0, tiled=True
    )
    return summed.astype(jnp.float32)


def per_device(
    tokens,
    segment_ids,
    pad_mask,
    joint_weight,
    joint_bias,
    output_weight,
    output_bias,
    first_gain,
    first_shift,
    up_weight,
    up_bias,
    down_weight,
    down_bias,
    second_gain,
    second_shift,
    cotangent,
):
    batch_rows, local_len, features = tokens.shape
    head_count = HEADS
    head_size = features // head_count
    scaling = head_size ** (-0.5)
    device_count = lax.axis_size("dp") * lax.axis_size("blk")
    small_parts = (
        joint_bias, output_bias, first_gain, first_shift, up_bias, down_bias, second_gain, second_shift
    )
    small_all = lax.all_gather(jnp.concatenate(small_parts), ("dp", "blk"), axis=0, tiled=True)
    small_all = small_all.reshape(device_count, -1)
    small_full = []
    small_at = 0
    for part in small_parts:
        small_full.append(small_all[:, small_at : small_at + part.shape[0]].reshape(-1))
        small_at += part.shape[0]
    full_joint_bias, full_output_bias, gain_one, shift_one = small_full[:4]
    full_up_bias, full_down_bias, gain_two, shift_two = small_full[4:]
    full_joint = lax.all_gather(joint_weight, ("dp", "blk"), axis=0, tiled=True)
    full_output = lax.all_gather(output_weight, ("dp", "blk"), axis=0, tiled=True)
    normed_one, unit_one, inverse_one = normalize(
        tokens, gain_one.astype(jnp.float32), shift_one.astype(jnp.float32)
    )
    normed_one_low = normed_one.astype(jnp.bfloat16)
    joint = project(normed_one_low, full_joint)
    bias_values = full_joint_bias.astype(jnp.float32)
    query = (joint[..., :features] + bias_values[:features]).astype(jnp.bfloat16)
    keys = joint[..., features : 2 * features].astype(jnp.bfloat16)
    values = (joint[..., 2 * features :] + bias_values[features:]).astype(jnp.bfloat16)
    key_segment = jnp.where(pad_mask == 1, segment_ids, -1)
    query_heads = split_heads(query, head_count)
    top_score = jnp.full((batch_rows, head_count, local_len), masked_score, jnp.float32)
    key_portion = lax.all_gather(keys, "blk", axis=1, tiled=True)
    value_portion = lax.all_gather(values, "blk", axis=1, tiled=True)
    segment_portion = lax.all_gather(key_segment, "blk", axis=1, tiled=True)
    scores, allowed = masked_scores(
        query_heads, split_heads(key_portion, head_count), segment_ids, segment_portion, scaling
    )
    new_top = jnp.maximum(top_score, jnp.max(scores, axis=-1))
    weights = jnp.where(allowed, jnp.exp(scores - new_top[..., None]), 0.0)
    total_weight = jnp.sum(weights, axis=-1)
    weighted = jnp.einsum(
        "rhqk,rkhd->rhqd",
        weights.astype(jnp.bfloat16),
        split_heads(value_portion, head_count),
        preferred_element_type=jnp.float32,
    )
    top_score, total_weight, weighted = (new_top, total_weight, weighted)
    log_total = top_score + jnp.log(total_weight)
    attended_heads = weighted / total_weight[..., None]
    attended = jnp.transpose(attended_heads, (0, 2, 1, 3)).reshape(batch_rows, local_len, features)
    attended_low = attended.astype(jnp.bfloat16)
    middle = tokens + project(attended_low, full_output) + full_output_bias.astype(jnp.float32)
    full_up = lax.all_gather(up_weight, ("dp", "blk"), axis=0, tiled=True)
    full_down = lax.all_gather(down_weight, ("dp", "blk"), axis=0, tiled=True)
    normed_two, unit_two, inverse_two = normalize(
        middle, gain_two.astype(jnp.float32), shift_two.astype(jnp.float32)
    )
    normed_two_low = normed_two.astype(jnp.bfloat16)
    hidden = project(normed_two_low, full_up) + full_up_bias.astype(jnp.float32)
    activated, gelu_pullback = jax.vjp(jax.nn.gelu, hidden)
    activated_low = activated.astype(jnp.bfloat16)
    result = middle + project(activated_low, full_down) + full_down_bias.astype(jnp.float32)
    later_up, later_down, later_gain_two = full_up, full_down, gain_two
    grad_result = cotangent.astype(jnp.bfloat16)
    grad_down_weight = outer_sum(activated_low, grad_result)
    grad_down_bias = column_sums(grad_result)
    grad_activated = project_back(grad_result, later_down)
    grad_hidden = gelu_pullback(grad_activated)[0].astype(jnp.bfloat16)
    grad_up_bias = column_sums(grad_hidden)
    grad_up_weight = outer_sum(normed_two_low, grad_hidden)
    grad_normed_two = project_back(grad_hidden, later_up)
    grad_from_second, grad_gain_two, grad_shift_two = normalize_back(
        grad_normed_two, unit_two, inverse_two, later_gain_two.astype(jnp.float32)
    )
    grad_middle = cotangent + grad_from_second
    grad_up_shard = scatter_sum(grad_up_weight)
    grad_down_shard = scatter_sum(grad_down_weight)
    later_joint, later_output, later_gain_one = full_joint, full_output, gain_one
    grad_branch = grad_middle.astype(jnp.bfloat16)
    grad_output_weight = outer_sum(attended_low, grad_branch)
    grad_output_bias = column_sums(grad_branch)
    grad_attended = project_back(grad_branch, later_output).astype(jnp.bfloat16)
    grad_heads = split_heads(grad_attended, head_count)
    delta = jnp.einsum("rqhd,rhqd->rhq", grad_heads.astype(jnp.float32), attended_heads)
    key_heads = split_heads(key_portion, head_count)
    scores, allowed = masked_scores(query_heads, key_heads, segment_ids, segment_portion, scaling)
    probs = jnp.where(allowed, jnp.exp(scores - log_total[..., None]), 0.0)
    grad_probs = jnp.einsum(
        "rqhd,rkhd->rhqk",
        grad_heads,
        split_heads(value_portion, head_count),
        preferred_element_type=jnp.float32,
    )
    grad_scores = (probs * (grad_probs - delta[..., None])).astype(jnp.bfloat16)
    grad_query = scaling * jnp.einsum(
        "rhqk,rkhd->rqhd", grad_scores, key_heads, preferred_element_type=jnp.float32
    )
    every_total, every_delta = (
        lax.all_gather(log_total, "blk", axis=2, tiled=True),
        lax.all_gather(delta, "blk", axis=2, tiled=True),
    )
    own_keys = split_heads(keys, head_count)
    own_values = split_heads(values, head_count)
    query_portion = lax.all_gather(query, "blk", axis=1, tiled=True)
    grad_portion = lax.all_gather(grad_attended, "blk", axis=1, tiled=True)
    segment_portion = lax.all_gather(segment_ids, "blk", axis=1, tiled=True)
    portion_queries = split_heads(query_portion, head_count)
    portion_grads = split_heads(grad_portion, head_count)
    scores, allowed = masked_scores(
        portion_queries, own_keys, segment_portion, key_segment, scaling
    )
    probs = jnp.where(allowed, jnp.exp(scores - every_total[..., None]), 0.0)
    grad_values = jnp.einsum(
        "rhqk,rqhd->rkhd",
        probs.astype(jnp.bfloat16),
        portion_grads,
        preferred_element_type=jnp.float32,
    )
    grad_probs = jnp.einsum(
        "rqhd,rkhd->rhqk", portion_grads, own_values, preferred_element_type=jnp.float32
    )
    grad_scores = (probs * (grad_probs - every_delta[..., None])).astype(jnp.bfloat16)
    grad_keys = scaling * jnp.einsum(
        "rhqk,rqhd->rkhd", grad_scores, portion_queries, preferred_element_type=jnp.float32
    )
    grad_keys, grad_values = (grad_keys, grad_values)
    grad_joint = jnp.concatenate(
        [
            grad_query.reshape(batch_rows, local_len, features),
            grad_keys.reshape(batch_rows, local_len, features),
            grad_values.reshape(batch_rows, local_len, features),
        ],
        axis=-1,
    ).astype(jnp.bfloat16)
    grad_joint_weight = outer_sum(normed_one_low, grad_joint)
    grad_joint_bias = jnp.concatenate(
        [column_sums(grad_joint[..., :features]), column_sums(grad_joint[..., 2 * features :])]
    )
    grad_normed_one = project_back(grad_joint, later_joint)
    grad_from_first, grad_gain_one, grad_shift_one = normalize_back(
        grad_normed_one, unit_one, inverse_one, later_gain_one.astype(jnp.float32)
    )
    grad_tokens = grad_middle + grad_from_first
    small_grads = (
        grad_joint_bias, grad_output_bias, grad_gain_one, grad_shift_one,
        grad_up_bias, grad_down_bias, grad_gain_two, grad_shift_two,
    )
    packed = jnp.concatenate([part.reshape(device_count, -1) for part in small_grads], axis=1)
    own = lax.psum_scatter(packed, ("dp", "blk"), scatter_dimension=0, tiled=True)[0]
    small_shards = []
    small_at = 0
    for part in small_parts:
        small_shards.append(own[small_at : small_at + part.shape[0]])
        small_at += part.shape[0]
    return (
        result,
        grad_tokens,
        scatter_sum(grad_joint_weight),
        small_shards[0],
        scatter_sum(grad_output_weight),
        small_shards[1],
        small_shards[2],
        small_shards[3],
        grad_up_shard,
        small_shards[4],
        grad_down_shard,
        small_shards[5],
        small_shards[6],
        small_shards[7],
    )


Z_SIZE, Y_SIZE, BLK_SIZE = 4, 2, 4
MESH = pl.DeviceIdType.MESH
BF = jnp.bfloat16
F32 = jnp.float32


def dot_nn(left, right):
    return lax.dot_general(left, right, (((1,), (0,)), ((), ())), preferred_element_type=F32)


def dot_nt(left, right):
    return lax.dot_general(left, right, (((1,), (1,)), ((), ())), preferred_element_type=F32)


def dot_tn(left, right):
    return lax.dot_general(left, right, (((0,), (0,)), ((), ())), preferred_element_type=F32)


def lane_pieces(lanes, width):
    lane = lax.broadcasted_iota(jnp.int32, (1, lanes), 1).astype(F32)
    piece = jnp.floor((lane + 0.5) * (1.0 / width))
    return piece, lane - width * piece


def piece_placer(lanes, width):
    place = lax.broadcasted_iota(jnp.int32, (128, lanes), 0).astype(F32)
    _, within = lane_pieces(lanes, width)
    return jnp.where(place == within, 1.0, 0.0).astype(BF)


def layer_kernel(
    tok, cot, seg, wj4, wu4, wd, wo, small,
    result, grad_tok, out_j, out_o, out_u, out_d, out_s,
    G, SEG, KSEG, QSEG, PV, QVB,
    N1, N2, GR, WJS, WUS, WDS, WOS, WJ, WU, WO,
    U1, I1, U2, I2, MID, GM, GB,
    Q, K, V, PB, OF, AT, AR, DA, DR, DS, DOH, GJ,
    GP, ACT, GH, UBS,
    PT, RC, SX, RX,
    GDb, GUb, GJb, GOb, GO2, RYd, RYu, RYj, RYo, Sd, Su, Sj, So, RZd, RZu, RZj, RZo,
    AUs, AUr, AJs, AJr, RCo, SXo, RXo, TS, TR, VS, JBS,
    ssem, rsem,
):
    dp = lax.axis_index("dp")
    blk = lax.axis_index("blk")
    z, y = dp // 2, dp % 2
    x, c = blk // 2, blk % 2
    count = [0]
    started = []

    def send(src, dst, dev):
        n = count[0]
        count[0] += 1
        made = pltpu.make_async_remote_copy(
            src_ref=src, dst_ref=dst, send_sem=ssem.at[n], recv_sem=rsem.at[n],
            device_id=dev, device_id_type=MESH,
        )
        made.start()
        started.append(made)
        return made

    core_peer = (dp, 2 * x + 1 - c)
    x_peer = (dp, 2 * (1 - x) + c)
    far_peer = (dp, 2 * (1 - x) + 1 - c)
    blk_peers = (x_peer, far_peer, core_peer)
    y_peer = (2 * z + 1 - y, blk)

    def z_at(k):
        return (z + k) % Z_SIZE

    barrier = pltpu.get_barrier_semaphore()
    every = [
        ((dp + i) % (Z_SIZE * Y_SIZE), (blk + j) % BLK_SIZE)
        for i in range(Z_SIZE * Y_SIZE) for j in range(BLK_SIZE) if i or j
    ]
    for dev in every:
        pl.semaphore_signal(barrier, inc=1, device_id=dev, device_id_type=MESH)
    pl.semaphore_wait(barrier, len(every))

    def swap_columns(parts, slabs):
        slabs[dp, blk] = parts[blk]
        return [send(parts.at[dev[1]], slabs.at[dp, blk], dev) for dev in blk_peers]

    j_first = swap_columns(wj4, WJS)
    SEG[blk] = seg[...]
    seg_copies = [send(seg, SEG.at[blk], dev) for dev in blk_peers]
    G[dp, blk] = small[...]
    small_copies = [send(small, G.at[dp, blk], dev) for dev in every]

    def stats(values):
        mean = jnp.mean(values, axis=-1, keepdims=True)
        centered = values - mean
        inverse = lax.rsqrt(jnp.mean(centered * centered, axis=-1, keepdims=True) + epsilon)
        return centered * inverse, inverse

    for r in range(2):
        unit, inverse = stats(tok[r])
        U1[r] = unit
        I1[r] = inverse

    def gather_start(buf, r):
        return [send(buf.at[r, blk], buf.at[r, blk], dev) for dev in (x_peer, core_peer)]

    def gather_forward(buf, r, first):
        first[0].wait_recv()
        return send(buf.at[r, x_peer[1]], buf.at[r, x_peer[1]], core_peer)

    def gather_end(first, second):
        first[1].wait_recv()
        second.wait_recv()

    for made in small_copies:
        made.wait_recv()
    tiles = G[...].reshape(32 * 8, 128).astype(BF)
    dev_id = lax.broadcasted_iota(jnp.int32, (32, 1, 1), 0).astype(F32)
    blk_f = blk.astype(F32)
    piece24, _ = lane_pieces(768, 24)
    piece48, _ = lane_pieces(192, 48)
    piece96, _ = lane_pieces(768, 96)

    def mask24():
        return piece24[None] == dev_id

    def mask48(first_dev):
        return piece48[None] + (4.0 * blk_f + first_dev) == dev_id

    def mask96():
        return 4.0 * piece96[None] + blk_f == dev_id

    def placed(placer, mask, lanes):
        spread = dot_nn(tiles, placer).reshape(32, 8, lanes)
        return jnp.sum(jnp.where(mask, spread, 0.0), axis=0)

    place24 = piece_placer(768, 24)
    place48 = piece_placer(192, 48)
    place96 = piece_placer(768, 96)
    PV[0:8] = placed(place24, mask24(), 768)
    PV[8:16] = placed(place96, mask96(), 768)
    QVB[0:8] = placed(place48, mask48(0.0), 192)
    QVB[8:16] = placed(place48, mask48(16.0), 192)
    gain1, shift1, obias = PV[0:1], PV[1:2], PV[2:3]
    gain2, shift2, dbias = PV[3:4], PV[4:5], PV[5:6]
    ubias = PV[15:16]
    qbias, vbias = QVB[6:7], QVB[14:15]

    n1_first = []
    for r in range(2):
        N1[r, blk] = (U1[r] * gain1 + shift1).astype(BF)
        n1_first.append(gather_start(N1, r))

    def dp_start(slab):
        over_z = [send(slab(dp), slab(dp), (2 * z_at(k) + y, blk)) for k in range(1, Z_SIZE)]
        return over_z, [send(slab(dp), slab(dp), y_peer)]

    def dp_forward(slab, over_z, over_y):
        for k in range(1, Z_SIZE):
            over_z[k - 1].wait_recv()
            there = 2 * z_at(Z_SIZE - k) + y
            over_y.append(send(slab(there), slab(there), y_peer))

    def dp_end(over_y):
        for made in over_y:
            made.wait_recv()

    def j_slab(i):
        return WJS.at[i]

    def u_slab(i):
        return WUS.at[i]

    def d_slab(i):
        return WDS.at[i]

    def o_slab(i):
        return WOS.at[blk, i]

    for made in j_first:
        made.wait_recv()
    j_over = dp_start(j_slab)

    WOS[blk, dp] = wo[...]
    WDS[dp] = wd[...]
    for r in range(2):
        GR[r, blk] = cot[r].astype(BF)
    for made in seg_copies:
        made.wait_recv()
    eye = jnp.where(
        lax.broadcasted_iota(jnp.int32, (128, 128), 0)
        == lax.broadcasted_iota(jnp.int32, (128, 128), 1), 1.0, 0.0,
    ).astype(BF)
    for b in range(BLK_SIZE):
        part = SEG[b]
        KSEG[:, 128 * b : 128 * (b + 1)] = part
        QSEG[b] = dot_nt(eye, part.astype(BF))

    n1_second = [gather_forward(N1, 0, n1_first[0])]
    u_first = swap_columns(wu4, WUS)
    n1_second.append(gather_forward(N1, 1, n1_first[1]))
    gr_first = [gather_start(GR, r) for r in range(2)]
    dp_forward(j_slab, *j_over)
    o_over = dp_start(o_slab)
    for made in u_first:
        made.wait_recv()
    u_over = dp_start(u_slab)
    d_over = dp_start(d_slab)

    def compact(slabs, whole):
        @pl.loop(0, 8)
        def _(i):
            rows = slabs(i).astype(F32)
            rows = rows.reshape(96, rows.shape[-1])
            whole[pl.ds(pl.multiple_of(96 * i, 96), 96), :] = rows.astype(BF)

    dp_end(j_over[1])
    compact(lambda i: WJS[i], WJ)

    def qkv(r):
        gather_end(n1_first[r], n1_second[r])

        @pl.loop(0, 4)
        def _(t):
            joint = dot_nn(N1[r, t], WJ[...])
            rows = pl.ds(pl.multiple_of(128 * t, 128), 128)
            query = ((joint[:, :192] + qbias).astype(BF).astype(F32) * 0.125).astype(BF)
            keys = joint[:, 192:384].astype(BF)
            values = (joint[:, 384:] + vbias).astype(BF)
            for h in range(3):
                Q[r, h, rows, :] = query[:, 64 * h : 64 * (h + 1)]
                K[r, h, rows, :] = keys[:, 64 * h : 64 * (h + 1)]
                V[r, h, rows, :] = values[:, 64 * h : 64 * (h + 1)]

    def attend(r):
        key_seg = KSEG[2 + r : 3 + r, :]
        for h in range(3):
            @pl.loop(0, 4)
            def _(t):
                rows = pl.ds(pl.multiple_of(128 * t, 128), 128)
                scores = dot_nt(Q[r, h, rows, :], K[r, h])
                scores = jnp.where(QSEG[t][:, r : r + 1] == key_seg, scores, masked_score)
                top = jnp.max(scores, axis=-1, keepdims=True)
                expos = jnp.exp(scores - top)
                total = jnp.sum(expos, axis=-1, keepdims=True)
                probs = (expos * (1.0 / total)).astype(BF)
                PB[r, h, rows, :] = probs
                out = dot_nn(probs, V[r, h])
                OF[r, h, rows, :] = out
                AT[r, t, :, 64 * h : 64 * (h + 1)] = out.astype(BF)

    def swap_heads(src, dst, r):
        dst[r, blk] = src[r, blk]
        return [send(src.at[r, dev[1]], dst.at[r, blk], dev) for dev in blk_peers]

    at_copies = []
    for r in range(2):
        qkv(r)
        attend(r)
        at_copies.append(swap_heads(AT, AR, r))
        if r == 0:
            dp_forward(o_slab, *o_over)
            gr_second = [gather_forward(GR, 0, gr_first[0])]

    dp_end(o_over[1])
    wo_first = [send(WOS.at[blk], WOS.at[blk], dev) for dev in (x_peer, core_peer)]
    gr_second.append(gather_forward(GR, 1, gr_first[1]))
    dp_forward(u_slab, *u_over)
    wo_first[0].wait_recv()
    wo_second = send(WOS.at[x_peer[1]], WOS.at[x_peer[1]], core_peer)
    wo_first[1].wait_recv()
    wo_second.wait_recv()
    compact(lambda i: WOS[:, i], WO)

    n2_first = []
    for r in range(2):
        for made in at_copies[r]:
            made.wait_recv()
        total = tok[r] + obias
        for b in range(BLK_SIZE):
            total = total + dot_nn(AR[r, b], WO[192 * b : 192 * (b + 1), :])
        MID[r] = total
        unit, inverse = stats(total)
        U2[r] = unit
        I2[r] = inverse
        N2[r, blk] = (unit * gain2 + shift2).astype(BF)
        n2_first.append(gather_start(N2, r))

    dp_forward(d_slab, *d_over)
    dp_end(u_over[1])
    compact(lambda i: WUS[i], WU)
    n2_second = [gather_forward(N2, r, n2_first[r]) for r in range(2)]

    def rows_of(buf, r):
        return buf[r].reshape(512, 768)

    def up(r):
        gather_end(n2_first[r], n2_second[r])

        @pl.loop(0, 3)
        def _(n):
            cols = pl.ds(pl.multiple_of(256 * n, 256), 256)
            hidden = dot_nn(rows_of(N2, r), WU[:, cols]) + PV[15:16, cols]
            square = hidden * hidden
            bent = jnp.tanh(0.7978845608028654 * hidden * (1.0 + 0.044715 * square))
            half = 0.5 * (1.0 + bent)
            ACT[r, :, cols] = (hidden * half).astype(BF)
            slope = 0.7978845608028654 * (1.0 + 3 * 0.044715 * square)
            GP[r, :, cols] = half + 0.5 * hidden * (1.0 - bent * bent) * slope

    for r in range(2):
        up(r)

    def down_rows(rows):
        return WDS[rows]

    dp_end(d_over[1])

    def hidden_back(r):
        gather_end(gr_first[r], gr_second[r])

        @pl.loop(0, 2)
        def _(n):
            cols = pl.ds(pl.multiple_of(384 * n, 384), 384)
            weight = WDS[pl.ds(4 * n, 4)].reshape(384, 768)
            grad = dot_nt(rows_of(GR, r), weight)
            grad = (grad * GP[r, :, cols]).astype(BF)
            GH[r, :, cols] = grad
            UBS[r, :, cols] = jnp.sum(grad.astype(F32), axis=0, keepdims=True)

    def sum_store(i, r, cols, values):
        PT[i, r, :, :, :, cols] = values.reshape(2, 2, 128, values.shape[-1]).astype(BF)

    def sum_start(i, r):
        return send(PT.at[i, r, :, 1 - c], RC.at[i, r], core_peer)

    def sum_middle(i, r, first):
        first.wait_recv()
        SX[i, r] = (PT[i, r, 1 - x, c].astype(F32) + RC[i, r, 1 - x].astype(F32)).astype(BF)
        return send(SX.at[i, r], RX.at[i, r], x_peer)

    def sum_end(i, r, second):
        second.wait_recv()
        return (
            PT[i, r, x, c].astype(F32) + RC[i, r, x].astype(F32) + RX[i, r].astype(F32)
        )

    def back_to_input(i, r, grads, weight):
        @pl.loop(0, 3)
        def _(n):
            cols = pl.ds(pl.multiple_of(256 * n, 256), 256)
            sum_store(i, r, cols, dot_nt(grads(r), weight[cols, :]))

        return sum_start(i, r)

    def down(r):
        @pl.loop(0, 3)
        def _(n):
            cols = pl.ds(pl.multiple_of(256 * n, 256), 256)
            weight = WDS[:, :, cols].reshape(768, 256)
            sum_store(1, r, cols, dot_nn(ACT[r], weight))

        return sum_start(1, r)

    hidden_back(0)
    second_first = [back_to_input(0, 0, lambda r: GH[r], WU)]
    hidden_back(1)
    second_second = [sum_middle(0, 0, second_first[0])]
    second_first.append(back_to_input(0, 1, lambda r: GH[r], WU))

    def scatter_start(parts, recv):
        return send(parts.at[:, 1 - y], recv, y_peer)

    def scatter_middle(parts, recv, sums, landing, first):
        first.wait_recv()
        sums[...] = (parts[:, y].astype(F32) + recv[...].astype(F32)).astype(BF)
        return [
            send(sums.at[z_at(k)], landing.at[k - 1], (2 * z_at(k) + y, blk))
            for k in range(1, Z_SIZE)
        ]

    def scatter_end(sums, landing, second):
        for made in second:
            made.wait_recv()
        total = sums[z].astype(F32)
        for k in range(Z_SIZE - 1):
            total = total + landing[k].astype(F32)
        return total

    @pl.loop(0, 2)
    def _(m):
        cols = pl.ds(pl.multiple_of(384 * m, 384), 384)
        grad = dot_tn(ACT[:, :, cols].reshape(1024, 384), GR[...].reshape(1024, 768))
        GDb[pl.ds(2 * m, 2)] = grad.reshape(2, 2, 96, 768).astype(BF)

    d_first = scatter_start(GDb, RYd)
    second_second.append(sum_middle(0, 1, second_first[1]))

    @pl.loop(0, 2)
    def _(m):
        cols = pl.ds(pl.multiple_of(384 * m, 384), 384)
        grad = dot_tn(N2[:, :, :, cols].reshape(1024, 384), GH[...].reshape(1024, 768))
        GUb[pl.ds(2 * m, 2)] = grad.reshape(2, 2, 4, 24, 768).astype(BF)

    u_grad_first = scatter_start(GUb, RYu)

    def norm_back(e, unit, inverse, gain):
        f = e * gain
        grad = inverse * (
            f - jnp.mean(f, axis=-1, keepdims=True)
            - unit * jnp.mean(f * unit, axis=-1, keepdims=True)
        )
        return (
            grad, jnp.sum(e * unit, axis=0, keepdims=True), jnp.sum(e, axis=0, keepdims=True)
        )

    VS[...] = jnp.zeros_like(VS)
    da_copies = []
    for r in range(2):
        e = sum_end(0, r, second_second[r])
        grad, of_gain, of_shift = norm_back(e, U2[r], I2[r], gain2)
        grad = grad + cot[r]
        GM[r] = grad
        low = grad.astype(BF)
        GB[r] = low
        VS[3:4] += of_gain
        VS[4:5] += of_shift
        VS[2:3] += jnp.sum(low.astype(F32), axis=0, keepdims=True)
        VS[5:6] += jnp.sum(cot[r].astype(BF).astype(F32), axis=0, keepdims=True)
        for b in range(BLK_SIZE):
            DA[r, b] = dot_nt(low, WO[192 * b : 192 * (b + 1), :]).astype(BF)
        da_copies.append(swap_heads(DA, DR, r))

    d_second = scatter_middle(GDb, RYd, Sd, RZd, d_first)
    result_first = [down(r) for r in range(2)]

    def attend_back(r):
        for made in da_copies[r]:
            made.wait_recv()
        for h in range(3):
            @pl.loop(0, 4)
            def _(t):
                rows = pl.ds(pl.multiple_of(128 * t, 128), 128)
                grad_out = DR[r, t][:, 64 * h : 64 * (h + 1)]
                DOH[rows, :] = grad_out
                delta = jnp.sum(grad_out.astype(F32) * OF[r, h, rows, :], axis=-1, keepdims=True)
                grad_probs = dot_nt(grad_out, V[r, h])
                DS[rows, :] = (PB[r, h, rows, :].astype(F32) * (grad_probs - delta)).astype(BF)

            at = 64 * h
            GJ[r, :, at : at + 64] = (dot_nn(DS[...], K[r, h]) * 0.125).astype(BF)
            GJ[r, :, 192 + at : 256 + at] = dot_tn(DS[...], Q[r, h]).astype(BF)
            GJ[r, :, 384 + at : 448 + at] = dot_tn(PB[r, h], DOH[...]).astype(BF)
        JBS[r] = jnp.sum(GJ[r].astype(F32), axis=0, keepdims=True)

    attend_back(0)
    u_grad_second = scatter_middle(GUb, RYu, Su, RZu, u_grad_first)
    first_first = [back_to_input(2, 0, lambda r: GJ[r], WJ)]
    result_second = [sum_middle(1, r, result_first[r]) for r in range(2)]
    attend_back(1)
    first_second = [sum_middle(2, 0, first_first[0])]
    first_first.append(back_to_input(2, 1, lambda r: GJ[r], WJ))

    @pl.loop(0, 2)
    def _(m):
        cols = pl.ds(pl.multiple_of(384 * m, 384), 384)
        grad = dot_tn(N1[:, :, :, cols].reshape(1024, 384), GJ[...].reshape(1024, 576))
        GJb[pl.ds(2 * m, 2)] = grad.reshape(2, 2, 4, 24, 576).astype(BF)

    j_grad_first = scatter_start(GJb, RYj)
    first_second.append(sum_middle(2, 1, first_first[1]))

    for b in range(BLK_SIZE):
        grad = dot_tn(AR[:, b].reshape(256, 192), GB[...].reshape(256, 768))
        grad = grad.reshape(2, 4, 24, 768).astype(BF)
        for i in range(4):
            GOb[i // 2, i % 2, 2 * b : 2 * b + 2] = grad[:, i]
    o_grad_core = send(GOb.at[:, 1 - c], RCo, core_peer)

    d_grad = scatter_end(Sd, RZd, d_second)
    out_d[...] = d_grad
    u_grad = scatter_end(Su, RZu, u_grad_second)

    o_grad_core.wait_recv()
    SXo[...] = (GOb[1 - x, c].astype(F32) + RCo[1 - x].astype(F32)).astype(BF)
    o_grad_x = send(SXo, RXo, x_peer)

    def return_columns(total, sends, recvs):
        sends[...] = total.astype(BF)
        recvs[blk] = sends[blk]
        return [send(sends.at[dev[1]], recvs.at[blk], dev) for dev in blk_peers]

    u_back = return_columns(u_grad, AUs, AUr)
    j_grad_second = scatter_middle(GJb, RYj, Sj, RZj, j_grad_first)
    for r in range(2):
        result[r] = MID[r] + sum_end(1, r, result_second[r]) + dbias
    o_grad_x.wait_recv()
    GO2[...] = (
        GOb[x, c].astype(F32) + RCo[x].astype(F32) + RXo[...].astype(F32)
    ).astype(BF).reshape(4, 2, 24, 768)
    o_grad_first = scatter_start(GO2, RYo)

    for r in range(2):
        e = sum_end(2, r, first_second[r])
        grad, of_gain, of_shift = norm_back(e, U1[r], I1[r], gain1)
        grad_tok[r] = GM[r] + grad
        VS[0:1] += of_gain
        VS[1:2] += of_shift


    o_grad_second = scatter_middle(GO2, RYo, So, RZo, o_grad_first)
    j_back = return_columns(scatter_end(Sj, RZj, j_grad_second), AJs, AJr)

    row = lax.broadcasted_iota(jnp.int32, (8, 1), 0)

    def picked(values, mask, placer):
        wide = jnp.where(mask, values[None], 0.0)
        wide = wide.reshape(256, wide.shape[-1])
        high = wide.astype(BF)
        rest = (wide - high.astype(F32)).astype(BF)
        return dot_nt(high, placer) + dot_nt(rest, placer)

    joint_sums = JBS[0] + JBS[1]
    up_sums = UBS[0] + UBS[1]
    pieces = picked(VS[...], mask24(), place24)
    pieces += picked(jnp.where(row == 7, up_sums, 0.0), mask96(), place96)
    pieces += picked(jnp.where(row == 6, joint_sums[:, :192], 0.0), mask48(0.0), place48)
    pieces += picked(jnp.where(row == 6, joint_sums[:, 384:], 0.0), mask48(16.0), place48)
    TS[...] = pieces.reshape(8, 4, 8, 128)
    TR[dp, blk] = TS[dp, blk]
    sums_sent = [send(TS.at[dev], TR.at[dp, blk], dev) for dev in every]

    out_o[...] = scatter_end(So, RZo, o_grad_second)
    for made in u_back:
        made.wait_recv()
    out_u[...] = AUr[...].astype(F32)
    for made in j_back:
        made.wait_recv()
    out_j[...] = AJr[...].astype(F32)
    for made in sums_sent:
        made.wait_recv()
    out_s[...] = jnp.sum(TR[...].reshape(32, 8, 128), axis=0)
    for made in started:
        made.wait_send()


def fast_device(
    tokens, segment_ids, pad_mask, joint_weight, joint_bias, output_weight, output_bias,
    first_gain, first_shift, up_weight, up_bias, down_weight, down_bias,
    second_gain, second_shift, cotangent,
):
    key_segment = jnp.where(pad_mask == 1, segment_ids, -1)
    segments = jnp.concatenate(
        [segment_ids, key_segment, jnp.zeros((4, 128), jnp.int32)], axis=0
    ).astype(F32)
    joint_parts = joint_weight.reshape(24, 3, 4, 192).transpose(2, 0, 1, 3).reshape(4, 24, 576)
    up_parts = up_weight.reshape(24, 8, 4, 96).transpose(2, 0, 1, 3).reshape(4, 24, 768)
    vectors = (
        first_gain, first_shift, output_bias, second_gain, second_shift, down_bias,
        joint_bias, up_bias,
    )
    small = jnp.stack([jnp.pad(part, (0, 128 - part.shape[0])) for part in vectors]).astype(F32)

    def vm(*shape, dtype=BF):
        return pltpu.VMEM(shape, dtype)

    scratch = [
        vm(8, 4, 8, 128, dtype=F32), vm(4, 8, 128, dtype=F32), vm(8, 512, dtype=F32),
        vm(4, 128, 8, dtype=F32), vm(16, 768, dtype=F32), vm(16, 192, dtype=F32),
        vm(2, 4, 128, 768), vm(2, 4, 128, 768), vm(2, 4, 128, 768),
        vm(8, 4, 24, 576), vm(8, 4, 24, 768), vm(8, 96, 768), vm(4, 8, 24, 768),
        vm(768, 576), vm(768, 768), vm(768, 768),
        vm(2, 128, 768, dtype=F32), vm(2, 128, 1, dtype=F32),
        vm(2, 128, 768, dtype=F32), vm(2, 128, 1, dtype=F32),
        vm(2, 128, 768, dtype=F32), vm(2, 128, 768, dtype=F32), vm(2, 128, 768),
        vm(2, 3, 512, 64), vm(2, 3, 512, 64), vm(2, 3, 512, 64), vm(2, 3, 512, 512),
        vm(2, 3, 512, 64, dtype=F32), vm(2, 4, 128, 192), vm(2, 4, 128, 192),
        vm(2, 4, 128, 192), vm(2, 4, 128, 192), vm(512, 512), vm(512, 64),
        vm(2, 512, 576),
        vm(2, 512, 768, dtype=F32), vm(2, 512, 768), vm(2, 512, 768), vm(2, 1, 768, dtype=F32),
        vm(3, 2, 2, 2, 128, 768), vm(3, 2, 2, 128, 768), vm(3, 2, 128, 768), vm(3, 2, 128, 768),
        vm(4, 2, 96, 768), vm(4, 2, 4, 24, 768), vm(4, 2, 4, 24, 576), vm(2, 2, 8, 24, 768),
        vm(4, 2, 24, 768),
        vm(4, 96, 768), vm(4, 4, 24, 768), vm(4, 4, 24, 576), vm(4, 24, 768),
        vm(4, 96, 768), vm(4, 4, 24, 768), vm(4, 4, 24, 576), vm(4, 24, 768),
        vm(3, 96, 768), vm(3, 4, 24, 768), vm(3, 4, 24, 576), vm(3, 24, 768),
        vm(4, 24, 768), vm(4, 24, 768), vm(4, 24, 576), vm(4, 24, 576),
        vm(2, 8, 24, 768), vm(8, 24, 768), vm(8, 24, 768),
        vm(8, 4, 8, 128, dtype=F32), vm(8, 4, 8, 128, dtype=F32), vm(8, 768, dtype=F32),
        vm(2, 1, 576, dtype=F32),
        pltpu.SemaphoreType.DMA((COPIES,)), pltpu.SemaphoreType.DMA((COPIES,)),
    ]
    vmem = pl.BlockSpec(memory_space=pltpu.VMEM)
    out_shapes = [
        (2, 128, 768), (2, 128, 768), (4, 24, 576), (24, 768), (4, 24, 768), (96, 768), (8, 128),
    ]
    result, grad_tokens, grad_j, grad_o, grad_u, grad_d, sums = pl.pallas_call(
        layer_kernel,
        out_shape=[jax.ShapeDtypeStruct(shape, F32) for shape in out_shapes],
        in_specs=[vmem] * 8,
        out_specs=[vmem] * 7,
        scratch_shapes=scratch,
        compiler_params=pltpu.CompilerParams(
            collective_id=0, has_side_effects=True, vmem_limit_bytes=60 * 2**20
        ),
        cost_estimate=pl.CostEstimate(
            flops=13 * 10**9, bytes_accessed=6 * 10**6, transcendentals=4 * 10**6
        ),
    )(tokens, cotangent, segments, joint_parts, up_parts, down_weight, output_weight, small)
    grad_joint = grad_j.reshape(4, 24, 3, 192).transpose(1, 2, 0, 3).reshape(24, 2304)
    grad_up = grad_u.reshape(4, 24, 8, 96).transpose(1, 2, 0, 3).reshape(24, 3072)
    return (
        result, grad_tokens, grad_joint, sums[6, :48], grad_o, sums[2, :24], sums[0, :24],
        sums[1, :24], grad_up, sums[7, :96], grad_d, sums[5, :24], sums[3, :24], sums[4, :24],
    )


def solution(mesh):
    placed = (
        P("dp", "blk", None),
        P("dp", "blk"),
        P("dp", "blk"),
        P(("dp", "blk"), None),
        P(("dp", "blk")),
        P(("dp", "blk"), None),
        P(("dp", "blk")),
        P(("dp", "blk")),
        P(("dp", "blk")),
        P(("dp", "blk"), None),
        P(("dp", "blk")),
        P(("dp", "blk"), None),
        P(("dp", "blk")),
        P(("dp", "blk")),
        P(("dp", "blk")),
        P("dp", "blk", None),
    )

    def layer(*arrays):
        rows, length, features = arrays[0].shape
        hidden = arrays[9].shape[1]
        shape = dict(mesh.shape)
        fits = (
            shape == {"dp": Z_SIZE * Y_SIZE, "blk": BLK_SIZE}
            and (rows, length, features, hidden) == (2 * shape["dp"], 512, 768, 3072)
        )
        return spread(fast_device if fits else per_device)(*arrays)

    def spread(device_part):
      return jax.shard_map(
        device_part,
        mesh=mesh,
        in_specs=placed,
        out_specs=(
            P("dp", "blk", None),
            P("dp", "blk", None),
            P(("dp", "blk"), None),
            P(("dp", "blk")),
            P(("dp", "blk"), None),
            P(("dp", "blk")),
            P(("dp", "blk")),
            P(("dp", "blk")),
            P(("dp", "blk"), None),
            P(("dp", "blk")),
            P(("dp", "blk"), None),
            P(("dp", "blk")),
            P(("dp", "blk")),
            P(("dp", "blk")),
        ),
        check_vma=False,
    )

    return layer
```

```python
import jax
import jax.numpy as jnp
from jax import lax
from jax.experimental import pallas as pl
from jax.experimental.pallas import tpu as pltpu
from jax.sharding import PartitionSpec as P

HEADS = 12
COPIES = 96
VMEM_MIB = 60


epsilon = 1e-05
masked_score = -1e30


def normalize(values_in, gain, shift):
    centered = values_in - jnp.mean(values_in, axis=-1, keepdims=True)
    inverse = lax.rsqrt(jnp.mean(centered * centered, axis=-1, keepdims=True) + epsilon)
    unit_rows = centered * inverse
    return (unit_rows * gain + shift, unit_rows, inverse)


def normalize_back(grad_normed, unit_rows, inverse, gain):
    scaled = grad_normed * gain
    grad_input = inverse * (
        scaled
        - jnp.mean(scaled, axis=-1, keepdims=True)
        - unit_rows * jnp.mean(scaled * unit_rows, axis=-1, keepdims=True)
    )
    return (
        grad_input,
        jnp.sum(grad_normed * unit_rows, axis=(0, 1)),
        jnp.sum(grad_normed, axis=(0, 1)),
    )


def project(activation, weight):
    return jnp.einsum("rcd,dn->rcn", activation, weight, preferred_element_type=jnp.float32)


def project_back(gradient, weight):
    return jnp.einsum("rcn,dn->rcd", gradient, weight, preferred_element_type=jnp.float32)


def outer_sum(activation, gradient):
    return jnp.einsum("rcd,rcn->dn", activation, gradient, preferred_element_type=jnp.float32)


def split_heads(matrix, head_count):
    return matrix.reshape(
        matrix.shape[0], matrix.shape[1], head_count, matrix.shape[2] // head_count
    )


def masked_scores(query_heads, key_heads, query_segment, key_segment, scaling):
    raw_scores = (
        jnp.einsum("rqhd,rkhd->rhqk", query_heads, key_heads, preferred_element_type=jnp.float32)
        * scaling
    )
    allowed = (query_segment[:, :, None] == key_segment[:, None, :])[:, None]
    return (jnp.where(allowed, raw_scores, masked_score), allowed)


def column_sums(gradient):
    return jnp.sum(gradient.astype(jnp.float32), axis=(0, 1))


def scatter_sum(gradient):
    summed = lax.psum_scatter(
        gradient.astype(jnp.bfloat16), ("dp", "blk"), scatter_dimension=0, tiled=True
    )
    return summed.astype(jnp.float32)


def per_device(
    tokens,
    segment_ids,
    pad_mask,
    joint_weight,
    joint_bias,
    output_weight,
    output_bias,
    first_gain,
    first_shift,
    up_weight,
    up_bias,
    down_weight,
    down_bias,
    second_gain,
    second_shift,
    cotangent,
):
    batch_rows, local_len, features = tokens.shape
    head_count = HEADS
    head_size = features // head_count
    scaling = head_size ** (-0.5)
    device_count = lax.axis_size("dp") * lax.axis_size("blk")
    small_parts = (
        joint_bias, output_bias, first_gain, first_shift, up_bias, down_bias, second_gain, second_shift
    )
    small_all = lax.all_gather(jnp.concatenate(small_parts), ("dp", "blk"), axis=0, tiled=True)
    small_all = small_all.reshape(device_count, -1)
    small_full = []
    small_at = 0
    for part in small_parts:
        small_full.append(small_all[:, small_at : small_at + part.shape[0]].reshape(-1))
        small_at += part.shape[0]
    full_joint_bias, full_output_bias, gain_one, shift_one = small_full[:4]
    full_up_bias, full_down_bias, gain_two, shift_two = small_full[4:]
    full_joint = lax.all_gather(joint_weight, ("dp", "blk"), axis=0, tiled=True)
    full_output = lax.all_gather(output_weight, ("dp", "blk"), axis=0, tiled=True)
    normed_one, unit_one, inverse_one = normalize(
        tokens, gain_one.astype(jnp.float32), shift_one.astype(jnp.float32)
    )
    normed_one_low = normed_one.astype(jnp.bfloat16)
    joint = project(normed_one_low, full_joint)
    bias_values = full_joint_bias.astype(jnp.float32)
    query = (joint[..., :features] + bias_values[:features]).astype(jnp.bfloat16)
    keys = joint[..., features : 2 * features].astype(jnp.bfloat16)
    values = (joint[..., 2 * features :] + bias_values[features:]).astype(jnp.bfloat16)
    key_segment = jnp.where(pad_mask == 1, segment_ids, -1)
    query_heads = split_heads(query, head_count)
    top_score = jnp.full((batch_rows, head_count, local_len), masked_score, jnp.float32)
    key_portion = lax.all_gather(keys, "blk", axis=1, tiled=True)
    value_portion = lax.all_gather(values, "blk", axis=1, tiled=True)
    segment_portion = lax.all_gather(key_segment, "blk", axis=1, tiled=True)
    scores, allowed = masked_scores(
        query_heads, split_heads(key_portion, head_count), segment_ids, segment_portion, scaling
    )
    new_top = jnp.maximum(top_score, jnp.max(scores, axis=-1))
    weights = jnp.where(allowed, jnp.exp(scores - new_top[..., None]), 0.0)
    total_weight = jnp.sum(weights, axis=-1)
    weighted = jnp.einsum(
        "rhqk,rkhd->rhqd",
        weights.astype(jnp.bfloat16),
        split_heads(value_portion, head_count),
        preferred_element_type=jnp.float32,
    )
    top_score, total_weight, weighted = (new_top, total_weight, weighted)
    log_total = top_score + jnp.log(total_weight)
    attended_heads = weighted / total_weight[..., None]
    attended = jnp.transpose(attended_heads, (0, 2, 1, 3)).reshape(batch_rows, local_len, features)
    attended_low = attended.astype(jnp.bfloat16)
    middle = tokens + project(attended_low, full_output) + full_output_bias.astype(jnp.float32)
    full_up = lax.all_gather(up_weight, ("dp", "blk"), axis=0, tiled=True)
    full_down = lax.all_gather(down_weight, ("dp", "blk"), axis=0, tiled=True)
    normed_two, unit_two, inverse_two = normalize(
        middle, gain_two.astype(jnp.float32), shift_two.astype(jnp.float32)
    )
    normed_two_low = normed_two.astype(jnp.bfloat16)
    hidden = project(normed_two_low, full_up) + full_up_bias.astype(jnp.float32)
    activated, gelu_pullback = jax.vjp(jax.nn.gelu, hidden)
    activated_low = activated.astype(jnp.bfloat16)
    result = middle + project(activated_low, full_down) + full_down_bias.astype(jnp.float32)
    later_up, later_down, later_gain_two = full_up, full_down, gain_two
    grad_result = cotangent.astype(jnp.bfloat16)
    grad_down_weight = outer_sum(activated_low, grad_result)
    grad_down_bias = column_sums(grad_result)
    grad_activated = project_back(grad_result, later_down)
    grad_hidden = gelu_pullback(grad_activated)[0].astype(jnp.bfloat16)
    grad_up_bias = column_sums(grad_hidden)
    grad_up_weight = outer_sum(normed_two_low, grad_hidden)
    grad_normed_two = project_back(grad_hidden, later_up)
    grad_from_second, grad_gain_two, grad_shift_two = normalize_back(
        grad_normed_two, unit_two, inverse_two, later_gain_two.astype(jnp.float32)
    )
    grad_middle = cotangent + grad_from_second
    grad_up_shard = scatter_sum(grad_up_weight)
    grad_down_shard = scatter_sum(grad_down_weight)
    later_joint, later_output, later_gain_one = full_joint, full_output, gain_one
    grad_branch = grad_middle.astype(jnp.bfloat16)
    grad_output_weight = outer_sum(attended_low, grad_branch)
    grad_output_bias = column_sums(grad_branch)
    grad_attended = project_back(grad_branch, later_output).astype(jnp.bfloat16)
    grad_heads = split_heads(grad_attended, head_count)
    delta = jnp.einsum("rqhd,rhqd->rhq", grad_heads.astype(jnp.float32), attended_heads)
    key_heads = split_heads(key_portion, head_count)
    scores, allowed = masked_scores(query_heads, key_heads, segment_ids, segment_portion, scaling)
    probs = jnp.where(allowed, jnp.exp(scores - log_total[..., None]), 0.0)
    grad_probs = jnp.einsum(
        "rqhd,rkhd->rhqk",
        grad_heads,
        split_heads(value_portion, head_count),
        preferred_element_type=jnp.float32,
    )
    grad_scores = (probs * (grad_probs - delta[..., None])).astype(jnp.bfloat16)
    grad_query = scaling * jnp.einsum(
        "rhqk,rkhd->rqhd", grad_scores, key_heads, preferred_element_type=jnp.float32
    )
    every_total, every_delta = (
        lax.all_gather(log_total, "blk", axis=2, tiled=True),
        lax.all_gather(delta, "blk", axis=2, tiled=True),
    )
    own_keys = split_heads(keys, head_count)
    own_values = split_heads(values, head_count)
    query_portion = lax.all_gather(query, "blk", axis=1, tiled=True)
    grad_portion = lax.all_gather(grad_attended, "blk", axis=1, tiled=True)
    segment_portion = lax.all_gather(segment_ids, "blk", axis=1, tiled=True)
    portion_queries = split_heads(query_portion, head_count)
    portion_grads = split_heads(grad_portion, head_count)
    scores, allowed = masked_scores(
        portion_queries, own_keys, segment_portion, key_segment, scaling
    )
    probs = jnp.where(allowed, jnp.exp(scores - every_total[..., None]), 0.0)
    grad_values = jnp.einsum(
        "rhqk,rqhd->rkhd",
        probs.astype(jnp.bfloat16),
        portion_grads,
        preferred_element_type=jnp.float32,
    )
    grad_probs = jnp.einsum(
        "rqhd,rkhd->rhqk", portion_grads, own_values, preferred_element_type=jnp.float32
    )
    grad_scores = (probs * (grad_probs - every_delta[..., None])).astype(jnp.bfloat16)
    grad_keys = scaling * jnp.einsum(
        "rhqk,rqhd->rkhd", grad_scores, portion_queries, preferred_element_type=jnp.float32
    )
    grad_keys, grad_values = (grad_keys, grad_values)
    grad_joint = jnp.concatenate(
        [
            grad_query.reshape(batch_rows, local_len, features),
            grad_keys.reshape(batch_rows, local_len, features),
            grad_values.reshape(batch_rows, local_len, features),
        ],
        axis=-1,
    ).astype(jnp.bfloat16)
    grad_joint_weight = outer_sum(normed_one_low, grad_joint)
    grad_joint_bias = jnp.concatenate(
        [column_sums(grad_joint[..., :features]), column_sums(grad_joint[..., 2 * features :])]
    )
    grad_normed_one = project_back(grad_joint, later_joint)
    grad_from_first, grad_gain_one, grad_shift_one = normalize_back(
        grad_normed_one, unit_one, inverse_one, later_gain_one.astype(jnp.float32)
    )
    grad_tokens = grad_middle + grad_from_first
    small_grads = (
        grad_joint_bias, grad_output_bias, grad_gain_one, grad_shift_one,
        grad_up_bias, grad_down_bias, grad_gain_two, grad_shift_two,
    )
    packed = jnp.concatenate([part.reshape(device_count, -1) for part in small_grads], axis=1)
    own = lax.psum_scatter(packed, ("dp", "blk"), scatter_dimension=0, tiled=True)[0]
    small_shards = []
    small_at = 0
    for part in small_parts:
        small_shards.append(own[small_at : small_at + part.shape[0]])
        small_at += part.shape[0]
    return (
        result,
        grad_tokens,
        scatter_sum(grad_joint_weight),
        small_shards[0],
        scatter_sum(grad_output_weight),
        small_shards[1],
        small_shards[2],
        small_shards[3],
        grad_up_shard,
        small_shards[4],
        grad_down_shard,
        small_shards[5],
        small_shards[6],
        small_shards[7],
    )


Z_SIZE, Y_SIZE, BLK_SIZE = 4, 2, 4
DP_SIZE = Z_SIZE * Y_SIZE
MESH = pl.DeviceIdType.MESH
BF = jnp.bfloat16
F32 = jnp.float32
TILE_WIDTHS = (24, 24, 24, 24, 24, 24, 48, 96)


def dot_nn(left, right):
    return lax.dot_general(left, right, (((1,), (0,)), ((), ())), preferred_element_type=F32)


def dot_nt(left, right):
    return lax.dot_general(left, right, (((1,), (1,)), ((), ())), preferred_element_type=F32)


def dot_tn(left, right):
    return lax.dot_general(left, right, (((0,), (0,)), ((), ())), preferred_element_type=F32)


def lane_pieces(lanes, width):
    lane = lax.broadcasted_iota(jnp.int32, (1, lanes), 1).astype(F32)
    piece = jnp.floor((lane + 0.5) * (1.0 / width))
    return piece, lane - width * piece


def piece_placer(lanes, width):
    place = lax.broadcasted_iota(jnp.int32, (128, lanes), 0).astype(F32)
    _, within = lane_pieces(lanes, width)
    return jnp.where(place == within, 1.0, 0.0).astype(BF)


def layer_kernel(*refs):
    ins, outs, scr = refs[:16], refs[16:23], refs[23:]
    (tok_in, cot_in, seg_in, pad_in, jw_in, uw_in, dw_in, ow_in), vectors = ins[:8], ins[8:]
    result_out, grad_tok_out, out_j, out_o, out_u, out_d, out_s = outs
    (
        TOK, COT, JW, UW, DW, JP0, JP1, UP, TILE, SEGT, G, SEG, KSEG, QSEG, PV, QVB,
        N1, N2, GR, WJS0, WJS1, WUS, WDS, WOS, WJ0, WJ1, WU, WO,
        U1, I1, U2, I2, MID, GM, GB,
        Q, K, V, PB, OF, AT, AR, DA, DR, DOH, GJ0, GJ1,
        GP, ACT, GH, UBS, PT, RC, SX, RX,
        GD, GU, GA, GC, GO, GO2, RYd, RYu, RYa, RYc, RYo, Sd, Su, Sa, Sc, So,
        RZd, RZu, RZa, RZc, RZo, AUs, AUr, AAs, AAr, ACs, ACr, RCo, SXo, RXo,
        TS, TR, VS, JBS, OJ, OU, OD, OO, OS, ssem, rsem, lsem,
    ) = scr
    dp = lax.axis_index("dp")
    blk = lax.axis_index("blk")
    z, y = dp // 2, dp % 2
    x, c = blk // 2, blk % 2
    count = [0, 0]
    started = []

    def local(src, dst):
        n = count[1]
        count[1] += 1
        made = pltpu.make_async_copy(src, dst, lsem.at[n])
        made.start()
        return made

    def group():
        n = count[0]
        count[0] += 1
        return ssem.at[n], rsem.at[n]

    def send(src, dst, dev, sems):
        made = pltpu.make_async_remote_copy(
            src_ref=src, dst_ref=dst, send_sem=sems[0], recv_sem=sems[1],
            device_id=dev, device_id_type=MESH,
        )
        made.start()
        return made

    def wait_bytes(sem, ref):
        pltpu.make_async_copy(ref, ref, sem).wait()

    def received(copies):
        wait_bytes(copies[0][1], copies[1])

    def later_sent(copies):
        started.append(copies)

    def sent(copies):
        wait_bytes(copies[0][0], copies[1])

    core_peer = (dp, 2 * x + 1 - c)
    x_peer = (dp, 2 * (1 - x) + c)
    far_peer = (dp, 2 * (1 - x) + 1 - c)
    blk_peers = (x_peer, far_peer, core_peer)
    y_peer = (2 * z + 1 - y, blk)

    def z_at(k):
        return (z + k) % Z_SIZE

    ow_copy = local(ow_in, WOS.at[blk, dp])
    jw_copy = local(jw_in, JW)
    tok_copy = local(tok_in, TOK)
    uw_copy = local(uw_in, UW)
    dw_copy = local(dw_in, DW)
    cot_copy = local(cot_in, COT)

    every = [
        ((dp + i) % DP_SIZE, (blk + j) % BLK_SIZE)
        for i in range(DP_SIZE) for j in range(BLK_SIZE) if i or j
    ]

    def entry_barrier():
        barrier = pltpu.get_barrier_semaphore()
        for dev in every:
            pl.semaphore_signal(barrier, inc=1, device_id=dev, device_id_type=MESH)
        pl.semaphore_wait(barrier, len(every))

    entry_barrier()

    def stats(values):
        mean = jnp.mean(values, axis=-1, keepdims=True)
        centered = values - mean
        inverse = lax.rsqrt(jnp.mean(centered * centered, axis=-1, keepdims=True) + epsilon)
        return centered * inverse, inverse

    def dp_start(slab, span):
        over_z, over_y = group(), group()
        for k in range(1, Z_SIZE):
            send(slab(dp), slab(dp), (2 * z_at(k) + y, blk), over_z)
        send(slab(dp), slab(dp), y_peer, over_y)
        later_sent((over_z, span(3)))
        later_sent((over_y, span(4)))
        return slab, span, over_z, over_y

    def dp_forward(part):
        slab, span, over_z, over_y = part
        received((over_z, span(3)))
        for k in range(1, Z_SIZE):
            there = 2 * z_at(Z_SIZE - k) + y
            send(slab(there), slab(there), y_peer, over_y)

    def dp_end(part):
        _, span, _, over_y = part
        received((over_y, span(4)))

    def swap_parts(parts, landing):
        sems = group()
        for dev in blk_peers:
            send(parts(dev[1]), landing.at[blk], dev, sems)
        span = landing.at[pl.ds(c, 3)]
        later_sent((sems, span))
        return sems, span

    def gather_start(buf, r):
        over_x, to_core = group(), group()
        send(buf.at[r, blk], buf.at[r, blk], x_peer, over_x)
        send(buf.at[r, blk], buf.at[r, blk], core_peer, to_core)
        later_sent((over_x, buf.at[r, blk]))
        later_sent((to_core, buf.at[r, pl.ds(c, 2)]))
        return buf, r, over_x, to_core

    def gather_forward(part):
        buf, r, over_x, to_core = part
        received((over_x, buf.at[r, x_peer[1]]))
        send(buf.at[r, x_peer[1]], buf.at[r, x_peer[1]], core_peer, to_core)

    def gather_end(part):
        buf, r, _, to_core = part
        received((to_core, buf.at[r, pl.ds(c, 2)]))

    ow_copy.wait()
    o_part = dp_start(lambda i: WOS.at[blk, i], lambda n: WOS.at[blk, pl.ds(c, n)])

    def split_joint():
        jw_copy.wait()
        for b in range(BLK_SIZE):
            for s in range(3):
                at = 768 * s + 192 * b
                JP0[b, :, 64 * s : 64 * (s + 1)] = JW[:, at : at + 64]
                JP1[b, :, 128 * s : 128 * (s + 1)] = JW[:, at + 64 : at + 192]

    def swap_columns(parts, slabs):
        slabs[dp, blk] = parts[blk]
        return swap_parts(lambda b: parts.at[b], slabs.at[dp])

    split_joint()
    a_first = swap_columns(JP0, WJS0)
    c_first = swap_columns(JP1, WJS1)

    def first_stats():
        tok_copy.wait()
        firsts = []
        for r in range(2):
            unit, inverse = stats(TOK[r])
            U1[r] = unit
            I1[r] = inverse
            N1[r, blk] = unit.astype(BF)
            firsts.append(gather_start(N1, r))
        return firsts

    n1_part = first_stats()
    n1_sent = (started[-4:-2], started[-2:])
    del started[-4:]

    def send_all(src, landing):
        sems = group()
        for dev in every:
            send(src(dev), landing.at[4 * dp + blk], dev, sems)
        span = landing.at[pl.ds(c, 31)]
        later_sent((sems, span))
        return sems, span

    def small_start():
        TILE[...] = jnp.zeros_like(TILE)
        for row, (ref, width) in enumerate(zip(vectors, TILE_WIDTHS)):
            TILE[row : row + 1, 0:width] = ref[...].astype(F32).reshape(1, width)
        G[4 * dp + blk] = TILE[...]
        segment = seg_in[...].astype(F32)
        SEGT[...] = jnp.zeros_like(SEGT)
        SEGT[0:2] = segment
        SEGT[2:4] = jnp.where(pad_in[...] == 1, segment, -1.0)
        SEG[blk] = SEGT[...]
        return (
            swap_parts(lambda b: SEGT, SEG),
            send_all(lambda dev: TILE, G),
        )

    seg_copies, small_copies = small_start()

    def dp_part(slabs):
        return dp_start(lambda i: slabs.at[i], lambda n: slabs.at[pl.ds(c, n)])

    def split_up():
        uw_copy.wait()
        for i in range(DP_SIZE):
            for b in range(BLK_SIZE):
                at = 96 * (BLK_SIZE * i + b)
                UP[i // 4, b, :, 96 * (i % 4) : 96 * (i % 4 + 1)] = UW[:, at : at + 96]

    def split_down():
        dw_copy.wait()
        for n in range(2):
            WDS[n, dp] = DW[:, 384 * n : 384 * (n + 1)]

    received(a_first)
    a_part = dp_part(WJS0)
    split_up()
    received(c_first)
    dp_forward(o_part)
    c_part = dp_part(WJS1)
    u_first = [swap_columns(UP.at[n], WUS.at[n]) for n in range(2)]
    split_down()

    dev_id = lax.broadcasted_iota(jnp.int32, (32, 1, 1), 0).astype(F32)
    blk_f = blk.astype(F32)
    piece24, _ = lane_pieces(768, 24)
    piece48, _ = lane_pieces(192, 48)
    piece96, _ = lane_pieces(768, 96)

    def mask24():
        return piece24[None] == dev_id

    def mask48(first_dev):
        return piece48[None] + (4.0 * blk_f + first_dev) == dev_id

    def mask96():
        return 4.0 * piece96[None] + blk_f == dev_id

    def place24():
        return piece_placer(768, 24)

    def place48():
        return piece_placer(192, 48)

    def place96():
        return piece_placer(768, 96)

    def small_end():
        received(small_copies)
        tiles = G[...].reshape(32 * 8, 128).astype(BF)

        def placed(placer, mask, lanes):
            spread = dot_nn(tiles, placer).reshape(32, 8, lanes)
            return jnp.sum(jnp.where(mask, spread, 0.0), axis=0)

        PV[0:8] = placed(place24(), mask24(), 768)
        PV[8:16] = placed(place96(), mask96(), 768)
        QVB[0:8] = placed(place48(), mask48(0.0), 192)
        QVB[8:16] = placed(place48(), mask48(16.0), 192)

    def segments_end():
        received(seg_copies)
        eye = jnp.where(
            lax.broadcasted_iota(jnp.int32, (128, 128), 0)
            == lax.broadcasted_iota(jnp.int32, (128, 128), 1), 1.0, 0.0,
        ).astype(BF)
        for b in range(BLK_SIZE):
            part = SEG[b]
            KSEG[:, 128 * b : 128 * (b + 1)] = part
            QSEG[128 * b : 128 * (b + 1)] = dot_nt(eye, part.astype(BF))


    dp_forward(a_part)
    received(u_first[0])
    u_part = [dp_part(WUS.at[0])]
    gather_forward(n1_part[0])
    dp_end(o_part)
    wo_x, wo_core = group(), group()
    send(WOS.at[blk], WOS.at[blk], x_peer, wo_x)
    send(WOS.at[blk], WOS.at[blk], core_peer, wo_core)
    later_sent((wo_x, WOS.at[blk]))
    later_sent((wo_core, WOS.at[pl.ds(c, 2)]))
    small_end()
    segments_end()
    gain1, shift1, obias = PV[0:1], PV[1:2], PV[2:3]
    gain2, shift2, dbias = PV[3:4], PV[4:5], PV[5:6]

    def compact(slabs, whole):
        for i in range(DP_SIZE):
            rows = slabs(i).astype(F32)
            rows = rows.reshape(96, rows.shape[-1])
            whole[96 * i : 96 * (i + 1), :] = rows.astype(BF)

    def norm_rows(r):
        gather_end(n1_part[r])
        for copies in n1_sent[r]:
            sent(copies)
        for b in range(BLK_SIZE):
            N1[r, b] = (N1[r, b].astype(F32) * gain1 + shift1).astype(BF)

    def qkv_one(r):
        joint = dot_nn(N1[r].reshape(512, 768), WJ0[...])
        qbias, vbias = QVB[6:7, 0:64], QVB[14:15, 0:64]
        Q[r, 0] = ((joint[:, :64] + qbias).astype(BF).astype(F32) * 0.125).astype(BF)
        K[r, 0] = joint[:, 64:128].astype(BF)
        V[r, 0] = (joint[:, 128:] + vbias).astype(BF)

    def qkv_two(r):
        joint = dot_nn(N1[r].reshape(512, 768), WJ1[...])
        qbias, vbias = QVB[6:7, 64:192], QVB[14:15, 64:192]
        query = ((joint[:, :128] + qbias).astype(BF).astype(F32) * 0.125).astype(BF)
        keys = joint[:, 128:256].astype(BF)
        values = (joint[:, 256:] + vbias).astype(BF)
        for h in (1, 2):
            lanes = slice(64 * (h - 1), 64 * h)
            Q[r, h] = query[:, lanes]
            K[r, h] = keys[:, lanes]
            V[r, h] = values[:, lanes]

    def attend(r, h):
        scores = dot_nt(Q[r, h], K[r, h])
        scores = jnp.where(QSEG[:, r : r + 1] == KSEG[2 + r : 3 + r, :], scores, masked_score)
        top = jnp.max(scores, axis=-1, keepdims=True)
        expos = jnp.exp(scores - top)
        total = jnp.sum(expos, axis=-1, keepdims=True)
        probs = (expos * (1.0 / total)).astype(BF)
        PB[r, h] = probs
        out = dot_nn(probs, V[r, h])
        OF[r, h] = out
        AT[r, :, :, 64 * h : 64 * (h + 1)] = out.astype(BF).reshape(4, 128, 64)

    def swap_heads(src, dst, r):
        dst[r, blk] = src[r, blk]
        return swap_parts(lambda b: src.at[r, b], dst.at[r])

    dp_end(a_part)
    compact(lambda i: WJS0[i], WJ0)
    norm_rows(0)
    qkv_one(0)
    dp_forward(c_part)
    received(u_first[1])
    u_part.append(dp_part(WUS.at[1]))
    attend(0, 0)
    gather_forward(n1_part[1])

    def low_cotangent():
        cot_copy.wait()
        for r in range(2):
            GR[r, blk] = COT[r].astype(BF)

    low_cotangent()
    norm_rows(1)
    qkv_one(1)
    attend(1, 0)
    gr_part = [gather_start(GR, 0)]
    dp_end(c_part)
    compact(lambda i: WJS1[i], WJ1)
    dp_forward(u_part[0])
    d_part = [dp_part(WDS.at[0])]
    qkv_two(0)
    attend(0, 1)
    attend(0, 2)
    at_copies = [swap_heads(AT, AR, 0)]
    received((wo_x, WOS.at[x_peer[1]]))
    send(WOS.at[x_peer[1]], WOS.at[x_peer[1]], core_peer, wo_core)
    qkv_two(1)
    dp_forward(u_part[1])
    d_part.append(dp_part(WDS.at[1]))
    attend(1, 1)
    attend(1, 2)
    at_copies.append(swap_heads(AT, AR, 1))
    received((wo_core, WOS.at[pl.ds(c, 2)]))
    compact(lambda i: WOS[:, i], WO)
    gather_forward(gr_part[0])

    def middle_rows(r):
        received(at_copies[r])
        total = TOK[r] + obias
        for b in range(BLK_SIZE):
            total = total + dot_nn(AR[r, b], WO[192 * b : 192 * (b + 1), :])
        MID[r] = total
        unit, inverse = stats(total)
        U2[r] = unit
        I2[r] = inverse
        N2[r, blk] = (unit * gain2 + shift2).astype(BF)
        return gather_start(N2, r)

    n2_part = [middle_rows(0)]
    gr_part.append(gather_start(GR, 1))
    n2_part.append(middle_rows(1))
    for n in range(2):
        dp_end(u_part[n])
        compact(lambda i: WUS[n, i], WU.at[n])
    dp_forward(d_part[0])
    gather_forward(n2_part[0])
    gather_end(n2_part[0])

    def rows_of(buf, r):
        return buf[r].reshape(512, 768)

    def up(r):
        for n in range(2):
            cols = slice(384 * n, 384 * (n + 1))
            hidden = dot_nn(rows_of(N2, r), WU[n]) + PV[15:16, cols]
            square = hidden * hidden
            bent = jnp.tanh(hidden * (0.7978845608028654 + 0.035677408136300125 * square))
            half = 0.5 * (1.0 + bent)
            ACT[r, :, cols] = (hidden * half).astype(BF)
            slope = 0.3989422804014327 + 0.05351611220445019 * square
            GP[r, :, cols] = (half + hidden * (1.0 - bent * bent) * slope).astype(BF)

    def hidden_back(r):
        for n in range(2):
            cols = slice(384 * n, 384 * (n + 1))
            low, high = (WDS[m, 4 * n : 4 * (n + 1)].reshape(384, 384) for m in range(2))
            rows = rows_of(GR, r)
            grad = dot_nt(rows[:, :384], low) + dot_nt(rows[:, 384:], high)
            grad = (grad * GP[r, :, cols].astype(F32)).astype(BF)
            GH[r, :, cols] = grad
            UBS[r, :, cols] = jnp.sum(grad.astype(F32), axis=0, keepdims=True)

    def sum_store(i, r, cols, values):
        PT[i, r, :, :, :, cols] = values.reshape(2, 2, 128, values.shape[-1]).astype(BF)

    def sum_start(i, r):
        sems = group()
        send(PT.at[i, r, :, 1 - c], RC.at[i, r], core_peer, sems)
        later_sent((sems, RC.at[i, r]))
        return sems, RC.at[i, r]

    def sum_middle(i, r, first):
        received(first)
        SX[i, r] = (PT[i, r, 1 - x, c].astype(F32) + RC[i, r, 1 - x].astype(F32)).astype(BF)
        sems = group()
        send(SX.at[i, r], RX.at[i, r], x_peer, sems)
        later_sent((sems, RX.at[i, r]))
        return sems, RX.at[i, r]

    def sum_end(i, r, second):
        received(second)
        return PT[i, r, x, c].astype(F32) + RC[i, r, x].astype(F32) + RX[i, r].astype(F32)

    def second_back(r):
        for n in range(3):
            cols = slice(256 * n, 256 * (n + 1))
            left, right = GH[r, :, :384], GH[r, :, 384:]
            sum_store(0, r, cols, dot_nt(left, WU[0, cols, :]) + dot_nt(right, WU[1, cols, :]))
        return sum_start(0, r)

    def first_back(r):
        for n in range(3):
            cols = slice(256 * n, 256 * (n + 1))
            sum_store(
                2, r, cols, dot_nt(GJ0[r], WJ0[cols, :]) + dot_nt(GJ1[r], WJ1[cols, :])
            )
        return sum_start(2, r)

    def down(r):
        for n in range(2):
            cols = slice(384 * n, 384 * (n + 1))
            sum_store(1, r, cols, dot_nn(ACT[r], WDS[n].reshape(768, 384)))
        return sum_start(1, r)

    def scatter_start(parts, recv):
        sems = group()
        send(parts.at[:, 1 - y], recv, y_peer, sems)
        later_sent((sems, recv))
        return sems, recv

    def scatter_middle(parts, recv, sums, landing, first):
        received(first)
        sums[...] = (parts[:, y].astype(F32) + recv[...].astype(F32)).astype(BF)
        sems = group()
        for k in range(1, Z_SIZE):
            send(sums.at[z_at(k)], landing.at[k - 1], (2 * z_at(k) + y, blk), sems)
        later_sent((sems, landing))
        return sems, landing

    def scatter_end(sums, landing, second):
        received(second)
        total = sums[z].astype(F32)
        for k in range(Z_SIZE - 1):
            total = total + landing[k].astype(F32)
        return total

    def return_columns(total, sends, recvs):
        sends[...] = total.astype(BF)
        recvs[blk] = sends[blk]
        return swap_parts(lambda b: sends.at[b], recvs)

    def down_grad(n):
        grads = GR[:, :, :, 384 * n : 384 * (n + 1)].reshape(1024, 384)
        for m in range(2):
            cols = slice(384 * m, 384 * (m + 1))
            grad = dot_tn(ACT[:, :, cols].reshape(1024, 384), grads)
            GD[n, 2 * m : 2 * m + 2] = grad.reshape(2, 2, 96, 384).astype(BF)
        return scatter_start(GD.at[n], RYd.at[n])

    def row_grad(rows, grads, parts):
        for m in range(2):
            cols = slice(384 * m, 384 * (m + 1))
            grad = dot_tn(rows[:, :, :, cols].reshape(1024, 384), grads)
            parts[2 * m : 2 * m + 2] = grad.reshape(2, 2, 4, 24, grad.shape[-1]).astype(BF)

    def up_grad(n):
        row_grad(N2, GH[:, :, 384 * n : 384 * (n + 1)].reshape(1024, 384), GU.at[n])

    def joint_grad_one():
        row_grad(N1, GJ0[...].reshape(1024, 192), GA)
        return scatter_start(GA, RYa)

    def joint_grad_two():
        row_grad(N1, GJ1[...].reshape(1024, 384), GC)
        return scatter_start(GC, RYc)

    def output_grad():
        for b in range(BLK_SIZE):
            grad = dot_tn(AR[:, b].reshape(256, 192), GB[...].reshape(256, 768))
            grad = grad.reshape(2, 4, 24, 768).astype(BF)
            for i in range(4):
                GO[i // 2, i % 2, 2 * b : 2 * b + 2] = grad[:, i]
        sems = group()
        send(GO.at[:, 1 - c], RCo, core_peer, sems)
        later_sent((sems, RCo))
        return sems, RCo

    def output_grad_middle(first):
        received(first)
        SXo[...] = (GO[1 - x, c].astype(F32) + RCo[1 - x].astype(F32)).astype(BF)
        sems = group()
        send(SXo, RXo, x_peer, sems)
        later_sent((sems, RXo))
        return sems, RXo

    def norm_back(e, unit, inverse, gain):
        f = e * gain
        grad = inverse * (
            f - jnp.mean(f, axis=-1, keepdims=True)
            - unit * jnp.mean(f * unit, axis=-1, keepdims=True)
        )
        return (
            grad, jnp.sum(e * unit, axis=0, keepdims=True), jnp.sum(e, axis=0, keepdims=True)
        )

    def second_norm_back(r, second):
        e = sum_end(0, r, second)
        grad, of_gain, of_shift = norm_back(e, U2[r], I2[r], gain2)
        grad = grad + COT[r]
        GM[r] = grad
        low = grad.astype(BF)
        GB[r] = low
        for b in range(BLK_SIZE):
            DA[r, b] = dot_nt(low, WO[192 * b : 192 * (b + 1), :]).astype(BF)
        copies = swap_heads(DA, DR, r)
        VS[3:4] += of_gain
        VS[4:5] += of_shift
        VS[2:3] += jnp.sum(low.astype(F32), axis=0, keepdims=True)
        VS[5:6] += jnp.sum(COT[r].astype(BF).astype(F32), axis=0, keepdims=True)
        return copies

    def attend_back(r, h):
        grad_out = DR[r, :, :, 64 * h : 64 * (h + 1)].reshape(512, 64)
        DOH[...] = grad_out
        grad_out = DOH[...]
        delta = jnp.sum(grad_out.astype(F32) * OF[r, h], axis=-1, keepdims=True)
        grad_probs = dot_nt(grad_out, V[r, h])
        grad_scores = (PB[r, h].astype(F32) * (grad_probs - delta)).astype(BF)
        grads = (
            (dot_nn(grad_scores, K[r, h]) * 0.125).astype(BF),
            dot_tn(grad_scores, Q[r, h]).astype(BF),
            dot_tn(PB[r, h], grad_out).astype(BF),
        )
        for s, grad in enumerate(grads):
            if h == 0:
                GJ0[r, :, 64 * s : 64 * (s + 1)] = grad
            else:
                at = 128 * s + 64 * (h - 1)
                GJ1[r, :, at : at + 64] = grad

    def output_grad_over_dp(second):
        received(second)
        GO2[...] = (
            GO[x, c].astype(F32) + RCo[x].astype(F32) + RXo[...].astype(F32)
        ).astype(BF).reshape(4, 2, 24, 768)
        return scatter_start(GO2, RYo)

    def vector_sums():
        for r in range(2):
            JBS[r, :, 0:192] = jnp.sum(GJ0[r].astype(F32), axis=0, keepdims=True)
            JBS[r, :, 192:576] = jnp.sum(GJ1[r].astype(F32), axis=0, keepdims=True)

    def first_norm_back(r, second):
        e = sum_end(2, r, second)
        grad, of_gain, of_shift = norm_back(e, U1[r], I1[r], gain1)
        GM[r] = GM[r] + grad
        VS[0:1] += of_gain
        VS[1:2] += of_shift

    VS[...] = jnp.zeros_like(VS)
    up(0)
    gather_forward(n2_part[1])
    dp_forward(d_part[1])
    gather_end(n2_part[1])
    up(1)
    gather_forward(gr_part[1])
    gather_end(gr_part[0])
    gather_end(gr_part[1])
    d_first = [down_grad(0)]
    dp_end(d_part[0])
    dp_end(d_part[1])
    hidden_back(0)
    second_first = [second_back(0)]
    d_first.append(down_grad(1))
    hidden_back(1)
    second_second = [sum_middle(0, 0, second_first[0])]
    second_first.append(second_back(1))
    up_grad(0)
    second_second.append(sum_middle(0, 1, second_first[1]))
    d_second = [scatter_middle(GD.at[0], RYd.at[0], Sd.at[0], RZd.at[0], d_first[0])]
    u_grad_first = [scatter_start(GU.at[0], RYu.at[0])]
    result_first = [down(0)]
    up_grad(1)
    result_second = [sum_middle(1, 0, result_first[0])]
    da_copies = [second_norm_back(0, second_second[0])]
    d_second.append(scatter_middle(GD.at[1], RYd.at[1], Sd.at[1], RZd.at[1], d_first[1]))
    u_grad_first.append(scatter_start(GU.at[1], RYu.at[1]))
    result_first.append(down(1))
    da_copies.append(second_norm_back(1, second_second[1]))
    o_first = output_grad()
    received(da_copies[0])
    for h in (1, 2, 0):
        attend_back(0, h)
    u_grad_second = [scatter_middle(GU.at[0], RYu.at[0], Su.at[0], RZu.at[0], u_grad_first[0])]
    first_first = [first_back(0)]
    o_second = output_grad_middle(o_first)
    received(da_copies[1])
    attend_back(1, 1)
    attend_back(1, 2)
    c_grad_first = joint_grad_two()
    first_second = [sum_middle(2, 0, first_first[0])]
    attend_back(1, 0)
    first_first.append(first_back(1))
    a_grad_first = joint_grad_one()
    u_grad_second.append(scatter_middle(GU.at[1], RYu.at[1], Su.at[1], RZu.at[1], u_grad_first[1]))
    first_second.append(sum_middle(2, 1, first_first[1]))
    o_grad_first = output_grad_over_dp(o_second)
    result_second.append(sum_middle(1, 1, result_first[1]))
    vector_sums()
    out_copies = []

    def down_out():
        for n in range(2):
            OD[:, 384 * n : 384 * (n + 1)] = scatter_end(Sd.at[n], RZd.at[n], d_second[n])
        out_copies.append(local(OD, out_d))

    down_out()
    first_norm_back(0, first_second[0])
    c_grad_second = scatter_middle(GC, RYc, Sc, RZc, c_grad_first)
    first_norm_back(1, first_second[1])
    out_copies.append(local(GM, grad_tok_out))

    def vectors_start():
        row = lax.broadcasted_iota(jnp.int32, (8, 1), 0)

        def picked(values, mask, placer):
            wide = jnp.where(mask, values[None], 0.0)
            wide = wide.reshape(256, wide.shape[-1])
            high = wide.astype(BF)
            rest = (wide - high.astype(F32)).astype(BF)
            return dot_nt(high, placer) + dot_nt(rest, placer)

        joint = JBS[0] + JBS[1]
        queries = jnp.concatenate([joint[:, 0:64], joint[:, 192:320]], axis=1)
        values = jnp.concatenate([joint[:, 128:192], joint[:, 448:576]], axis=1)
        pieces = picked(VS[...], mask24(), place24())
        pieces += picked(jnp.where(row == 7, UBS[0] + UBS[1], 0.0), mask96(), place96())
        pieces += picked(jnp.where(row == 6, queries, 0.0), mask48(0.0), place48())
        pieces += picked(jnp.where(row == 6, values, 0.0), mask48(16.0), place48())
        TS[...] = pieces.reshape(32, 8, 128)
        TR[4 * dp + blk] = TS[4 * dp + blk]
        return send_all(lambda dev: TS.at[4 * dev[0] + dev[1]], TR)

    vector_copies = vectors_start()
    a_grad_second = scatter_middle(GA, RYa, Sa, RZa, a_grad_first)
    u_back = [
        return_columns(scatter_end(Su.at[n], RZu.at[n], u_grad_second[n]), AUs.at[n], AUr.at[n])
        for n in range(2)
    ]
    o_grad_second = scatter_middle(GO2, RYo, So, RZo, o_grad_first)

    def result_end():
        for r in range(2):
            MID[r] = MID[r] + sum_end(1, r, result_second[r]) + dbias
        out_copies.append(local(MID, result_out))

    result_end()
    c_back = return_columns(scatter_end(Sc, RZc, c_grad_second), ACs, ACr)
    a_back = return_columns(scatter_end(Sa, RZa, a_grad_second), AAs, AAr)

    def up_out():
        for n in range(2):
            received(u_back[n])
            for b in range(BLK_SIZE):
                part = AUr[n, b].astype(F32)
                for i in range(4):
                    at = 96 * (BLK_SIZE * (4 * n + i) + b)
                    OU[:, at : at + 96] = part[:, 96 * i : 96 * (i + 1)]
        return local(OU, out_u)

    out_copies.append(up_out())
    OO[...] = scatter_end(So, RZo, o_grad_second)
    out_copies.append(local(OO, out_o))
    received(vector_copies)
    OS[...] = jnp.sum(TR[...], axis=0)
    out_copies.append(local(OS, out_s))

    def joint_out():
        received(c_back)
        received(a_back)
        for b in range(BLK_SIZE):
            one, two = AAr[b].astype(F32), ACr[b].astype(F32)
            for s in range(3):
                at = 768 * s + 192 * b
                OJ[:, at : at + 64] = one[:, 64 * s : 64 * (s + 1)]
                OJ[:, at + 64 : at + 192] = two[:, 128 * s : 128 * (s + 1)]
        return local(OJ, out_j)

    out_copies.append(joint_out())
    for copies in started:
        sent(copies)
    for made in out_copies:
        made.wait()


def finish_kernel(*refs):
    big_in, sums, big_out, small_out = refs[:6], refs[6], refs[7:13], refs[13:21]
    for source, target in zip(big_in, big_out):
        target[...] = source[...]
    for row, width in enumerate(TILE_WIDTHS):
        small_out[row][...] = sums[row, 0:width]


def fast_device(
    tokens, segment_ids, pad_mask, joint_weight, joint_bias, output_weight, output_bias,
    first_gain, first_shift, up_weight, up_bias, down_weight, down_bias,
    second_gain, second_shift, cotangent,
):
    vectors = (
        first_gain, first_shift, output_bias, second_gain, second_shift, down_bias,
        joint_bias, up_bias,
    )

    def vm(*shape, dtype=BF):
        return pltpu.VMEM(shape, dtype)

    def fm(*shape):
        return pltpu.VMEM(shape, F32)

    scratch = [
        fm(2, 128, 768), fm(2, 128, 768), vm(24, 2304), vm(24, 3072), vm(96, 768),
        vm(4, 24, 192), vm(4, 24, 384), vm(2, 4, 24, 384), fm(8, 128), fm(8, 128), fm(32, 8, 128),
        fm(4, 8, 128), fm(8, 512), fm(512, 8), fm(16, 768), fm(16, 192),
        vm(2, 4, 128, 768), vm(2, 4, 128, 768), vm(2, 4, 128, 768),
        vm(8, 4, 24, 192), vm(8, 4, 24, 384), vm(2, 8, 4, 24, 384), vm(2, 8, 96, 384),
        vm(4, 8, 24, 768), vm(768, 192), vm(768, 384), vm(2, 768, 384), vm(768, 768),
        fm(2, 128, 768), fm(2, 128, 1), fm(2, 128, 768), fm(2, 128, 1),
        fm(2, 128, 768), fm(2, 128, 768), vm(2, 128, 768),
        vm(2, 3, 512, 64), vm(2, 3, 512, 64), vm(2, 3, 512, 64), vm(2, 3, 512, 512),
        fm(2, 3, 512, 64), vm(2, 4, 128, 192), vm(2, 4, 128, 192),
        vm(2, 4, 128, 192), vm(2, 4, 128, 192), vm(512, 64), vm(2, 512, 192), vm(2, 512, 384),
        vm(2, 512, 768), vm(2, 512, 768), vm(2, 512, 768), fm(2, 1, 768),
        vm(3, 2, 2, 2, 128, 768), vm(3, 2, 2, 128, 768), vm(3, 2, 128, 768), vm(3, 2, 128, 768),
        vm(2, 4, 2, 96, 384), vm(2, 4, 2, 4, 24, 384), vm(4, 2, 4, 24, 192), vm(4, 2, 4, 24, 384),
        vm(2, 2, 8, 24, 768), vm(4, 2, 24, 768),
        vm(2, 4, 96, 384), vm(2, 4, 4, 24, 384), vm(4, 4, 24, 192), vm(4, 4, 24, 384), vm(4, 24, 768),
        vm(2, 4, 96, 384), vm(2, 4, 4, 24, 384), vm(4, 4, 24, 192), vm(4, 4, 24, 384), vm(4, 24, 768),
        vm(2, 3, 96, 384), vm(2, 3, 4, 24, 384), vm(3, 4, 24, 192), vm(3, 4, 24, 384), vm(3, 24, 768),
        vm(2, 4, 24, 384), vm(2, 4, 24, 384), vm(4, 24, 192), vm(4, 24, 192),
        vm(4, 24, 384), vm(4, 24, 384), vm(2, 8, 24, 768), vm(8, 24, 768), vm(8, 24, 768),
        fm(32, 8, 128), fm(32, 8, 128), fm(8, 768), fm(2, 1, 576),
        fm(24, 2304), fm(24, 3072), fm(96, 768), fm(24, 768), fm(8, 128),
        pltpu.SemaphoreType.DMA((COPIES,)), pltpu.SemaphoreType.DMA((COPIES,)),
        pltpu.SemaphoreType.DMA((16,)),
    ]
    vmem = pl.BlockSpec(memory_space=pltpu.VMEM)
    anywhere = pl.BlockSpec(memory_space=pl.ANY)
    out_shapes = [
        (2, 128, 768), (2, 128, 768), (24, 2304), (24, 768), (24, 3072), (96, 768), (8, 128),
    ]
    made = pl.pallas_call(
        layer_kernel,
        out_shape=[jax.ShapeDtypeStruct(shape, F32) for shape in out_shapes],
        in_specs=[anywhere] * 2 + [vmem] * 2 + [anywhere] * 4 + [vmem] * 8,
        out_specs=[anywhere] * 7,
        scratch_shapes=scratch,
        compiler_params=pltpu.CompilerParams(
            collective_id=0, has_side_effects=True, vmem_limit_bytes=VMEM_MIB * 2**20
        ),
        cost_estimate=pl.CostEstimate(
            flops=13 * 10**9, bytes_accessed=6 * 10**6, transcendentals=4 * 10**6
        ),
    )(
        tokens, cotangent, segment_ids, pad_mask, joint_weight, up_weight, down_weight,
        output_weight, *vectors,
    )
    ends = pl.pallas_call(
        finish_kernel,
        out_shape=[jax.ShapeDtypeStruct(shape, F32) for shape in out_shapes[:6]]
        + [jax.ShapeDtypeStruct((width,), F32) for width in TILE_WIDTHS],
        in_specs=[vmem] * 7,
        out_specs=[vmem] * 14,
    )(*made)
    result, grad_tokens, grad_j, grad_o, grad_u, grad_d = ends[:6]
    first_g, first_s, output_b, second_g, second_s, down_b, joint_b, up_b = ends[6:]
    return (
        result, grad_tokens, grad_j, joint_b, grad_o, output_b, first_g, first_s,
        grad_u, up_b, grad_d, down_b, second_g, second_s,
    )


def solution(mesh):
    placed = (
        P("dp", "blk", None),
        P("dp", "blk"),
        P("dp", "blk"),
        P(("dp", "blk"), None),
        P(("dp", "blk")),
        P(("dp", "blk"), None),
        P(("dp", "blk")),
        P(("dp", "blk")),
        P(("dp", "blk")),
        P(("dp", "blk"), None),
        P(("dp", "blk")),
        P(("dp", "blk"), None),
        P(("dp", "blk")),
        P(("dp", "blk")),
        P(("dp", "blk")),
        P("dp", "blk", None),
    )

    def spread(device_part):
        return jax.shard_map(
            device_part,
            mesh=mesh,
            in_specs=placed,
            out_specs=(
                P("dp", "blk", None),
                P("dp", "blk", None),
                P(("dp", "blk"), None),
                P(("dp", "blk")),
                P(("dp", "blk"), None),
                P(("dp", "blk")),
                P(("dp", "blk")),
                P(("dp", "blk")),
                P(("dp", "blk"), None),
                P(("dp", "blk")),
                P(("dp", "blk"), None),
                P(("dp", "blk")),
                P(("dp", "blk")),
                P(("dp", "blk")),
            ),
            check_vma=False,
        )

    def layer(*arrays):
        rows, length, features = arrays[0].shape
        shape = dict(mesh.shape)
        fits = (
            shape == {"dp": DP_SIZE, "blk": BLK_SIZE}
            and (rows, length, features) == (2 * shape["dp"], 512, 768)
            and arrays[9].shape[1] == 3072
        )
        return spread(fast_device if fits else per_device)(*arrays)

    return layer
```

```python
import jax
import jax.numpy as jnp
from jax import lax
from jax.experimental import pallas as pl
from jax.experimental.pallas import tpu as pltpu
from jax.sharding import PartitionSpec as P

HEADS = 12
COPIES = 140
VMEM_MIB = 60


epsilon = 1e-05
masked_score = -1e30


def normalize(values_in, gain, shift):
    centered = values_in - jnp.mean(values_in, axis=-1, keepdims=True)
    inverse = lax.rsqrt(jnp.mean(centered * centered, axis=-1, keepdims=True) + epsilon)
    unit_rows = centered * inverse
    return (unit_rows * gain + shift, unit_rows, inverse)


def normalize_back(grad_normed, unit_rows, inverse, gain):
    scaled = grad_normed * gain
    grad_input = inverse * (
        scaled
        - jnp.mean(scaled, axis=-1, keepdims=True)
        - unit_rows * jnp.mean(scaled * unit_rows, axis=-1, keepdims=True)
    )
    return (
        grad_input,
        jnp.sum(grad_normed * unit_rows, axis=(0, 1)),
        jnp.sum(grad_normed, axis=(0, 1)),
    )


def project(activation, weight):
    return jnp.einsum("rcd,dn->rcn", activation, weight, preferred_element_type=jnp.float32)


def project_back(gradient, weight):
    return jnp.einsum("rcn,dn->rcd", gradient, weight, preferred_element_type=jnp.float32)


def outer_sum(activation, gradient):
    return jnp.einsum("rcd,rcn->dn", activation, gradient, preferred_element_type=jnp.float32)


def split_heads(matrix, head_count):
    return matrix.reshape(
        matrix.shape[0], matrix.shape[1], head_count, matrix.shape[2] // head_count
    )


def masked_scores(query_heads, key_heads, query_segment, key_segment, scaling):
    raw_scores = (
        jnp.einsum("rqhd,rkhd->rhqk", query_heads, key_heads, preferred_element_type=jnp.float32)
        * scaling
    )
    allowed = (query_segment[:, :, None] == key_segment[:, None, :])[:, None]
    return (jnp.where(allowed, raw_scores, masked_score), allowed)


def column_sums(gradient):
    return jnp.sum(gradient.astype(jnp.float32), axis=(0, 1))


def scatter_sum(gradient):
    summed = lax.psum_scatter(
        gradient.astype(jnp.bfloat16), ("dp", "blk"), scatter_dimension=0, tiled=True
    )
    return summed.astype(jnp.float32)


def per_device(
    tokens,
    segment_ids,
    pad_mask,
    joint_weight,
    joint_bias,
    output_weight,
    output_bias,
    first_gain,
    first_shift,
    up_weight,
    up_bias,
    down_weight,
    down_bias,
    second_gain,
    second_shift,
    cotangent,
):
    batch_rows, local_len, features = tokens.shape
    head_count = HEADS
    head_size = features // head_count
    scaling = head_size ** (-0.5)
    device_count = lax.axis_size("dp") * lax.axis_size("blk")
    small_parts = (
        joint_bias, output_bias, first_gain, first_shift, up_bias, down_bias, second_gain, second_shift
    )
    small_all = lax.all_gather(jnp.concatenate(small_parts), ("dp", "blk"), axis=0, tiled=True)
    small_all = small_all.reshape(device_count, -1)
    small_full = []
    small_at = 0
    for part in small_parts:
        small_full.append(small_all[:, small_at : small_at + part.shape[0]].reshape(-1))
        small_at += part.shape[0]
    full_joint_bias, full_output_bias, gain_one, shift_one = small_full[:4]
    full_up_bias, full_down_bias, gain_two, shift_two = small_full[4:]
    full_joint = lax.all_gather(joint_weight, ("dp", "blk"), axis=0, tiled=True)
    full_output = lax.all_gather(output_weight, ("dp", "blk"), axis=0, tiled=True)
    normed_one, unit_one, inverse_one = normalize(
        tokens, gain_one.astype(jnp.float32), shift_one.astype(jnp.float32)
    )
    normed_one_low = normed_one.astype(jnp.bfloat16)
    joint = project(normed_one_low, full_joint)
    bias_values = full_joint_bias.astype(jnp.float32)
    query = (joint[..., :features] + bias_values[:features]).astype(jnp.bfloat16)
    keys = joint[..., features : 2 * features].astype(jnp.bfloat16)
    values = (joint[..., 2 * features :] + bias_values[features:]).astype(jnp.bfloat16)
    key_segment = jnp.where(pad_mask == 1, segment_ids, -1)
    query_heads = split_heads(query, head_count)
    top_score = jnp.full((batch_rows, head_count, local_len), masked_score, jnp.float32)
    key_portion = lax.all_gather(keys, "blk", axis=1, tiled=True)
    value_portion = lax.all_gather(values, "blk", axis=1, tiled=True)
    segment_portion = lax.all_gather(key_segment, "blk", axis=1, tiled=True)
    scores, allowed = masked_scores(
        query_heads, split_heads(key_portion, head_count), segment_ids, segment_portion, scaling
    )
    new_top = jnp.maximum(top_score, jnp.max(scores, axis=-1))
    weights = jnp.where(allowed, jnp.exp(scores - new_top[..., None]), 0.0)
    total_weight = jnp.sum(weights, axis=-1)
    weighted = jnp.einsum(
        "rhqk,rkhd->rhqd",
        weights.astype(jnp.bfloat16),
        split_heads(value_portion, head_count),
        preferred_element_type=jnp.float32,
    )
    top_score, total_weight, weighted = (new_top, total_weight, weighted)
    log_total = top_score + jnp.log(total_weight)
    attended_heads = weighted / total_weight[..., None]
    attended = jnp.transpose(attended_heads, (0, 2, 1, 3)).reshape(batch_rows, local_len, features)
    attended_low = attended.astype(jnp.bfloat16)
    middle = tokens + project(attended_low, full_output) + full_output_bias.astype(jnp.float32)
    full_up = lax.all_gather(up_weight, ("dp", "blk"), axis=0, tiled=True)
    full_down = lax.all_gather(down_weight, ("dp", "blk"), axis=0, tiled=True)
    normed_two, unit_two, inverse_two = normalize(
        middle, gain_two.astype(jnp.float32), shift_two.astype(jnp.float32)
    )
    normed_two_low = normed_two.astype(jnp.bfloat16)
    hidden = project(normed_two_low, full_up) + full_up_bias.astype(jnp.float32)
    activated, gelu_pullback = jax.vjp(jax.nn.gelu, hidden)
    activated_low = activated.astype(jnp.bfloat16)
    result = middle + project(activated_low, full_down) + full_down_bias.astype(jnp.float32)
    later_up, later_down, later_gain_two = full_up, full_down, gain_two
    grad_result = cotangent.astype(jnp.bfloat16)
    grad_down_weight = outer_sum(activated_low, grad_result)
    grad_down_bias = column_sums(grad_result)
    grad_activated = project_back(grad_result, later_down)
    grad_hidden = gelu_pullback(grad_activated)[0].astype(jnp.bfloat16)
    grad_up_bias = column_sums(grad_hidden)
    grad_up_weight = outer_sum(normed_two_low, grad_hidden)
    grad_normed_two = project_back(grad_hidden, later_up)
    grad_from_second, grad_gain_two, grad_shift_two = normalize_back(
        grad_normed_two, unit_two, inverse_two, later_gain_two.astype(jnp.float32)
    )
    grad_middle = cotangent + grad_from_second
    grad_up_shard = scatter_sum(grad_up_weight)
    grad_down_shard = scatter_sum(grad_down_weight)
    later_joint, later_output, later_gain_one = full_joint, full_output, gain_one
    grad_branch = grad_middle.astype(jnp.bfloat16)
    grad_output_weight = outer_sum(attended_low, grad_branch)
    grad_output_bias = column_sums(grad_branch)
    grad_attended = project_back(grad_branch, later_output).astype(jnp.bfloat16)
    grad_heads = split_heads(grad_attended, head_count)
    delta = jnp.einsum("rqhd,rhqd->rhq", grad_heads.astype(jnp.float32), attended_heads)
    key_heads = split_heads(key_portion, head_count)
    scores, allowed = masked_scores(query_heads, key_heads, segment_ids, segment_portion, scaling)
    probs = jnp.where(allowed, jnp.exp(scores - log_total[..., None]), 0.0)
    grad_probs = jnp.einsum(
        "rqhd,rkhd->rhqk",
        grad_heads,
        split_heads(value_portion, head_count),
        preferred_element_type=jnp.float32,
    )
    grad_scores = (probs * (grad_probs - delta[..., None])).astype(jnp.bfloat16)
    grad_query = scaling * jnp.einsum(
        "rhqk,rkhd->rqhd", grad_scores, key_heads, preferred_element_type=jnp.float32
    )
    every_total, every_delta = (
        lax.all_gather(log_total, "blk", axis=2, tiled=True),
        lax.all_gather(delta, "blk", axis=2, tiled=True),
    )
    own_keys = split_heads(keys, head_count)
    own_values = split_heads(values, head_count)
    query_portion = lax.all_gather(query, "blk", axis=1, tiled=True)
    grad_portion = lax.all_gather(grad_attended, "blk", axis=1, tiled=True)
    segment_portion = lax.all_gather(segment_ids, "blk", axis=1, tiled=True)
    portion_queries = split_heads(query_portion, head_count)
    portion_grads = split_heads(grad_portion, head_count)
    scores, allowed = masked_scores(
        portion_queries, own_keys, segment_portion, key_segment, scaling
    )
    probs = jnp.where(allowed, jnp.exp(scores - every_total[..., None]), 0.0)
    grad_values = jnp.einsum(
        "rhqk,rqhd->rkhd",
        probs.astype(jnp.bfloat16),
        portion_grads,
        preferred_element_type=jnp.float32,
    )
    grad_probs = jnp.einsum(
        "rqhd,rkhd->rhqk", portion_grads, own_values, preferred_element_type=jnp.float32
    )
    grad_scores = (probs * (grad_probs - every_delta[..., None])).astype(jnp.bfloat16)
    grad_keys = scaling * jnp.einsum(
        "rhqk,rqhd->rkhd", grad_scores, portion_queries, preferred_element_type=jnp.float32
    )
    grad_keys, grad_values = (grad_keys, grad_values)
    grad_joint = jnp.concatenate(
        [
            grad_query.reshape(batch_rows, local_len, features),
            grad_keys.reshape(batch_rows, local_len, features),
            grad_values.reshape(batch_rows, local_len, features),
        ],
        axis=-1,
    ).astype(jnp.bfloat16)
    grad_joint_weight = outer_sum(normed_one_low, grad_joint)
    grad_joint_bias = jnp.concatenate(
        [column_sums(grad_joint[..., :features]), column_sums(grad_joint[..., 2 * features :])]
    )
    grad_normed_one = project_back(grad_joint, later_joint)
    grad_from_first, grad_gain_one, grad_shift_one = normalize_back(
        grad_normed_one, unit_one, inverse_one, later_gain_one.astype(jnp.float32)
    )
    grad_tokens = grad_middle + grad_from_first
    small_grads = (
        grad_joint_bias, grad_output_bias, grad_gain_one, grad_shift_one,
        grad_up_bias, grad_down_bias, grad_gain_two, grad_shift_two,
    )
    packed = jnp.concatenate([part.reshape(device_count, -1) for part in small_grads], axis=1)
    own = lax.psum_scatter(packed, ("dp", "blk"), scatter_dimension=0, tiled=True)[0]
    small_shards = []
    small_at = 0
    for part in small_parts:
        small_shards.append(own[small_at : small_at + part.shape[0]])
        small_at += part.shape[0]
    return (
        result,
        grad_tokens,
        scatter_sum(grad_joint_weight),
        small_shards[0],
        scatter_sum(grad_output_weight),
        small_shards[1],
        small_shards[2],
        small_shards[3],
        grad_up_shard,
        small_shards[4],
        grad_down_shard,
        small_shards[5],
        small_shards[6],
        small_shards[7],
    )


Z_SIZE, Y_SIZE, BLK_SIZE = 4, 2, 4
DP_SIZE = Z_SIZE * Y_SIZE
MESH = pl.DeviceIdType.MESH
BF = jnp.bfloat16
F32 = jnp.float32
WIDE, CHUNKS = 256, 3
TILE_WIDTHS = (24, 24, 24, 24, 24, 24, 48, 96)


def dot_nn(left, right):
    return lax.dot_general(left, right, (((1,), (0,)), ((), ())), preferred_element_type=F32)


def dot_nt(left, right):
    return lax.dot_general(left, right, (((1,), (1,)), ((), ())), preferred_element_type=F32)


def dot_tn(left, right):
    return lax.dot_general(left, right, (((0,), (0,)), ((), ())), preferred_element_type=F32)


def lane_pieces(lanes, width):
    lane = lax.broadcasted_iota(jnp.int32, (1, lanes), 1).astype(F32)
    piece = jnp.floor((lane + 0.5) * (1.0 / width))
    return piece, lane - width * piece


def piece_placer(lanes, width):
    place = lax.broadcasted_iota(jnp.int32, (128, lanes), 0).astype(F32)
    _, within = lane_pieces(lanes, width)
    return jnp.where(place == within, 1.0, 0.0).astype(BF)


def layer_kernel(*refs):
    ins, outs, scr = refs[:16], refs[16:23], refs[23:]
    (tok_in, cot_in, seg_in, pad_in, jw_in, uw_in, dw_in, ow_in), vectors = ins[:8], ins[8:]
    result_out, grad_tok_out, out_j, out_o, out_u, out_d, out_s = outs
    (
        TOK, COT, JW, UW, DW, JP0, JP1, UPW, UP, TILE, SEGT, G, SEG, KSEG, QSEG, PV, QVB,
        N1, N2, GR, WJS0, WJS1, WUS, WDS, WOS, WJ0, WJ1, WU, WO,
        U1, I1, U2, I2, MID, GM, GB,
        Q, K, V, PB, OF, AT, AR, DA, DR, DOH, GJ0, GJ1,
        GP, ACT, GH, UBS, PT, RC, SX, RX,
        GD, GU, GA, GC, GO, GO2, RYd, RYu, RYa, RYc, RYo, Sd, Su, Sa, Sc, So,
        RZd, RZu, RZa, RZc, RZo, AUs, AUr, AAs, AAr, ACs, ACr, RCo, SXo, RXo,
        TS, TR, VS, JBS, OJ, OU, OD, OO, OS, ssem, rsem, lsem,
    ) = scr
    dp = lax.axis_index("dp")
    blk = lax.axis_index("blk")
    z, y = dp // 2, dp % 2
    x, c = blk // 2, blk % 2
    count = [0, 0]
    started = []

    def local(src, dst):
        n = count[1]
        count[1] += 1
        made = pltpu.make_async_copy(src, dst, lsem.at[n])
        made.start()
        return made

    def group():
        n = count[0]
        count[0] += 1
        return ssem.at[n], rsem.at[n]

    def send(src, dst, dev, sems):
        made = pltpu.make_async_remote_copy(
            src_ref=src, dst_ref=dst, send_sem=sems[0], recv_sem=sems[1],
            device_id=dev, device_id_type=MESH,
        )
        made.start()
        return made

    def wait_bytes(sem, ref):
        pltpu.make_async_copy(ref, ref, sem).wait()

    def received(copies):
        wait_bytes(copies[0][1], copies[1])

    def later_sent(copies):
        started.append(copies)

    def sent(copies):
        wait_bytes(copies[0][0], copies[1])

    started_over_z = []

    def later_sent_over_z(copies):
        started_over_z.append(copies)

    core_peer = (dp, 2 * x + 1 - c)
    x_peer = (dp, 2 * (1 - x) + c)
    far_peer = (dp, 2 * (1 - x) + 1 - c)
    blk_peers = (x_peer, far_peer, core_peer)
    y_peer = (2 * z + 1 - y, blk)
    inner = (z == 1) | (z == 2)
    z_left = (2 * ((z + Z_SIZE - 1) % Z_SIZE) + y, blk)
    z_right = (2 * ((z + 1) % Z_SIZE) + y, blk)
    z_side = (2 * ((z // 2) * 2 + 1 - z % 2) + y, blk)
    z_across = (2 * (Z_SIZE - 1 - z) + y, blk)

    def z_at(k):
        return (z + k) % Z_SIZE

    ow_copy = local(ow_in, WOS.at[blk, dp])
    jw_copy = local(jw_in, JW)
    tok_copy = local(tok_in, TOK)
    uw_copy = local(uw_in, UW)
    dw_copy = local(dw_in, DW)
    cot_copy = local(cot_in, COT)

    every = [
        ((dp + i) % DP_SIZE, (blk + j) % BLK_SIZE)
        for i in range(DP_SIZE) for j in range(BLK_SIZE) if i or j
    ]

    def entry_barrier():
        barrier = pltpu.get_barrier_semaphore()
        for dev in every:
            pl.semaphore_signal(barrier, inc=1, device_id=dev, device_id_type=MESH)
        pl.semaphore_wait(barrier, len(every))

    def swap_parts(parts, landing):
        sems = group()
        for dev in blk_peers:
            send(parts(dev[1]), landing.at[blk], dev, sems)
        span = landing.at[pl.ds(c, 3)]
        later_sent((sems, span))
        return sems, span

    def send_all(src, landing):
        sems = group()
        for dev in every:
            send(src(dev), landing.at[4 * dp + blk], dev, sems)
        span = landing.at[pl.ds(c, 31)]
        later_sent((sems, span))
        return sems, span

    def small_tiles():
        TILE[...] = jnp.zeros_like(TILE)
        for row, (ref, width) in enumerate(zip(vectors, TILE_WIDTHS)):
            TILE[row : row + 1, 0:width] = ref[...].astype(F32).reshape(1, width)
        segment = seg_in[...].astype(F32)
        SEGT[...] = jnp.zeros_like(SEGT)
        SEGT[0:2] = segment
        SEGT[2:4] = jnp.where(pad_in[...] == 1, segment, -1.0)
        G[dp, blk] = TILE[...]
        SEG[blk] = SEGT[...]


    small_tiles()
    entry_barrier()

    def stats(values):
        mean = jnp.mean(values, axis=-1, keepdims=True)
        centered = values - mean
        inverse = lax.rsqrt(jnp.mean(centered * centered, axis=-1, keepdims=True) + epsilon)
        return centered * inverse, inverse

    def dp_part(slab, span):
        return slab, span, [group() for _ in range(5)]

    def slabs_part(slabs):
        return dp_part(lambda i: slabs.at[i], lambda n: slabs.at[pl.ds(c, n)])

    def own_over_y(part):
        slab, span, sems = part
        send(slab(dp), slab(dp), y_peer, sems[0])
        later_sent((sems[0], span(4)))

    def own_over_z(part):
        slab, span, sems = part

        @pl.when(z < Z_SIZE - 1)
        def _():
            send(slab(dp), slab(dp), z_right, (sems[1][0], sems[1][1]))

        @pl.when(z > 0)
        def _():
            send(slab(dp), slab(dp), z_left, (sems[1][0], sems[2][1]))

        later_sent_over_z((sems[1], span(1), span(5)))

    def pass_on(part, there, arrived, onward, more, dev):
        slab, _, sems = part
        received((arrived, slab(there)))
        send(slab(there), slab(there), y_peer, sems[0])
        if onward is not None:

            @pl.when(more)
            def _():
                send(slab(there), slab(there), dev, (sems[1][0], onward[1]))

    def step_one(part):
        sems = part[2]

        @pl.when(z > 0)
        def _():
            pass_on(part, dp - 2, sems[1], sems[3], z < Z_SIZE - 1, z_right)

        @pl.when(z < Z_SIZE - 1)
        def _():
            pass_on(part, dp + 2, sems[2], sems[3], z > 0, z_left)

    def step_two(part):
        sems = part[2]

        @pl.when(z >= 2)
        def _():
            pass_on(part, dp - 4, sems[3], sems[4], z == 2, z_right)

        @pl.when(z < 2)
        def _():
            pass_on(part, dp + 4, sems[3], sems[4], z == 1, z_left)

    def step_three(part):
        sems = part[2]

        @pl.when(z == Z_SIZE - 1)
        def _():
            pass_on(part, dp - 6, sems[4], None, None, None)

        @pl.when(z == 0)
        def _():
            pass_on(part, dp + 6, sems[4], None, None, None)

    def dp_end(part):
        _, span, sems = part
        received((sems[0], span(4)))

    def gather_start(buf, r):
        over_x, to_core = group(), group()
        send(buf.at[r, blk], buf.at[r, blk], x_peer, over_x)
        send(buf.at[r, blk], buf.at[r, blk], core_peer, to_core)
        later_sent((over_x, buf.at[r, blk]))
        later_sent((to_core, buf.at[r, pl.ds(c, 2)]))
        return buf, r, over_x, to_core

    def gather_forward(part):
        buf, r, over_x, to_core = part
        received((over_x, buf.at[r, x_peer[1]]))
        send(buf.at[r, x_peer[1]], buf.at[r, x_peer[1]], core_peer, to_core)

    def gather_end(part):
        buf, r, _, to_core = part
        received((to_core, buf.at[r, pl.ds(c, 2)]))

    ow_copy.wait()
    o_part = dp_part(lambda i: WOS.at[blk, i], lambda n: WOS.at[blk, pl.ds(c, n)])
    a_part, c_part, g_part = slabs_part(WJS0), slabs_part(WJS1), slabs_part(G)
    u_part = [slabs_part(WUS.at[n]) for n in range(CHUNKS)]
    d_part = [slabs_part(WDS.at[n]) for n in range(CHUNKS)]
    own_over_z(o_part)
    own_over_y(o_part)

    def split_joint():
        jw_copy.wait()
        for b in range(BLK_SIZE):
            for s in range(3):
                at = 768 * s + 192 * b
                JP0[b, :, 64 * s : 64 * (s + 1)] = JW[:, at : at + 64]
                JP1[b, :, 128 * s : 128 * (s + 1)] = JW[:, at + 64 : at + 192]

    def swap_columns(parts, slabs):
        slabs[dp, blk] = parts[blk]
        return swap_parts(lambda b: parts.at[b], slabs.at[dp])

    split_joint()
    a_first = swap_columns(JP0, WJS0)
    g_first = swap_parts(lambda b: TILE, G.at[dp])
    c_first = swap_columns(JP1, WJS1)
    seg_copies = swap_parts(lambda b: SEGT, SEG)

    def first_stats():
        tok_copy.wait()
        firsts = []
        for r in range(2):
            unit, inverse = stats(TOK[r])
            U1[r] = unit
            I1[r] = inverse
            N1[r, blk] = unit.astype(BF)
            firsts.append(gather_start(N1, r))
        return firsts

    n1_part = first_stats()
    n1_sent = (started[-4:-2], started[-2:])
    del started[-4:]

    def split_up():
        uw_copy.wait()
        for i in range(DP_SIZE):
            for b in range(BLK_SIZE):
                at = 96 * (BLK_SIZE * i + b)
                UPW[b, :, 96 * i : 96 * (i + 1)] = UW[:, at : at + 96]
        for n in range(CHUNKS):
            for b in range(BLK_SIZE):
                UP[n, b] = UPW[b, :, WIDE * n : WIDE * (n + 1)]

    def split_down():
        dw_copy.wait()
        for n in range(CHUNKS):
            WDS[n, dp] = DW[:, WIDE * n : WIDE * (n + 1)]

    def early_down():
        split_down()
        for part in d_part:
            own_over_y(part)

    def low_cotangent():
        cot_copy.wait()
        for r in range(2):
            GR[r, blk] = COT[r].astype(BF)

    early_down()
    received(a_first)
    own_over_z(a_part)
    own_over_y(a_part)
    received(g_first)
    own_over_z(g_part)
    own_over_y(g_part)
    received(c_first)
    own_over_z(c_part)
    own_over_y(c_part)
    split_up()
    u_first = [swap_columns(UP.at[n], WUS.at[n]) for n in range(CHUNKS)]
    low_cotangent()
    gr_part = [gather_start(GR, 0)]
    step_one(a_part)
    step_one(g_part)
    gather_forward(n1_part[0])
    step_one(o_part)
    step_two(a_part)
    step_two(g_part)
    step_one(c_part)
    gather_forward(n1_part[1])
    step_three(a_part)
    step_three(g_part)
    step_two(o_part)
    step_two(c_part)
    for n in range(CHUNKS):
        received(u_first[n])
        own_over_y(u_part[n])
        own_over_z(u_part[n])

    dev_id = lax.broadcasted_iota(jnp.int32, (32, 1, 1), 0).astype(F32)
    blk_f = blk.astype(F32)
    piece24, _ = lane_pieces(768, 24)
    piece48, _ = lane_pieces(192, 48)
    piece96, _ = lane_pieces(768, 96)

    def mask24():
        return piece24[None] == dev_id

    def mask48(first_dev):
        return piece48[None] + (4.0 * blk_f + first_dev) == dev_id

    def mask96():
        return 4.0 * piece96[None] + blk_f == dev_id

    def place24():
        return piece_placer(768, 24)

    def place48():
        return piece_placer(192, 48)

    def place96():
        return piece_placer(768, 96)

    def small_end():
        dp_end(g_part)
        tiles = G[...].reshape(32 * 8, 128).astype(BF)

        def placed(placer, mask, lanes):
            spread = dot_nn(tiles, placer).reshape(32, 8, lanes)
            return jnp.sum(jnp.where(mask, spread, 0.0), axis=0)

        PV[0:8] = placed(place24(), mask24(), 768)
        PV[8:16] = placed(place96(), mask96(), 768)
        QVB[0:8] = placed(place48(), mask48(0.0), 192)
        QVB[8:16] = placed(place48(), mask48(16.0), 192)

    def segments_end():
        received(seg_copies)
        eye = jnp.where(
            lax.broadcasted_iota(jnp.int32, (128, 128), 0)
            == lax.broadcasted_iota(jnp.int32, (128, 128), 1), 1.0, 0.0,
        ).astype(BF)
        for b in range(BLK_SIZE):
            part = SEG[b]
            KSEG[:, 128 * b : 128 * (b + 1)] = part
            QSEG[128 * b : 128 * (b + 1)] = dot_nt(eye, part.astype(BF))


    segments_end()
    step_three(o_part)
    step_three(c_part)
    small_end()
    gain1, shift1, obias = PV[0:1], PV[1:2], PV[2:3]
    gain2, shift2, dbias = PV[3:4], PV[4:5], PV[5:6]

    def compact(slabs, whole):
        for i in range(DP_SIZE):
            rows = slabs(i).astype(F32)
            rows = rows.reshape(96, rows.shape[-1])
            whole[96 * i : 96 * (i + 1), :] = rows.astype(BF)

    def norm_rows(r):
        gather_end(n1_part[r])
        for copies in n1_sent[r]:
            sent(copies)
        for b in range(BLK_SIZE):
            N1[r, b] = (N1[r, b].astype(F32) * gain1 + shift1).astype(BF)

    def qkv_one(r):
        joint = dot_nn(N1[r].reshape(512, 768), WJ0[...])
        qbias, vbias = QVB[6:7, 0:64], QVB[14:15, 0:64]
        Q[r, 0] = ((joint[:, :64] + qbias).astype(BF).astype(F32) * 0.125).astype(BF)
        K[r, 0] = joint[:, 64:128].astype(BF)
        V[r, 0] = (joint[:, 128:] + vbias).astype(BF)

    def qkv_two(r):
        joint = dot_nn(N1[r].reshape(512, 768), WJ1[...])
        qbias, vbias = QVB[6:7, 64:192], QVB[14:15, 64:192]
        query = ((joint[:, :128] + qbias).astype(BF).astype(F32) * 0.125).astype(BF)
        keys = joint[:, 128:256].astype(BF)
        values = (joint[:, 256:] + vbias).astype(BF)
        for h in (1, 2):
            lanes = slice(64 * (h - 1), 64 * h)
            Q[r, h] = query[:, lanes]
            K[r, h] = keys[:, lanes]
            V[r, h] = values[:, lanes]

    def attend(r, h):
        scores = dot_nt(Q[r, h], K[r, h])
        scores = jnp.where(QSEG[:, r : r + 1] == KSEG[2 + r : 3 + r, :], scores, masked_score)
        top = jnp.max(scores, axis=-1, keepdims=True)
        expos = jnp.exp(scores - top)
        total = jnp.sum(expos, axis=-1, keepdims=True)
        probs = (expos * (1.0 / total)).astype(BF)
        PB[r, h] = probs
        out = dot_nn(probs, V[r, h])
        OF[r, h] = out
        AT[r, :, :, 64 * h : 64 * (h + 1)] = out.astype(BF).reshape(4, 128, 64)

    def swap_heads(src, dst, r):
        dst[r, blk] = src[r, blk]
        return swap_parts(lambda b: src.at[r, b], dst.at[r])

    dp_end(a_part)
    compact(lambda i: WJS0[i], WJ0)
    norm_rows(0)
    qkv_one(0)
    attend(0, 0)
    dp_end(o_part)
    wo_x, wo_core = group(), group()
    send(WOS.at[blk], WOS.at[blk], x_peer, wo_x)
    send(WOS.at[blk], WOS.at[blk], core_peer, wo_core)
    later_sent((wo_x, WOS.at[blk]))
    later_sent((wo_core, WOS.at[pl.ds(c, 2)]))
    norm_rows(1)
    qkv_one(1)
    step_one(u_part[0])
    attend(1, 0)
    dp_end(c_part)
    compact(lambda i: WJS1[i], WJ1)
    step_two(u_part[0])
    step_one(u_part[1])
    qkv_two(0)
    attend(0, 1)
    attend(0, 2)
    at_copies = [swap_heads(AT, AR, 0)]
    gather_forward(gr_part[0])
    step_three(u_part[0])
    step_two(u_part[1])
    step_one(u_part[2])
    for n in range(CHUNKS):
        own_over_z(d_part[n])
    qkv_two(1)
    attend(1, 1)
    step_three(u_part[1])
    step_two(u_part[2])
    step_one(d_part[0])
    attend(1, 2)
    at_copies.append(swap_heads(AT, AR, 1))
    received((wo_x, WOS.at[x_peer[1]]))
    send(WOS.at[x_peer[1]], WOS.at[x_peer[1]], core_peer, wo_core)
    step_three(u_part[2])
    step_two(d_part[0])
    step_one(d_part[1])
    received((wo_core, WOS.at[pl.ds(c, 2)]))
    compact(lambda i: WOS[:, i], WO)

    def middle_rows(r):
        received(at_copies[r])
        total = TOK[r] + obias
        for b in range(BLK_SIZE):
            total = total + dot_nn(AR[r, b], WO[192 * b : 192 * (b + 1), :])
        MID[r] = total
        unit, inverse = stats(total)
        U2[r] = unit
        I2[r] = inverse
        N2[r, blk] = (unit * gain2 + shift2).astype(BF)
        return gather_start(N2, r)

    n2_part = [middle_rows(0)]
    step_three(d_part[0])
    step_two(d_part[1])
    step_one(d_part[2])
    n2_part.append(middle_rows(1))
    gr_part.append(gather_start(GR, 1))
    for n in range(CHUNKS):
        dp_end(u_part[n])
        compact(lambda i: WUS[n, i], WU.at[n])
    step_three(d_part[1])
    step_two(d_part[2])
    gather_forward(n2_part[0])
    step_three(d_part[2])
    gather_end(n2_part[0])

    def rows_of(buf, r):
        return buf[r].reshape(512, 768)

    def up(r):
        for n in range(CHUNKS):
            cols = slice(WIDE * n, WIDE * (n + 1))
            hidden = dot_nn(rows_of(N2, r), WU[n]) + PV[15:16, cols]
            square = hidden * hidden
            bent = jnp.tanh(hidden * (0.7978845608028654 + 0.035677408136300125 * square))
            half = 0.5 * (1.0 + bent)
            ACT[r, :, cols] = (hidden * half).astype(BF)
            slope = 0.3989422804014327 + 0.05351611220445019 * square
            GP[r, :, cols] = (half + hidden * (1.0 - bent * bent) * slope).astype(BF)

    def hidden_back(r):
        for n in range(2):
            cols = slice(384 * n, 384 * (n + 1))
            rows = rows_of(GR, r)
            grad = 0.0
            for m in range(CHUNKS):
                weight = WDS[m, 4 * n : 4 * (n + 1)].reshape(384, WIDE)
                grad = grad + dot_nt(rows[:, WIDE * m : WIDE * (m + 1)], weight)
            grad = (grad * GP[r, :, cols].astype(F32)).astype(BF)
            GH[r, :, cols] = grad
            UBS[r, :, cols] = jnp.sum(grad.astype(F32), axis=0, keepdims=True)

    def sum_store(i, r, cols, values):
        PT[i, r, :, :, :, cols] = values.reshape(2, 2, 128, values.shape[-1]).astype(BF)

    def sum_start(i, r):
        sems = group()
        send(PT.at[i, r, :, 1 - c], RC.at[i, r], core_peer, sems)
        later_sent((sems, RC.at[i, r]))
        return sems, RC.at[i, r]

    def sum_middle(i, r, first):
        received(first)
        SX[i, r] = (PT[i, r, 1 - x, c].astype(F32) + RC[i, r, 1 - x].astype(F32)).astype(BF)
        sems = group()
        send(SX.at[i, r], RX.at[i, r], x_peer, sems)
        later_sent((sems, RX.at[i, r]))
        return sems, RX.at[i, r]

    def sum_end(i, r, second):
        received(second)
        return PT[i, r, x, c].astype(F32) + RC[i, r, x].astype(F32) + RX[i, r].astype(F32)

    def second_back(r):
        for n in range(3):
            cols = slice(256 * n, 256 * (n + 1))
            grad = 0.0
            for m in range(CHUNKS):
                grad = grad + dot_nt(GH[r, :, WIDE * m : WIDE * (m + 1)], WU[m, cols, :])
            sum_store(0, r, cols, grad)
        return sum_start(0, r)

    def first_back(r):
        for n in range(3):
            cols = slice(256 * n, 256 * (n + 1))
            sum_store(
                2, r, cols, dot_nt(GJ0[r], WJ0[cols, :]) + dot_nt(GJ1[r], WJ1[cols, :])
            )
        return sum_start(2, r)

    def down(r):
        for n in range(CHUNKS):
            cols = slice(WIDE * n, WIDE * (n + 1))
            sum_store(1, r, cols, dot_nn(ACT[r], WDS[n].reshape(768, WIDE)))
        return sum_start(1, r)

    def scatter_start(parts, recv):
        sems = group()
        send(parts.at[:, 1 - y], recv, y_peer, sems)
        later_sent((sems, recv))
        return sems, recv

    def scatter_middle(parts, recv, sums, landing, first):
        received(first)
        sums[...] = (parts[:, y].astype(F32) + recv[...].astype(F32)).astype(BF)
        sems = group()
        for k in range(1, Z_SIZE):
            send(sums.at[z_at(k)], landing.at[k - 1], (2 * z_at(k) + y, blk), sems)
        later_sent((sems, landing))
        return sums, landing, (sems, landing)

    def scatter_end(sums, landing, second):
        received(second)
        total = sums[z].astype(F32)
        for k in range(Z_SIZE - 1):
            total = total + landing[k].astype(F32)
        return total

    def return_columns(part, sends, recvs):
        sends[...] = scatter_end(*part).astype(BF)
        recvs[blk] = sends[blk]
        return swap_parts(lambda b: sends.at[b], recvs)

    def down_grad(n):
        grads = GR[:, :, :, WIDE * n : WIDE * (n + 1)].reshape(1024, WIDE)
        for m in range(2):
            cols = slice(384 * m, 384 * (m + 1))
            grad = dot_tn(ACT[:, :, cols].reshape(1024, 384), grads)
            GD[n, 2 * m : 2 * m + 2] = grad.reshape(2, 2, 96, WIDE).astype(BF)

    def row_grad(rows, grads, parts):
        for m in range(2):
            cols = slice(384 * m, 384 * (m + 1))
            grad = dot_tn(rows[:, :, :, cols].reshape(1024, 384), grads)
            parts[2 * m : 2 * m + 2] = grad.reshape(2, 2, 4, 24, grad.shape[-1]).astype(BF)

    def up_grad(n):
        row_grad(N2, GH[:, :, WIDE * n : WIDE * (n + 1)].reshape(1024, WIDE), GU.at[n])

    def joint_grad_one():
        row_grad(N1, GJ0[...].reshape(1024, 192), GA)
        return scatter_start(GA, RYa)

    def joint_grad_two():
        row_grad(N1, GJ1[...].reshape(1024, 384), GC)
        return scatter_start(GC, RYc)

    def output_grad():
        for b in range(BLK_SIZE):
            grad = dot_tn(AR[:, b].reshape(256, 192), GB[...].reshape(256, 768))
            grad = grad.reshape(2, 4, 24, 768).astype(BF)
            for i in range(4):
                GO[i // 2, i % 2, 2 * b : 2 * b + 2] = grad[:, i]
        sems = group()
        send(GO.at[:, 1 - c], RCo, core_peer, sems)
        later_sent((sems, RCo))
        return sems, RCo

    def output_grad_middle(first):
        received(first)
        SXo[...] = (GO[1 - x, c].astype(F32) + RCo[1 - x].astype(F32)).astype(BF)
        sems = group()
        send(SXo, RXo, x_peer, sems)
        later_sent((sems, RXo))
        return sems, RXo

    def norm_back(e, unit, inverse, gain):
        f = e * gain
        grad = inverse * (
            f - jnp.mean(f, axis=-1, keepdims=True)
            - unit * jnp.mean(f * unit, axis=-1, keepdims=True)
        )
        return (
            grad, jnp.sum(e * unit, axis=0, keepdims=True), jnp.sum(e, axis=0, keepdims=True)
        )

    def second_norm_back(r, second):
        e = sum_end(0, r, second)
        grad, of_gain, of_shift = norm_back(e, U2[r], I2[r], gain2)
        grad = grad + COT[r]
        GM[r] = grad
        low = grad.astype(BF)
        GB[r] = low
        for b in range(BLK_SIZE):
            DA[r, b] = dot_nt(low, WO[192 * b : 192 * (b + 1), :]).astype(BF)
        copies = swap_heads(DA, DR, r)
        VS[3:4] += of_gain
        VS[4:5] += of_shift
        VS[2:3] += jnp.sum(low.astype(F32), axis=0, keepdims=True)
        VS[5:6] += jnp.sum(COT[r].astype(BF).astype(F32), axis=0, keepdims=True)
        return copies

    def attend_back(r, h):
        grad_out = DR[r, :, :, 64 * h : 64 * (h + 1)].reshape(512, 64)
        DOH[...] = grad_out
        grad_out = DOH[...]
        delta = jnp.sum(grad_out.astype(F32) * OF[r, h], axis=-1, keepdims=True)
        grad_probs = dot_nt(grad_out, V[r, h])
        grad_scores = (PB[r, h].astype(F32) * (grad_probs - delta)).astype(BF)
        grads = (
            (dot_nn(grad_scores, K[r, h]) * 0.125).astype(BF),
            dot_tn(grad_scores, Q[r, h]).astype(BF),
            dot_tn(PB[r, h], grad_out).astype(BF),
        )
        for s, grad in enumerate(grads):
            if h == 0:
                GJ0[r, :, 64 * s : 64 * (s + 1)] = grad
            else:
                at = 128 * s + 64 * (h - 1)
                GJ1[r, :, at : at + 64] = grad

    def output_grad_over_dp(second):
        received(second)
        GO2[...] = (
            GO[x, c].astype(F32) + RCo[x].astype(F32) + RXo[...].astype(F32)
        ).astype(BF).reshape(4, 2, 24, 768)
        return scatter_start(GO2, RYo)

    def vector_sums():
        for r in range(2):
            JBS[r, :, 0:192] = jnp.sum(GJ0[r].astype(F32), axis=0, keepdims=True)
            JBS[r, :, 192:576] = jnp.sum(GJ1[r].astype(F32), axis=0, keepdims=True)

    def first_norm_back(r, second):
        e = sum_end(2, r, second)
        grad, of_gain, of_shift = norm_back(e, U1[r], I1[r], gain1)
        GM[r] = GM[r] + grad
        VS[0:1] += of_gain
        VS[1:2] += of_shift

    VS[...] = jnp.zeros_like(VS)
    d_first, d_second, u_grad_first, u_grad_second = [], [], [], []

    def d_over_y(n):
        d_first.append(scatter_start(GD.at[n], RYd.at[n]))

    def d_over_z(n):
        d_second.append(scatter_middle(GD.at[n], RYd.at[n], Sd.at[n], RZd.at[n], d_first[n]))

    def u_over_y(n):
        u_grad_first.append(scatter_start(GU.at[n], RYu.at[n]))

    def u_over_z(n):
        u_grad_second.append(
            scatter_middle(GU.at[n], RYu.at[n], Su.at[n], RZu.at[n], u_grad_first[n])
        )

    up(0)
    gather_end(gr_part[0])
    for n in range(CHUNKS):
        dp_end(d_part[n])
    hidden_back(0)
    second_first = [second_back(0)]
    gather_forward(n2_part[1])
    gather_end(n2_part[1])
    up(1)
    second_second = [sum_middle(0, 0, second_first[0])]
    gather_forward(gr_part[1])
    gather_end(gr_part[1])
    down_grad(0)
    d_over_y(0)
    down_grad(1)
    d_over_y(1)
    hidden_back(1)
    second_first.append(second_back(1))
    down_grad(2)
    d_over_y(2)
    up_grad(0)
    u_over_y(0)
    second_second.append(sum_middle(0, 1, second_first[1]))
    d_over_z(0)
    up_grad(1)
    u_over_y(1)
    up_grad(2)
    u_over_y(2)
    da_copies = [second_norm_back(0, second_second[0])]
    d_over_z(1)
    result_first = [down(0), down(1)]
    da_copies.append(second_norm_back(1, second_second[1]))
    d_over_z(2)
    result_second = [sum_middle(1, 0, result_first[0])]
    received(da_copies[0])
    attend_back(0, 1)
    attend_back(0, 2)
    o_first = output_grad()
    u_over_z(0)
    received(da_copies[1])
    attend_back(1, 1)
    attend_back(1, 2)
    c_grad_first = joint_grad_two()
    o_second = output_grad_middle(o_first)
    u_over_z(1)
    attend_back(0, 0)
    first_first = [first_back(0)]
    attend_back(1, 0)
    a_grad_first = joint_grad_one()
    u_over_z(2)
    first_second = [sum_middle(2, 0, first_first[0])]
    first_first.append(first_back(1))
    o_grad_first = output_grad_over_dp(o_second)
    first_second.append(sum_middle(2, 1, first_first[1]))
    result_second.append(sum_middle(1, 1, result_first[1]))
    vector_sums()
    out_copies = []

    def down_out():
        for n in range(CHUNKS):
            OD[:, WIDE * n : WIDE * (n + 1)] = scatter_end(*d_second[n])
        out_copies.append(local(OD, out_d))

    c_grad_second = scatter_middle(GC, RYc, Sc, RZc, c_grad_first)
    first_norm_back(0, first_second[0])
    a_grad_second = scatter_middle(GA, RYa, Sa, RZa, a_grad_first)
    first_norm_back(1, first_second[1])
    out_copies.append(local(GM, grad_tok_out))
    down_out()

    def vectors_start():
        row = lax.broadcasted_iota(jnp.int32, (8, 1), 0)

        def picked(values, mask, placer):
            wide = jnp.where(mask, values[None], 0.0)
            wide = wide.reshape(256, wide.shape[-1])
            high = wide.astype(BF)
            rest = (wide - high.astype(F32)).astype(BF)
            return dot_nt(high, placer) + dot_nt(rest, placer)

        joint = JBS[0] + JBS[1]
        queries = jnp.concatenate([joint[:, 0:64], joint[:, 192:320]], axis=1)
        values = jnp.concatenate([joint[:, 128:192], joint[:, 448:576]], axis=1)
        pieces = picked(VS[...], mask24(), place24())
        pieces += picked(jnp.where(row == 7, UBS[0] + UBS[1], 0.0), mask96(), place96())
        pieces += picked(jnp.where(row == 6, queries, 0.0), mask48(0.0), place48())
        pieces += picked(jnp.where(row == 6, values, 0.0), mask48(16.0), place48())
        TS[...] = pieces.reshape(32, 8, 128)
        TR[4 * dp + blk] = TS[4 * dp + blk]
        return send_all(lambda dev: TS.at[4 * dev[0] + dev[1]], TR)

    vector_copies = vectors_start()
    u_back = [
        return_columns(u_grad_second[n], AUs.at[n], AUr.at[n])
        for n in range(CHUNKS)
    ]
    o_grad_second = scatter_middle(GO2, RYo, So, RZo, o_grad_first)

    def result_end():
        for r in range(2):
            MID[r] = MID[r] + sum_end(1, r, result_second[r]) + dbias
        out_copies.append(local(MID, result_out))

    result_end()
    c_back = return_columns(c_grad_second, ACs, ACr)
    a_back = return_columns(a_grad_second, AAs, AAr)

    def up_out():
        for part in u_back:
            received(part)
        for b in range(BLK_SIZE):
            whole = jnp.concatenate([AUr[n, b] for n in range(CHUNKS)], axis=1).astype(F32)
            for i in range(DP_SIZE):
                at = 96 * (BLK_SIZE * i + b)
                OU[:, at : at + 96] = whole[:, 96 * i : 96 * (i + 1)]
        return local(OU, out_u)

    out_copies.append(up_out())
    OO[...] = scatter_end(*o_grad_second)
    out_copies.append(local(OO, out_o))
    received(vector_copies)
    OS[...] = jnp.sum(TR[...], axis=0)
    out_copies.append(local(OS, out_s))

    def joint_out():
        received(c_back)
        received(a_back)
        for b in range(BLK_SIZE):
            one, two = AAr[b].astype(F32), ACr[b].astype(F32)
            for s in range(3):
                at = 768 * s + 192 * b
                OJ[:, at : at + 64] = one[:, 64 * s : 64 * (s + 1)]
                OJ[:, at + 64 : at + 192] = two[:, 128 * s : 128 * (s + 1)]
        return local(OJ, out_j)

    out_copies.append(joint_out())
    for copies in started:
        sent(copies)

    @pl.when(inner)
    def _():
        for sems, _, five in started_over_z:
            sent((sems, five))

    @pl.when(jnp.logical_not(inner))
    def _():
        for sems, one, _ in started_over_z:
            sent((sems, one))

    for made in out_copies:
        made.wait()


def finish_kernel(*refs):
    big_in, sums, big_out, small_out = refs[:6], refs[6], refs[7:13], refs[13:21]
    for source, target in zip(big_in, big_out):
        target[...] = source[...]
    for row, width in enumerate(TILE_WIDTHS):
        small_out[row][...] = sums[row, 0:width]


def fast_device(
    tokens, segment_ids, pad_mask, joint_weight, joint_bias, output_weight, output_bias,
    first_gain, first_shift, up_weight, up_bias, down_weight, down_bias,
    second_gain, second_shift, cotangent,
):
    vectors = (
        first_gain, first_shift, output_bias, second_gain, second_shift, down_bias,
        joint_bias, up_bias,
    )

    def vm(*shape, dtype=BF):
        return pltpu.VMEM(shape, dtype)

    def fm(*shape):
        return pltpu.VMEM(shape, F32)

    scratch = [
        fm(2, 128, 768), fm(2, 128, 768), vm(24, 2304), vm(24, 3072), vm(96, 768),
        vm(4, 24, 192), vm(4, 24, 384), vm(4, 24, 768), vm(CHUNKS, 4, 24, WIDE), fm(8, 128), fm(8, 128), fm(8, 4, 8, 128),
        fm(4, 8, 128), fm(8, 512), fm(512, 8), fm(16, 768), fm(16, 192),
        vm(2, 4, 128, 768), vm(2, 4, 128, 768), vm(2, 4, 128, 768),
        vm(8, 4, 24, 192), vm(8, 4, 24, 384), vm(CHUNKS, 8, 4, 24, WIDE), vm(CHUNKS, 8, 96, WIDE),
        vm(4, 8, 24, 768), vm(768, 192), vm(768, 384), vm(CHUNKS, 768, WIDE), vm(768, 768),
        fm(2, 128, 768), fm(2, 128, 1), fm(2, 128, 768), fm(2, 128, 1),
        fm(2, 128, 768), fm(2, 128, 768), vm(2, 128, 768),
        vm(2, 3, 512, 64), vm(2, 3, 512, 64), vm(2, 3, 512, 64), vm(2, 3, 512, 512),
        fm(2, 3, 512, 64), vm(2, 4, 128, 192), vm(2, 4, 128, 192),
        vm(2, 4, 128, 192), vm(2, 4, 128, 192), vm(512, 64), vm(2, 512, 192), vm(2, 512, 384),
        vm(2, 512, 768), vm(2, 512, 768), vm(2, 512, 768), fm(2, 1, 768),
        vm(3, 2, 2, 2, 128, 768), vm(3, 2, 2, 128, 768), vm(3, 2, 128, 768), vm(3, 2, 128, 768),
        vm(CHUNKS, 4, 2, 96, WIDE), vm(CHUNKS, 4, 2, 4, 24, WIDE), vm(4, 2, 4, 24, 192), vm(4, 2, 4, 24, 384),
        vm(2, 2, 8, 24, 768), vm(4, 2, 24, 768),
        vm(CHUNKS, 4, 96, WIDE), vm(CHUNKS, 4, 4, 24, WIDE), vm(4, 4, 24, 192), vm(4, 4, 24, 384), vm(4, 24, 768),
        vm(CHUNKS, 4, 96, WIDE), vm(CHUNKS, 4, 4, 24, WIDE), vm(4, 4, 24, 192), vm(4, 4, 24, 384), vm(4, 24, 768),
        vm(CHUNKS, 3, 96, WIDE), vm(CHUNKS, 3, 4, 24, WIDE), vm(3, 4, 24, 192), vm(3, 4, 24, 384), vm(3, 24, 768),
        vm(CHUNKS, 4, 24, WIDE), vm(CHUNKS, 4, 24, WIDE), vm(4, 24, 192), vm(4, 24, 192),
        vm(4, 24, 384), vm(4, 24, 384), vm(2, 8, 24, 768), vm(8, 24, 768), vm(8, 24, 768),
        fm(32, 8, 128), fm(32, 8, 128), fm(8, 768), fm(2, 1, 576),
        fm(24, 2304), fm(24, 3072), fm(96, 768), fm(24, 768), fm(8, 128),
        pltpu.SemaphoreType.DMA((COPIES,)), pltpu.SemaphoreType.DMA((COPIES,)),
        pltpu.SemaphoreType.DMA((16,)),
    ]
    vmem = pl.BlockSpec(memory_space=pltpu.VMEM)
    anywhere = pl.BlockSpec(memory_space=pl.ANY)
    out_shapes = [
        (2, 128, 768), (2, 128, 768), (24, 2304), (24, 768), (24, 3072), (96, 768), (8, 128),
    ]
    made = pl.pallas_call(
        layer_kernel,
        out_shape=[jax.ShapeDtypeStruct(shape, F32) for shape in out_shapes],
        in_specs=[anywhere] * 2 + [vmem] * 2 + [anywhere] * 4 + [vmem] * 8,
        out_specs=[anywhere] * 7,
        scratch_shapes=scratch,
        compiler_params=pltpu.CompilerParams(
            collective_id=0, has_side_effects=True, vmem_limit_bytes=VMEM_MIB * 2**20
        ),
        cost_estimate=pl.CostEstimate(
            flops=13 * 10**9, bytes_accessed=6 * 10**6, transcendentals=4 * 10**6
        ),
    )(
        tokens, cotangent, segment_ids, pad_mask, joint_weight, up_weight, down_weight,
        output_weight, *vectors,
    )
    ends = pl.pallas_call(
        finish_kernel,
        out_shape=[jax.ShapeDtypeStruct(shape, F32) for shape in out_shapes[:6]]
        + [jax.ShapeDtypeStruct((width,), F32) for width in TILE_WIDTHS],
        in_specs=[vmem] * 7,
        out_specs=[vmem] * 14,
    )(*made)
    result, grad_tokens, grad_j, grad_o, grad_u, grad_d = ends[:6]
    first_g, first_s, output_b, second_g, second_s, down_b, joint_b, up_b = ends[6:]
    return (
        result, grad_tokens, grad_j, joint_b, grad_o, output_b, first_g, first_s,
        grad_u, up_b, grad_d, down_b, second_g, second_s,
    )


def solution(mesh):
    placed = (
        P("dp", "blk", None),
        P("dp", "blk"),
        P("dp", "blk"),
        P(("dp", "blk"), None),
        P(("dp", "blk")),
        P(("dp", "blk"), None),
        P(("dp", "blk")),
        P(("dp", "blk")),
        P(("dp", "blk")),
        P(("dp", "blk"), None),
        P(("dp", "blk")),
        P(("dp", "blk"), None),
        P(("dp", "blk")),
        P(("dp", "blk")),
        P(("dp", "blk")),
        P("dp", "blk", None),
    )

    def spread(device_part):
        return jax.shard_map(
            device_part,
            mesh=mesh,
            in_specs=placed,
            out_specs=(
                P("dp", "blk", None),
                P("dp", "blk", None),
                P(("dp", "blk"), None),
                P(("dp", "blk")),
                P(("dp", "blk"), None),
                P(("dp", "blk")),
                P(("dp", "blk")),
                P(("dp", "blk")),
                P(("dp", "blk"), None),
                P(("dp", "blk")),
                P(("dp", "blk"), None),
                P(("dp", "blk")),
                P(("dp", "blk")),
                P(("dp", "blk")),
            ),
            check_vma=False,
        )

    def layer(*arrays):
        rows, length, features = arrays[0].shape
        shape = dict(mesh.shape)
        fits = (
            shape == {"dp": DP_SIZE, "blk": BLK_SIZE}
            and (rows, length, features) == (2 * shape["dp"], 512, 768)
            and arrays[9].shape[1] == 3072
        )
        return spread(fast_device if fits else per_device)(*arrays)

    return layer
```

```python
import jax
import jax.numpy as jnp
from jax import lax
from jax.experimental import pallas as pl
from jax.experimental.pallas import tpu as pltpu
from jax.sharding import PartitionSpec as P

HEADS = 12
SENDS, RECEIVES = 85, 115
VMEM_MIB = 60


epsilon = 1e-05
masked_score = -1e30


def normalize(values_in, gain, shift):
    centered = values_in - jnp.mean(values_in, axis=-1, keepdims=True)
    inverse = lax.rsqrt(jnp.mean(centered * centered, axis=-1, keepdims=True) + epsilon)
    unit_rows = centered * inverse
    return (unit_rows * gain + shift, unit_rows, inverse)


def normalize_back(grad_normed, unit_rows, inverse, gain):
    scaled = grad_normed * gain
    grad_input = inverse * (
        scaled
        - jnp.mean(scaled, axis=-1, keepdims=True)
        - unit_rows * jnp.mean(scaled * unit_rows, axis=-1, keepdims=True)
    )
    return (
        grad_input,
        jnp.sum(grad_normed * unit_rows, axis=(0, 1)),
        jnp.sum(grad_normed, axis=(0, 1)),
    )


def project(activation, weight):
    return jnp.einsum("rcd,dn->rcn", activation, weight, preferred_element_type=jnp.float32)


def project_back(gradient, weight):
    return jnp.einsum("rcn,dn->rcd", gradient, weight, preferred_element_type=jnp.float32)


def outer_sum(activation, gradient):
    return jnp.einsum("rcd,rcn->dn", activation, gradient, preferred_element_type=jnp.float32)


def split_heads(matrix, head_count):
    return matrix.reshape(
        matrix.shape[0], matrix.shape[1], head_count, matrix.shape[2] // head_count
    )


def masked_scores(query_heads, key_heads, query_segment, key_segment, scaling):
    raw_scores = (
        jnp.einsum("rqhd,rkhd->rhqk", query_heads, key_heads, preferred_element_type=jnp.float32)
        * scaling
    )
    allowed = (query_segment[:, :, None] == key_segment[:, None, :])[:, None]
    return (jnp.where(allowed, raw_scores, masked_score), allowed)


def column_sums(gradient):
    return jnp.sum(gradient.astype(jnp.float32), axis=(0, 1))


def scatter_sum(gradient):
    summed = lax.psum_scatter(
        gradient.astype(jnp.bfloat16), ("dp", "blk"), scatter_dimension=0, tiled=True
    )
    return summed.astype(jnp.float32)


def per_device(
    tokens,
    segment_ids,
    pad_mask,
    joint_weight,
    joint_bias,
    output_weight,
    output_bias,
    first_gain,
    first_shift,
    up_weight,
    up_bias,
    down_weight,
    down_bias,
    second_gain,
    second_shift,
    cotangent,
):
    batch_rows, local_len, features = tokens.shape
    head_count = HEADS
    head_size = features // head_count
    scaling = head_size ** (-0.5)
    device_count = lax.axis_size("dp") * lax.axis_size("blk")
    small_parts = (
        joint_bias, output_bias, first_gain, first_shift, up_bias, down_bias, second_gain, second_shift
    )
    small_all = lax.all_gather(jnp.concatenate(small_parts), ("dp", "blk"), axis=0, tiled=True)
    small_all = small_all.reshape(device_count, -1)
    small_full = []
    small_at = 0
    for part in small_parts:
        small_full.append(small_all[:, small_at : small_at + part.shape[0]].reshape(-1))
        small_at += part.shape[0]
    full_joint_bias, full_output_bias, gain_one, shift_one = small_full[:4]
    full_up_bias, full_down_bias, gain_two, shift_two = small_full[4:]
    full_joint = lax.all_gather(joint_weight, ("dp", "blk"), axis=0, tiled=True)
    full_output = lax.all_gather(output_weight, ("dp", "blk"), axis=0, tiled=True)
    normed_one, unit_one, inverse_one = normalize(
        tokens, gain_one.astype(jnp.float32), shift_one.astype(jnp.float32)
    )
    normed_one_low = normed_one.astype(jnp.bfloat16)
    joint = project(normed_one_low, full_joint)
    bias_values = full_joint_bias.astype(jnp.float32)
    query = (joint[..., :features] + bias_values[:features]).astype(jnp.bfloat16)
    keys = joint[..., features : 2 * features].astype(jnp.bfloat16)
    values = (joint[..., 2 * features :] + bias_values[features:]).astype(jnp.bfloat16)
    key_segment = jnp.where(pad_mask == 1, segment_ids, -1)
    query_heads = split_heads(query, head_count)
    top_score = jnp.full((batch_rows, head_count, local_len), masked_score, jnp.float32)
    key_portion = lax.all_gather(keys, "blk", axis=1, tiled=True)
    value_portion = lax.all_gather(values, "blk", axis=1, tiled=True)
    segment_portion = lax.all_gather(key_segment, "blk", axis=1, tiled=True)
    scores, allowed = masked_scores(
        query_heads, split_heads(key_portion, head_count), segment_ids, segment_portion, scaling
    )
    new_top = jnp.maximum(top_score, jnp.max(scores, axis=-1))
    weights = jnp.where(allowed, jnp.exp(scores - new_top[..., None]), 0.0)
    total_weight = jnp.sum(weights, axis=-1)
    weighted = jnp.einsum(
        "rhqk,rkhd->rhqd",
        weights.astype(jnp.bfloat16),
        split_heads(value_portion, head_count),
        preferred_element_type=jnp.float32,
    )
    top_score, total_weight, weighted = (new_top, total_weight, weighted)
    log_total = top_score + jnp.log(total_weight)
    attended_heads = weighted / total_weight[..., None]
    attended = jnp.transpose(attended_heads, (0, 2, 1, 3)).reshape(batch_rows, local_len, features)
    attended_low = attended.astype(jnp.bfloat16)
    middle = tokens + project(attended_low, full_output) + full_output_bias.astype(jnp.float32)
    full_up = lax.all_gather(up_weight, ("dp", "blk"), axis=0, tiled=True)
    full_down = lax.all_gather(down_weight, ("dp", "blk"), axis=0, tiled=True)
    normed_two, unit_two, inverse_two = normalize(
        middle, gain_two.astype(jnp.float32), shift_two.astype(jnp.float32)
    )
    normed_two_low = normed_two.astype(jnp.bfloat16)
    hidden = project(normed_two_low, full_up) + full_up_bias.astype(jnp.float32)
    activated, gelu_pullback = jax.vjp(jax.nn.gelu, hidden)
    activated_low = activated.astype(jnp.bfloat16)
    result = middle + project(activated_low, full_down) + full_down_bias.astype(jnp.float32)
    later_up, later_down, later_gain_two = full_up, full_down, gain_two
    grad_result = cotangent.astype(jnp.bfloat16)
    grad_down_weight = outer_sum(activated_low, grad_result)
    grad_down_bias = column_sums(grad_result)
    grad_activated = project_back(grad_result, later_down)
    grad_hidden = gelu_pullback(grad_activated)[0].astype(jnp.bfloat16)
    grad_up_bias = column_sums(grad_hidden)
    grad_up_weight = outer_sum(normed_two_low, grad_hidden)
    grad_normed_two = project_back(grad_hidden, later_up)
    grad_from_second, grad_gain_two, grad_shift_two = normalize_back(
        grad_normed_two, unit_two, inverse_two, later_gain_two.astype(jnp.float32)
    )
    grad_middle = cotangent + grad_from_second
    grad_up_shard = scatter_sum(grad_up_weight)
    grad_down_shard = scatter_sum(grad_down_weight)
    later_joint, later_output, later_gain_one = full_joint, full_output, gain_one
    grad_branch = grad_middle.astype(jnp.bfloat16)
    grad_output_weight = outer_sum(attended_low, grad_branch)
    grad_output_bias = column_sums(grad_branch)
    grad_attended = project_back(grad_branch, later_output).astype(jnp.bfloat16)
    grad_heads = split_heads(grad_attended, head_count)
    delta = jnp.einsum("rqhd,rhqd->rhq", grad_heads.astype(jnp.float32), attended_heads)
    key_heads = split_heads(key_portion, head_count)
    scores, allowed = masked_scores(query_heads, key_heads, segment_ids, segment_portion, scaling)
    probs = jnp.where(allowed, jnp.exp(scores - log_total[..., None]), 0.0)
    grad_probs = jnp.einsum(
        "rqhd,rkhd->rhqk",
        grad_heads,
        split_heads(value_portion, head_count),
        preferred_element_type=jnp.float32,
    )
    grad_scores = (probs * (grad_probs - delta[..., None])).astype(jnp.bfloat16)
    grad_query = scaling * jnp.einsum(
        "rhqk,rkhd->rqhd", grad_scores, key_heads, preferred_element_type=jnp.float32
    )
    every_total, every_delta = (
        lax.all_gather(log_total, "blk", axis=2, tiled=True),
        lax.all_gather(delta, "blk", axis=2, tiled=True),
    )
    own_keys = split_heads(keys, head_count)
    own_values = split_heads(values, head_count)
    query_portion = lax.all_gather(query, "blk", axis=1, tiled=True)
    grad_portion = lax.all_gather(grad_attended, "blk", axis=1, tiled=True)
    segment_portion = lax.all_gather(segment_ids, "blk", axis=1, tiled=True)
    portion_queries = split_heads(query_portion, head_count)
    portion_grads = split_heads(grad_portion, head_count)
    scores, allowed = masked_scores(
        portion_queries, own_keys, segment_portion, key_segment, scaling
    )
    probs = jnp.where(allowed, jnp.exp(scores - every_total[..., None]), 0.0)
    grad_values = jnp.einsum(
        "rhqk,rqhd->rkhd",
        probs.astype(jnp.bfloat16),
        portion_grads,
        preferred_element_type=jnp.float32,
    )
    grad_probs = jnp.einsum(
        "rqhd,rkhd->rhqk", portion_grads, own_values, preferred_element_type=jnp.float32
    )
    grad_scores = (probs * (grad_probs - every_delta[..., None])).astype(jnp.bfloat16)
    grad_keys = scaling * jnp.einsum(
        "rhqk,rqhd->rkhd", grad_scores, portion_queries, preferred_element_type=jnp.float32
    )
    grad_keys, grad_values = (grad_keys, grad_values)
    grad_joint = jnp.concatenate(
        [
            grad_query.reshape(batch_rows, local_len, features),
            grad_keys.reshape(batch_rows, local_len, features),
            grad_values.reshape(batch_rows, local_len, features),
        ],
        axis=-1,
    ).astype(jnp.bfloat16)
    grad_joint_weight = outer_sum(normed_one_low, grad_joint)
    grad_joint_bias = jnp.concatenate(
        [column_sums(grad_joint[..., :features]), column_sums(grad_joint[..., 2 * features :])]
    )
    grad_normed_one = project_back(grad_joint, later_joint)
    grad_from_first, grad_gain_one, grad_shift_one = normalize_back(
        grad_normed_one, unit_one, inverse_one, later_gain_one.astype(jnp.float32)
    )
    grad_tokens = grad_middle + grad_from_first
    small_grads = (
        grad_joint_bias, grad_output_bias, grad_gain_one, grad_shift_one,
        grad_up_bias, grad_down_bias, grad_gain_two, grad_shift_two,
    )
    packed = jnp.concatenate([part.reshape(device_count, -1) for part in small_grads], axis=1)
    own = lax.psum_scatter(packed, ("dp", "blk"), scatter_dimension=0, tiled=True)[0]
    small_shards = []
    small_at = 0
    for part in small_parts:
        small_shards.append(own[small_at : small_at + part.shape[0]])
        small_at += part.shape[0]
    return (
        result,
        grad_tokens,
        scatter_sum(grad_joint_weight),
        small_shards[0],
        scatter_sum(grad_output_weight),
        small_shards[1],
        small_shards[2],
        small_shards[3],
        grad_up_shard,
        small_shards[4],
        grad_down_shard,
        small_shards[5],
        small_shards[6],
        small_shards[7],
    )


Z_SIZE, Y_SIZE, BLK_SIZE = 4, 2, 4
DP_SIZE = Z_SIZE * Y_SIZE
MESH = pl.DeviceIdType.MESH
BF = jnp.bfloat16
F32 = jnp.float32
WIDE, CHUNKS = 256, 3
TILE_WIDTHS = (24, 24, 24, 24, 24, 24, 48, 96)


def dot_nn(left, right):
    return lax.dot_general(left, right, (((1,), (0,)), ((), ())), preferred_element_type=F32)


def dot_nt(left, right):
    return lax.dot_general(left, right, (((1,), (1,)), ((), ())), preferred_element_type=F32)


def dot_tn(left, right):
    return lax.dot_general(left, right, (((0,), (0,)), ((), ())), preferred_element_type=F32)


def lane_pieces(lanes, width):
    lane = lax.broadcasted_iota(jnp.int32, (1, lanes), 1).astype(F32)
    piece = jnp.floor((lane + 0.5) * (1.0 / width))
    return piece, lane - width * piece


def piece_placer(lanes, width):
    place = lax.broadcasted_iota(jnp.int32, (128, lanes), 0).astype(F32)
    _, within = lane_pieces(lanes, width)
    return jnp.where(place == within, 1.0, 0.0).astype(BF)


def layer_kernel(*refs):
    ins, outs, scr = refs[:16], refs[16:23], refs[23:]
    (tok_in, cot_in, seg_in, pad_in, jw_in, uw_in, dw_in, ow_in), vectors = ins[:8], ins[8:]
    result_out, grad_tok_out, out_j, out_o, out_u, out_d, out_s = outs
    (
        TOK, COT, JW, UW, DW, JP0, JP1, UPW, UP, TILE, SEGT, G, SEG, KSEG, QSEG, PV, QVB,
        N1, N2, GR, WJS0, WJS1, WUS, WDS, WOS, WJ0, WJ1, WU, WO,
        U1, I1, U2, I2, MID, GM, GB,
        Q, K, V, PB, OF, AT, AR, DA, DR, DOH, GJ0, GJ1,
        GP, ACT, GH, UBS, PT, RC, SX, RX,
        GD, GU, GA, GC, GO, GO2, RYd, RYu, RYa, RYc, RYo, Sd, Su, Sa, Sc, So,
        RZd, RZu, RZa, RZc, RZo, RZ0, S0, RY0, AUs, AUr, AAs, AAr, ACs, ACr, RCo, SXo, RXo,
        TS, TB, TL, TY, TV, TZ, TW, VS, JBS, OJ, OU, OD, OO, OS, ssem, rsem, lsem,
    ) = scr
    dp = lax.axis_index("dp")
    blk = lax.axis_index("blk")
    z, y = dp // 2, dp % 2
    x, c = blk // 2, blk % 2
    count = [0, 0, 0]
    started = []

    def local(src, dst):
        n = count[1]
        count[1] += 1
        made = pltpu.make_async_copy(src, dst, lsem.at[n])
        made.start()
        return made

    def to_send():
        n = count[0]
        count[0] += 1
        return ssem.at[n]

    def to_receive():
        n = count[2]
        count[2] += 1
        return rsem.at[n]

    def group():
        return to_send(), to_receive()

    def send(src, dst, dev, sems):
        made = pltpu.make_async_remote_copy(
            src_ref=src, dst_ref=dst, send_sem=sems[0], recv_sem=sems[1],
            device_id=dev, device_id_type=MESH,
        )
        made.start()
        return made

    def wait_bytes(sem, ref):
        pltpu.make_async_copy(ref, ref, sem).wait()

    def received(copies):
        wait_bytes(copies[0][1], copies[1])

    def later_sent(copies):
        started.append(copies)

    def sent(copies):
        wait_bytes(copies[0][0], copies[1])

    started_over_z = []

    def later_sent_over_z(copies):
        started_over_z.append(copies)

    core_peer = (dp, 2 * x + 1 - c)
    x_peer = (dp, 2 * (1 - x) + c)
    far_peer = (dp, 2 * (1 - x) + 1 - c)
    blk_peers = (x_peer, far_peer, core_peer)
    y_peer = (2 * z + 1 - y, blk)
    inner = (z == 1) | (z == 2)
    z_left = (2 * ((z + Z_SIZE - 1) % Z_SIZE) + y, blk)
    z_right = (2 * ((z + 1) % Z_SIZE) + y, blk)
    z_side = (2 * ((z // 2) * 2 + 1 - z % 2) + y, blk)
    z_across = (2 * (Z_SIZE - 1 - z) + y, blk)

    def z_at(k):
        return (z + k) % Z_SIZE

    ow_copy = local(ow_in, WOS.at[blk, dp])
    jw_copy = local(jw_in, JW)
    tok_copy = local(tok_in, TOK)
    uw_copy = local(uw_in, UW)
    dw_copy = local(dw_in, DW)
    cot_copy = local(cot_in, COT)

    every = [
        ((dp + i) % DP_SIZE, (blk + j) % BLK_SIZE)
        for i in range(DP_SIZE) for j in range(BLK_SIZE) if i or j
    ]

    def entry_barrier():
        barrier = pltpu.get_barrier_semaphore()
        for dev in every:
            pl.semaphore_signal(barrier, inc=1, device_id=dev, device_id_type=MESH)
        pl.semaphore_wait(barrier, len(every))

    def swap_parts(parts, landing):
        sems = group()
        for dev in blk_peers:
            send(parts(dev[1]), landing.at[blk], dev, sems)
        span = landing.at[pl.ds(c, 3)]
        later_sent((sems, span))
        return sems, span

    def small_tiles():
        TILE[...] = jnp.zeros_like(TILE)
        for row, (ref, width) in enumerate(zip(vectors, TILE_WIDTHS)):
            TILE[row : row + 1, 0:width] = ref[...].astype(F32).reshape(1, width)
        segment = seg_in[...].astype(F32)
        SEGT[...] = jnp.zeros_like(SEGT)
        SEGT[0:2] = segment
        SEGT[2:4] = jnp.where(pad_in[...] == 1, segment, -1.0)
        G[dp, blk] = TILE[...]
        SEG[blk] = SEGT[...]


    small_tiles()
    entry_barrier()

    def stats(values):
        mean = jnp.mean(values, axis=-1, keepdims=True)
        centered = values - mean
        inverse = lax.rsqrt(jnp.mean(centered * centered, axis=-1, keepdims=True) + epsilon)
        return centered * inverse, inverse

    def dp_part(slab, span):
        return slab, span, [group(), group()] + [(None, to_receive()) for _ in range(3)]

    def slabs_part(slabs):
        return dp_part(lambda i: slabs.at[i], lambda n: slabs.at[pl.ds(c, n)])

    def own_over_y(part):
        slab, span, sems = part
        send(slab(dp), slab(dp), y_peer, sems[0])
        later_sent((sems[0], span(4)))

    def own_over_z(part):
        slab, span, sems = part

        @pl.when(z < Z_SIZE - 1)
        def _():
            send(slab(dp), slab(dp), z_right, (sems[1][0], sems[1][1]))

        @pl.when(z > 0)
        def _():
            send(slab(dp), slab(dp), z_left, (sems[1][0], sems[2][1]))

        later_sent_over_z((sems[1], span(1), span(5)))

    def pass_on(part, there, arrived, onward, more, dev):
        slab, _, sems = part
        received((arrived, slab(there)))
        send(slab(there), slab(there), y_peer, sems[0])
        if onward is not None:

            @pl.when(more)
            def _():
                send(slab(there), slab(there), dev, (sems[1][0], onward[1]))

    def step_one(part):
        sems = part[2]

        @pl.when(z > 0)
        def _():
            pass_on(part, dp - 2, sems[1], sems[3], z < Z_SIZE - 1, z_right)

        @pl.when(z < Z_SIZE - 1)
        def _():
            pass_on(part, dp + 2, sems[2], sems[3], z > 0, z_left)

    def step_two(part):
        sems = part[2]

        @pl.when(z >= 2)
        def _():
            pass_on(part, dp - 4, sems[3], sems[4], z == 2, z_right)

        @pl.when(z < 2)
        def _():
            pass_on(part, dp + 4, sems[3], sems[4], z == 1, z_left)

    def step_three(part):
        sems = part[2]

        @pl.when(z == Z_SIZE - 1)
        def _():
            pass_on(part, dp - 6, sems[4], None, None, None)

        @pl.when(z == 0)
        def _():
            pass_on(part, dp + 6, sems[4], None, None, None)

    def dp_end(part):
        _, span, sems = part
        received((sems[0], span(4)))

    def gather_start(buf, r):
        over_x, to_core = group(), group()
        send(buf.at[r, blk], buf.at[r, blk], x_peer, over_x)
        send(buf.at[r, blk], buf.at[r, blk], core_peer, to_core)
        later_sent((over_x, buf.at[r, blk]))
        later_sent((to_core, buf.at[r, pl.ds(c, 2)]))
        return buf, r, over_x, to_core

    def gather_forward(part):
        buf, r, over_x, to_core = part
        received((over_x, buf.at[r, x_peer[1]]))
        send(buf.at[r, x_peer[1]], buf.at[r, x_peer[1]], core_peer, to_core)

    def gather_end(part):
        buf, r, _, to_core = part
        received((to_core, buf.at[r, pl.ds(c, 2)]))

    ow_copy.wait()
    o_part = dp_part(lambda i: WOS.at[blk, i], lambda n: WOS.at[blk, pl.ds(c, n)])
    a_part, c_part, g_part = slabs_part(WJS0), slabs_part(WJS1), slabs_part(G)
    u_part = [slabs_part(WUS.at[n]) for n in range(CHUNKS)]
    d_part = [slabs_part(WDS.at[n]) for n in range(CHUNKS)]
    own_over_z(o_part)
    own_over_y(o_part)

    def split_joint():
        jw_copy.wait()
        for b in range(BLK_SIZE):
            for s in range(3):
                at = 768 * s + 192 * b
                JP0[b, :, 64 * s : 64 * (s + 1)] = JW[:, at : at + 64]
                JP1[b, :, 128 * s : 128 * (s + 1)] = JW[:, at + 64 : at + 192]

    def swap_columns(parts, slabs):
        slabs[dp, blk] = parts[blk]
        return swap_parts(lambda b: parts.at[b], slabs.at[dp])

    split_joint()
    a_first = swap_columns(JP0, WJS0)
    g_first = swap_parts(lambda b: TILE, G.at[dp])
    c_first = swap_columns(JP1, WJS1)
    seg_copies = swap_parts(lambda b: SEGT, SEG)

    def first_stats():
        tok_copy.wait()
        firsts = []
        for r in range(2):
            unit, inverse = stats(TOK[r])
            U1[r] = unit
            I1[r] = inverse
            N1[r, blk] = unit.astype(BF)
            firsts.append(gather_start(N1, r))
        return firsts

    n1_part = first_stats()
    n1_sent = (started[-4:-2], started[-2:])
    del started[-4:]

    def split_up():
        uw_copy.wait()
        for i in range(DP_SIZE):
            for b in range(BLK_SIZE):
                at = 96 * (BLK_SIZE * i + b)
                UPW[b, :, 96 * i : 96 * (i + 1)] = UW[:, at : at + 96]
        for n in range(CHUNKS):
            for b in range(BLK_SIZE):
                UP[n, b] = UPW[b, :, WIDE * n : WIDE * (n + 1)]

    def split_down():
        dw_copy.wait()
        for n in range(CHUNKS):
            WDS[n, dp] = DW[:, WIDE * n : WIDE * (n + 1)]

    def early_down():
        split_down()
        for part in d_part:
            own_over_y(part)

    def low_cotangent():
        cot_copy.wait()
        for r in range(2):
            GR[r, blk] = COT[r].astype(BF)

    early_down()
    received(a_first)
    own_over_z(a_part)
    own_over_y(a_part)
    received(g_first)
    own_over_z(g_part)
    own_over_y(g_part)
    received(c_first)
    own_over_z(c_part)
    own_over_y(c_part)
    split_up()
    u_first = [swap_columns(UP.at[n], WUS.at[n]) for n in range(CHUNKS)]
    low_cotangent()
    gr_part = [gather_start(GR, r) for r in range(2)]
    step_one(a_part)
    step_one(g_part)
    step_one(o_part)
    step_two(a_part)
    step_two(g_part)
    step_two(o_part)
    gather_forward(n1_part[0])
    step_one(c_part)
    step_three(a_part)
    step_three(g_part)
    step_three(o_part)
    step_two(c_part)
    for n in range(CHUNKS):
        received(u_first[n])
        own_over_z(u_part[n])
    own_over_z(d_part[0])
    own_over_z(d_part[1])
    gather_forward(n1_part[1])
    dev_id = lax.broadcasted_iota(jnp.int32, (32, 1, 1), 0).astype(F32)
    blk_f = blk.astype(F32)
    piece24, _ = lane_pieces(768, 24)
    piece48, _ = lane_pieces(192, 48)
    piece96, _ = lane_pieces(768, 96)

    def mask24():
        return piece24[None] == dev_id

    def mask48(first_dev):
        return piece48[None] + (4.0 * blk_f + first_dev) == dev_id

    def mask96():
        return 4.0 * piece96[None] + blk_f == dev_id

    def place24():
        return piece_placer(768, 24)

    def place48():
        return piece_placer(192, 48)

    def place96():
        return piece_placer(768, 96)

    def small_end():
        dp_end(g_part)
        tiles = G[...].reshape(32 * 8, 128).astype(BF)

        def placed(placer, mask, lanes):
            spread = dot_nn(tiles, placer).reshape(32, 8, lanes)
            return jnp.sum(jnp.where(mask, spread, 0.0), axis=0)

        PV[0:8] = placed(place24(), mask24(), 768)
        PV[8:16] = placed(place96(), mask96(), 768)
        QVB[0:8] = placed(place48(), mask48(0.0), 192)
        QVB[8:16] = placed(place48(), mask48(16.0), 192)

    def segments_end():
        received(seg_copies)
        eye = jnp.where(
            lax.broadcasted_iota(jnp.int32, (128, 128), 0)
            == lax.broadcasted_iota(jnp.int32, (128, 128), 1), 1.0, 0.0,
        ).astype(BF)
        for b in range(BLK_SIZE):
            part = SEG[b]
            KSEG[:, 128 * b : 128 * (b + 1)] = part
            QSEG[128 * b : 128 * (b + 1)] = dot_nt(eye, part.astype(BF))


    segments_end()
    small_end()
    gain1, shift1, obias = PV[0:1], PV[1:2], PV[2:3]
    gain2, shift2, dbias = PV[3:4], PV[4:5], PV[5:6]

    def compact(slabs, whole):
        for i in range(DP_SIZE):
            rows = slabs(i).astype(F32)
            rows = rows.reshape(96, rows.shape[-1])
            whole[96 * i : 96 * (i + 1), :] = rows.astype(BF)

    def norm_rows(r):
        gather_end(n1_part[r])
        for copies in n1_sent[r]:
            sent(copies)
        for b in range(BLK_SIZE):
            N1[r, b] = (N1[r, b].astype(F32) * gain1 + shift1).astype(BF)

    def qkv_one(r):
        joint = dot_nn(N1[r].reshape(512, 768), WJ0[...])
        qbias, vbias = QVB[6:7, 0:64], QVB[14:15, 0:64]
        Q[r, 0] = ((joint[:, :64] + qbias).astype(BF).astype(F32) * 0.125).astype(BF)
        K[r, 0] = joint[:, 64:128].astype(BF)
        V[r, 0] = (joint[:, 128:] + vbias).astype(BF)

    def qkv_two(r):
        joint = dot_nn(N1[r].reshape(512, 768), WJ1[...])
        qbias, vbias = QVB[6:7, 64:192], QVB[14:15, 64:192]
        query = ((joint[:, :128] + qbias).astype(BF).astype(F32) * 0.125).astype(BF)
        keys = joint[:, 128:256].astype(BF)
        values = (joint[:, 256:] + vbias).astype(BF)
        for h in (1, 2):
            lanes = slice(64 * (h - 1), 64 * h)
            Q[r, h] = query[:, lanes]
            K[r, h] = keys[:, lanes]
            V[r, h] = values[:, lanes]

    def attend(r, h):
        scores = dot_nt(Q[r, h], K[r, h])
        scores = jnp.where(QSEG[:, r : r + 1] == KSEG[2 + r : 3 + r, :], scores, masked_score)
        top = jnp.max(scores, axis=-1, keepdims=True)
        expos = jnp.exp(scores - top)
        total = jnp.sum(expos, axis=-1, keepdims=True)
        probs = (expos * (1.0 / total)).astype(BF)
        PB[r, h] = probs
        out = dot_nn(probs, V[r, h])
        OF[r, h] = out
        if h:
            AT[r, :, 0:128, 64 * (h - 1) : 64 * h] = out.astype(BF).reshape(4, 128, 64)
        else:
            halves = out.astype(BF).reshape(4, 2, 64, 64)
            AT[r, :, 128:192, 0:64] = halves[:, 0]
            AT[r, :, 128:192, 64:128] = halves[:, 1]

    def swap_heads(src, dst, r):
        dst[r, blk] = src[r, blk]
        return swap_parts(lambda b: src.at[r, b], dst.at[r])

    dp_end(a_part)
    compact(lambda i: WJS0[i], WJ0)
    norm_rows(0)
    qkv_one(0)
    step_three(c_part)
    attend(0, 0)
    for n in range(CHUNKS):
        own_over_y(u_part[n])
    dp_end(o_part)
    wo_x, wo_core = group(), group()
    send(WOS.at[blk], WOS.at[blk], x_peer, wo_x)
    send(WOS.at[blk], WOS.at[blk], core_peer, wo_core)
    later_sent((wo_x, WOS.at[blk]))
    later_sent((wo_core, WOS.at[pl.ds(c, 2)]))
    norm_rows(1)
    qkv_one(1)
    attend(1, 0)
    for n in range(CHUNKS):
        step_one(u_part[n])
    own_over_z(d_part[2])
    dp_end(c_part)
    compact(lambda i: WJS1[i], WJ1)
    qkv_two(0)
    attend(0, 1)
    attend(0, 2)
    at_copies = [swap_heads(AT, AR, 0)]
    gather_forward(gr_part[0])
    for n in range(CHUNKS):
        step_two(u_part[n])
    for n in range(CHUNKS):
        step_one(d_part[n])
    qkv_two(1)
    attend(1, 1)
    attend(1, 2)
    at_copies.append(swap_heads(AT, AR, 1))
    received((wo_x, WOS.at[x_peer[1]]))
    send(WOS.at[x_peer[1]], WOS.at[x_peer[1]], core_peer, wo_core)
    received((wo_core, WOS.at[pl.ds(c, 2)]))
    compact(lambda i: WOS[:, i], WO)

    def head_zero(block):
        packed = block[128:192]
        return jnp.concatenate([packed[:, 0:64], packed[:, 64:128]], axis=0)

    def middle_rows(r):
        received(at_copies[r])
        total = TOK[r] + obias
        for b in range(BLK_SIZE):
            block = AR[r, b]
            total = total + dot_nn(head_zero(block), WO[192 * b : 192 * b + 64, :])
            total = total + dot_nn(block[0:128], WO[192 * b + 64 : 192 * (b + 1), :])
        MID[r] = total
        unit, inverse = stats(total)
        U2[r] = unit
        I2[r] = inverse
        N2[r, blk] = (unit * gain2 + shift2).astype(BF)
        return gather_start(N2, r)

    n2_part = [middle_rows(0)]
    for n in range(CHUNKS):
        step_three(u_part[n])
    for n in range(CHUNKS):
        step_two(d_part[n])
    n2_part.append(middle_rows(1))
    gather_forward(gr_part[1])
    for n in range(CHUNKS):
        dp_end(u_part[n])
        compact(lambda i: WUS[n, i], WU.at[n])
    gather_forward(n2_part[0])
    for n in range(CHUNKS):
        step_three(d_part[n])
    gather_end(n2_part[0])

    def rows_of(buf, r):
        return buf[r].reshape(512, 768)

    def up(r):
        for n in range(CHUNKS):
            cols = slice(WIDE * n, WIDE * (n + 1))
            hidden = dot_nn(rows_of(N2, r), WU[n]) + PV[15:16, cols]
            square = hidden * hidden
            bent = jnp.tanh(hidden * (0.7978845608028654 + 0.035677408136300125 * square))
            half = 0.5 * (1.0 + bent)
            ACT[r, :, cols] = (hidden * half).astype(BF)
            slope = 0.3989422804014327 + 0.05351611220445019 * square
            GP[r, :, cols] = (half + hidden * (1.0 - bent * bent) * slope).astype(BF)

    def hidden_back(r):
        for n in range(2):
            cols = slice(384 * n, 384 * (n + 1))
            rows = rows_of(GR, r)
            grad = 0.0
            for m in range(CHUNKS):
                weight = WDS[m, 4 * n : 4 * (n + 1)].reshape(384, WIDE)
                grad = grad + dot_nt(rows[:, WIDE * m : WIDE * (m + 1)], weight)
            grad = (grad * GP[r, :, cols].astype(F32)).astype(BF)
            GH[r, :, cols] = grad
            UBS[r, :, cols] = jnp.sum(grad.astype(F32), axis=0, keepdims=True)

    def sum_store(i, r, cols, values):
        PT[i, r, :, :, :, cols] = values.reshape(2, 2, 128, values.shape[-1]).astype(BF)

    def sum_start(i, r):
        sems = group()
        send(PT.at[i, r, :, 1 - c], RC.at[i, r], core_peer, sems)
        later_sent((sems, RC.at[i, r]))
        return sems, RC.at[i, r]

    def sum_middle(i, r, first):
        received(first)
        SX[i, r] = (PT[i, r, 1 - x, c].astype(F32) + RC[i, r, 1 - x].astype(F32)).astype(BF)
        sems = group()
        send(SX.at[i, r], RX.at[i, r], x_peer, sems)
        later_sent((sems, RX.at[i, r]))
        return sems, RX.at[i, r]

    def sum_end(i, r, second):
        received(second)
        return PT[i, r, x, c].astype(F32) + RC[i, r, x].astype(F32) + RX[i, r].astype(F32)

    def second_back(r):
        for n in range(3):
            cols = slice(256 * n, 256 * (n + 1))
            grad = 0.0
            for m in range(CHUNKS):
                grad = grad + dot_nt(GH[r, :, WIDE * m : WIDE * (m + 1)], WU[m, cols, :])
            sum_store(0, r, cols, grad)
        return sum_start(0, r)

    def first_back(r):
        for n in range(3):
            cols = slice(256 * n, 256 * (n + 1))
            sum_store(
                2, r, cols, dot_nt(GJ0[r], WJ0[cols, :]) + dot_nt(GJ1[r], WJ1[cols, :])
            )
        return sum_start(2, r)

    def down(r):
        for n in range(CHUNKS):
            cols = slice(WIDE * n, WIDE * (n + 1))
            sum_store(1, r, cols, dot_nn(ACT[r], WDS[n].reshape(768, WIDE)))
        return sum_start(1, r)

    def scatter_start(parts, recv):
        sems = group()
        send(parts.at[:, 1 - y], recv, y_peer, sems)
        later_sent((sems, recv))
        return sems, recv

    def scatter_middle(parts, recv, sums, landing, first):
        received(first)
        sums[...] = (parts[:, y].astype(F32) + recv[...].astype(F32)).astype(BF)
        sems = group()
        for k in range(1, Z_SIZE):
            send(sums.at[z_at(k)], landing.at[k - 1], (2 * z_at(k) + y, blk), sems)
        later_sent((sems, landing))
        return sums, landing, (sems, landing)

    def scatter_end(sums, landing, second):
        received(second)
        total = sums[z].astype(F32)
        for k in range(Z_SIZE - 1):
            total = total + landing[k].astype(F32)
        return total

    def return_columns(part, sends, recvs):
        sends[...] = scatter_end(*part).astype(BF)
        recvs[blk] = sends[blk]
        return swap_parts(lambda b: sends.at[b], recvs)

    def down_grad(n):
        grads = GR[:, :, :, WIDE * n : WIDE * (n + 1)].reshape(1024, WIDE)
        for m in range(2):
            cols = slice(384 * m, 384 * (m + 1))
            grad = dot_tn(ACT[:, :, cols].reshape(1024, 384), grads)
            GD[n, 2 * m : 2 * m + 2] = grad.reshape(2, 2, 96, WIDE).astype(BF)

    def row_grad(rows, grads, parts):
        for m in range(2):
            cols = slice(384 * m, 384 * (m + 1))
            grad = dot_tn(rows[:, :, :, cols].reshape(1024, 384), grads)
            parts[2 * m : 2 * m + 2] = grad.reshape(2, 2, 4, 24, grad.shape[-1]).astype(BF)

    def up_grad(n):
        row_grad(N2, GH[:, :, WIDE * n : WIDE * (n + 1)].reshape(1024, WIDE), GU.at[n])

    def joint_grad_one():
        row_grad(N1, GJ0[...].reshape(1024, 192), GA)
        return scatter_start(GA, RYa)

    def joint_grad_two():
        row_grad(N1, GJ1[...].reshape(1024, 384), GC)
        return scatter_start(GC, RYc)

    def output_grad():
        for b in range(BLK_SIZE):
            blocks = [AR[r, b] for r in range(2)]
            zero = jnp.concatenate([head_zero(block) for block in blocks], axis=0)
            rest = jnp.concatenate([block[0:128] for block in blocks], axis=0)
            grads = GB[...].reshape(256, 768)
            grad = jnp.concatenate([dot_tn(zero, grads), dot_tn(rest, grads)], axis=0)
            grad = grad.reshape(2, 4, 24, 768).astype(BF)
            for i in range(4):
                GO[i // 2, i % 2, 2 * b : 2 * b + 2] = grad[:, i]
        sems = group()
        send(GO.at[:, 1 - c], RCo, core_peer, sems)
        later_sent((sems, RCo))
        return sems, RCo

    def output_grad_middle(first):
        received(first)
        SXo[...] = (GO[1 - x, c].astype(F32) + RCo[1 - x].astype(F32)).astype(BF)
        sems = group()
        send(SXo, RXo, x_peer, sems)
        later_sent((sems, RXo))
        return sems, RXo

    def norm_back(e, unit, inverse, gain):
        f = e * gain
        grad = inverse * (
            f - jnp.mean(f, axis=-1, keepdims=True)
            - unit * jnp.mean(f * unit, axis=-1, keepdims=True)
        )
        return (
            grad, jnp.sum(e * unit, axis=0, keepdims=True), jnp.sum(e, axis=0, keepdims=True)
        )

    def second_norm_back(r, second):
        e = sum_end(0, r, second)
        grad, of_gain, of_shift = norm_back(e, U2[r], I2[r], gain2)
        grad = grad + COT[r]
        GM[r] = grad
        low = grad.astype(BF)
        GB[r] = low
        for b in range(BLK_SIZE):
            zero = dot_nt(low, WO[192 * b : 192 * b + 64, :]).astype(BF)
            DA[r, b, 128:192, 0:64] = zero[0:64]
            DA[r, b, 128:192, 64:128] = zero[64:128]
            DA[r, b, 0:128] = dot_nt(low, WO[192 * b + 64 : 192 * (b + 1), :]).astype(BF)
        copies = swap_heads(DA, DR, r)
        VS[3:4] += of_gain
        VS[4:5] += of_shift
        VS[2:3] += jnp.sum(low.astype(F32), axis=0, keepdims=True)
        VS[5:6] += jnp.sum(COT[r].astype(BF).astype(F32), axis=0, keepdims=True)
        return copies

    def attend_back(r, h):
        if h:
            DOH[...] = DR[r, :, 0:128, 64 * (h - 1) : 64 * h].reshape(512, 64)
        else:
            for t in range(4):
                DOH[128 * t : 128 * t + 64] = DR[r, t, 128:192, 0:64]
                DOH[128 * t + 64 : 128 * (t + 1)] = DR[r, t, 128:192, 64:128]
        grad_out = DOH[...]
        delta = jnp.sum(grad_out.astype(F32) * OF[r, h], axis=-1, keepdims=True)
        grad_probs = dot_nt(grad_out, V[r, h])
        grad_scores = (PB[r, h].astype(F32) * (grad_probs - delta)).astype(BF)
        grads = (
            (dot_nn(grad_scores, K[r, h]) * 0.125).astype(BF),
            dot_tn(grad_scores, Q[r, h]).astype(BF),
            dot_tn(PB[r, h], grad_out).astype(BF),
        )
        for s, grad in enumerate(grads):
            if h == 0:
                GJ0[r, :, 64 * s : 64 * (s + 1)] = grad
            else:
                at = 128 * s + 64 * (h - 1)
                GJ1[r, :, at : at + 64] = grad

    def z_first_start(parts, landing):
        sems = group()
        for k in range(1, Z_SIZE):
            send(parts.at[z_at(k)], landing.at[k - 1], (2 * z_at(k) + y, blk), sems)
        later_sent((sems, landing))
        return sems, landing

    def z_first_middle(parts, landing, sums, recv, first):
        received(first)
        total = parts[z].astype(F32)
        for k in range(Z_SIZE - 1):
            total = total + landing[k].astype(F32)
        sums[...] = total.astype(BF)
        sems = group()
        send(sums.at[1 - y], recv, y_peer, sems)
        later_sent((sems, recv))
        return sems, recv

    def z_first_end(sums, recv, second):
        received(second)
        return sums[y].astype(F32) + recv[...].astype(F32)

    def output_grad_over_dp(second):
        received(second)
        GO2[...] = (
            GO[x, c].astype(F32) + RCo[x].astype(F32) + RXo[...].astype(F32)
        ).astype(BF).reshape(4, 2, 24, 768)
        return scatter_start(GO2, RYo)

    def vector_sums():
        for r in range(2):
            JBS[r, :, 0:192] = jnp.sum(GJ0[r].astype(F32), axis=0, keepdims=True)
            JBS[r, :, 192:576] = jnp.sum(GJ1[r].astype(F32), axis=0, keepdims=True)

    def first_norm_back(r, second):
        e = sum_end(2, r, second)
        grad, of_gain, of_shift = norm_back(e, U1[r], I1[r], gain1)
        GM[r] = GM[r] + grad
        VS[0:1] += of_gain
        VS[1:2] += of_shift

    VS[...] = jnp.zeros_like(VS)
    d_first, d_second, u_grad_first, u_grad_second = [], [], [], []

    def d_over_y(n):
        d_first.append(scatter_start(GD.at[n], RYd.at[n]))

    def d_over_z(n):
        d_second.append(scatter_middle(GD.at[n], RYd.at[n], Sd.at[n], RZd.at[n], d_first[n]))

    def u_over_y(n):
        u_grad_first.append(scatter_start(GU.at[n], RYu.at[n]))

    def u_over_z(n):
        u_grad_second.append(
            scatter_middle(GU.at[n], RYu.at[n], Su.at[n], RZu.at[n], u_grad_first[n])
        )

    up(0)
    gather_forward(n2_part[1])
    gather_end(gr_part[0])
    gather_end(gr_part[1])
    gather_end(n2_part[1])
    up(1)
    down_grad(0)
    d_near_first = z_first_start(GD.at[0], RZ0)
    d_first.append(None)
    d_second.append(None)
    down_grad(1)
    d_over_y(1)
    for n in range(CHUNKS):
        dp_end(d_part[n])
    hidden_back(0)
    second_first = [second_back(0)]
    down_grad(2)
    d_over_y(2)
    hidden_back(1)
    second_second = [sum_middle(0, 0, second_first[0])]
    second_first.append(second_back(1))
    up_grad(0)
    u_over_y(0)
    second_second.append(sum_middle(0, 1, second_first[1]))
    up_grad(1)
    u_over_y(1)
    d_over_z(1)
    up_grad(2)
    u_over_y(2)
    da_copies = [second_norm_back(0, second_second[0])]
    d_over_z(2)
    result_first = [down(0), down(1)]
    da_copies.append(second_norm_back(1, second_second[1]))
    o_first = output_grad()
    received(da_copies[0])
    attend_back(0, 1)
    o_second = output_grad_middle(o_first)
    attend_back(0, 2)
    d_near_second = z_first_middle(GD.at[0], RZ0, S0, RY0, d_near_first)
    u_over_z(0)
    received(da_copies[1])
    attend_back(1, 1)
    attend_back(1, 2)
    c_grad_first = joint_grad_two()
    u_over_z(1)
    attend_back(0, 0)
    first_first = [first_back(0)]
    attend_back(1, 0)
    a_grad_first = joint_grad_one()
    first_second = [sum_middle(2, 0, first_first[0])]
    u_over_z(2)
    first_first.append(first_back(1))
    o_grad_first = output_grad_over_dp(o_second)
    first_second.append(sum_middle(2, 1, first_first[1]))
    result_second = [sum_middle(1, 0, result_first[0])]
    vector_sums()
    out_copies = []

    def down_out():
        OD[:, 0:WIDE] = z_first_end(S0, RY0, d_near_second)
        for n in range(1, CHUNKS):
            OD[:, WIDE * n : WIDE * (n + 1)] = scatter_end(*d_second[n])
        out_copies.append(local(OD, out_d))

    row = lax.broadcasted_iota(jnp.int32, (8, 1), 0)

    def picked(values, mask, placer):
        wide = jnp.where(mask, values[None], 0.0)
        wide = wide.reshape(256, wide.shape[-1])
        high = wide.astype(BF)
        rest = (wide - high.astype(F32)).astype(BF)
        return dot_nt(high, placer) + dot_nt(rest, placer)

    def vectors_early():
        joint = JBS[0] + JBS[1]
        queries = jnp.concatenate([joint[:, 0:64], joint[:, 192:320]], axis=1)
        values = jnp.concatenate([joint[:, 128:192], joint[:, 448:576]], axis=1)
        pieces = picked(jnp.where(row == 7, UBS[0] + UBS[1], 0.0), mask96(), place96())
        pieces += picked(jnp.where(row == 6, queries, 0.0), mask48(0.0), place48())
        pieces += picked(jnp.where(row == 6, values, 0.0), mask48(16.0), place48())
        TS[...] = pieces

    def vectors_over_blk():
        pieces = (TS[...] + picked(VS[...], mask24(), place24())).reshape(8, 4, 8, 128)
        for b in range(BLK_SIZE):
            TB[b] = pieces[:, b]
        TL[blk] = TB[blk]
        return swap_parts(lambda b: TB.at[b], TL)

    def vectors_over_y(first):
        received(first)
        TY[...] = ((TL[0] + TL[1]) + (TL[2] + TL[3])).reshape(4, 2, 8, 128)
        sems = group()
        send(TY.at[:, 1 - y], TV, y_peer, sems)
        later_sent((sems, TV))
        return sems, TV

    def vectors_over_z(first):
        received(first)
        TZ[...] = TY[:, y] + TV[...]
        sems = group()
        for k in range(1, Z_SIZE):
            send(TZ.at[z_at(k)], TW.at[k - 1], (2 * z_at(k) + y, blk), sems)
        later_sent((sems, TW))
        return sems, TW

    def vectors_end(first):
        received(first)
        OS[...] = TZ[z] + (TW[0] + (TW[1] + TW[2]))
        out_copies.append(local(OS, out_s))

    vectors_early()
    c_grad_second = scatter_middle(GC, RYc, Sc, RZc, c_grad_first)
    first_norm_back(0, first_second[0])
    a_grad_second = scatter_middle(GA, RYa, Sa, RZa, a_grad_first)
    first_norm_back(1, first_second[1])
    o_grad_second = scatter_middle(GO2, RYo, So, RZo, o_grad_first)
    vector_part = vectors_over_blk()
    result_second.append(sum_middle(1, 1, result_first[1]))
    out_copies.append(local(GM, grad_tok_out))
    vector_part = vectors_over_y(vector_part)
    down_out()

    u_back = [
        return_columns(u_grad_second[n], AUs.at[n], AUr.at[n])
        for n in range(CHUNKS)
    ]

    vector_part = vectors_over_z(vector_part)
    c_back = return_columns(c_grad_second, ACs, ACr)
    a_back = return_columns(a_grad_second, AAs, AAr)

    def up_out():
        for part in u_back:
            received(part)
        for b in range(BLK_SIZE):
            whole = jnp.concatenate([AUr[n, b] for n in range(CHUNKS)], axis=1).astype(F32)
            for i in range(DP_SIZE):
                at = 96 * (BLK_SIZE * i + b)
                OU[:, at : at + 96] = whole[:, 96 * i : 96 * (i + 1)]
        return local(OU, out_u)

    out_copies.append(up_out())
    OO[...] = scatter_end(*o_grad_second)
    out_copies.append(local(OO, out_o))
    def joint_out():
        received(c_back)
        received(a_back)
        for b in range(BLK_SIZE):
            one, two = AAr[b].astype(F32), ACr[b].astype(F32)
            for s in range(3):
                at = 768 * s + 192 * b
                OJ[:, at : at + 64] = one[:, 64 * s : 64 * (s + 1)]
                OJ[:, at + 64 : at + 192] = two[:, 128 * s : 128 * (s + 1)]
        return local(OJ, out_j)

    def result_end():
        for r in range(2):
            MID[r] = MID[r] + sum_end(1, r, result_second[r]) + dbias
        out_copies.append(local(MID, result_out))

    result_end()
    vectors_end(vector_part)
    out_copies.append(joint_out())
    assert count[0] <= SENDS and count[2] <= RECEIVES
    for copies in started:
        sent(copies)

    @pl.when(inner)
    def _():
        for sems, _, five in started_over_z:
            sent((sems, five))

    @pl.when(jnp.logical_not(inner))
    def _():
        for sems, one, _ in started_over_z:
            sent((sems, one))

    for made in out_copies:
        made.wait()


def finish_kernel(*refs):
    big_in, sums, big_out, small_out = refs[:6], refs[6], refs[7:13], refs[13:21]
    for source, target in zip(big_in, big_out):
        target[...] = source[...]
    for row, width in enumerate(TILE_WIDTHS):
        small_out[row][...] = sums[row, 0:width]


def fast_device(
    tokens, segment_ids, pad_mask, joint_weight, joint_bias, output_weight, output_bias,
    first_gain, first_shift, up_weight, up_bias, down_weight, down_bias,
    second_gain, second_shift, cotangent,
):
    vectors = (
        first_gain, first_shift, output_bias, second_gain, second_shift, down_bias,
        joint_bias, up_bias,
    )

    def vm(*shape, dtype=BF):
        return pltpu.VMEM(shape, dtype)

    def fm(*shape):
        return pltpu.VMEM(shape, F32)

    scratch = [
        fm(2, 128, 768), fm(2, 128, 768), vm(24, 2304), vm(24, 3072), vm(96, 768),
        vm(4, 24, 192), vm(4, 24, 384), vm(4, 24, 768), vm(CHUNKS, 4, 24, WIDE), fm(8, 128), fm(8, 128), fm(8, 4, 8, 128),
        fm(4, 8, 128), fm(8, 512), fm(512, 8), fm(16, 768), fm(16, 192),
        vm(2, 4, 128, 768), vm(2, 4, 128, 768), vm(2, 4, 128, 768),
        vm(8, 4, 24, 192), vm(8, 4, 24, 384), vm(CHUNKS, 8, 4, 24, WIDE), vm(CHUNKS, 8, 96, WIDE),
        vm(4, 8, 24, 768), vm(768, 192), vm(768, 384), vm(CHUNKS, 768, WIDE), vm(768, 768),
        fm(2, 128, 768), fm(2, 128, 1), fm(2, 128, 768), fm(2, 128, 1),
        fm(2, 128, 768), fm(2, 128, 768), vm(2, 128, 768),
        vm(2, 3, 512, 64), vm(2, 3, 512, 64), vm(2, 3, 512, 64), vm(2, 3, 512, 512),
        fm(2, 3, 512, 64), vm(2, 4, 192, 128), vm(2, 4, 192, 128),
        vm(2, 4, 192, 128), vm(2, 4, 192, 128), vm(512, 64), vm(2, 512, 192), vm(2, 512, 384),
        vm(2, 512, 768), vm(2, 512, 768), vm(2, 512, 768), fm(2, 1, 768),
        vm(3, 2, 2, 2, 128, 768), vm(3, 2, 2, 128, 768), vm(3, 2, 128, 768), vm(3, 2, 128, 768),
        vm(CHUNKS, 4, 2, 96, WIDE), vm(CHUNKS, 4, 2, 4, 24, WIDE), vm(4, 2, 4, 24, 192), vm(4, 2, 4, 24, 384),
        vm(2, 2, 8, 24, 768), vm(4, 2, 24, 768),
        vm(CHUNKS, 4, 96, WIDE), vm(CHUNKS, 4, 4, 24, WIDE), vm(4, 4, 24, 192), vm(4, 4, 24, 384), vm(4, 24, 768),
        vm(CHUNKS, 4, 96, WIDE), vm(CHUNKS, 4, 4, 24, WIDE), vm(4, 4, 24, 192), vm(4, 4, 24, 384), vm(4, 24, 768),
        vm(CHUNKS, 3, 96, WIDE), vm(CHUNKS, 3, 4, 24, WIDE), vm(3, 4, 24, 192), vm(3, 4, 24, 384), vm(3, 24, 768),
        vm(3, 2, 96, WIDE), vm(2, 96, WIDE), vm(96, WIDE),
        vm(CHUNKS, 4, 24, WIDE), vm(CHUNKS, 4, 24, WIDE), vm(4, 24, 192), vm(4, 24, 192),
        vm(4, 24, 384), vm(4, 24, 384), vm(2, 8, 24, 768), vm(8, 24, 768), vm(8, 24, 768),
        fm(256, 128), fm(4, 8, 8, 128), fm(4, 8, 8, 128), fm(4, 2, 8, 128), fm(4, 8, 128),
        fm(4, 8, 128), fm(3, 8, 128), fm(8, 768), fm(2, 1, 576),
        fm(24, 2304), fm(24, 3072), fm(96, 768), fm(24, 768), fm(8, 128),
        pltpu.SemaphoreType.DMA((SENDS,)), pltpu.SemaphoreType.DMA((RECEIVES,)),
        pltpu.SemaphoreType.DMA((16,)),
    ]
    vmem = pl.BlockSpec(memory_space=pltpu.VMEM)
    anywhere = pl.BlockSpec(memory_space=pl.ANY)
    out_shapes = [
        (2, 128, 768), (2, 128, 768), (24, 2304), (24, 768), (24, 3072), (96, 768), (8, 128),
    ]
    made = pl.pallas_call(
        layer_kernel,
        out_shape=[jax.ShapeDtypeStruct(shape, F32) for shape in out_shapes],
        in_specs=[anywhere] * 2 + [vmem] * 2 + [anywhere] * 4 + [vmem] * 8,
        out_specs=[anywhere] * 7,
        scratch_shapes=scratch,
        compiler_params=pltpu.CompilerParams(
            collective_id=0, has_side_effects=True, vmem_limit_bytes=VMEM_MIB * 2**20
        ),
        cost_estimate=pl.CostEstimate(
            flops=13 * 10**9, bytes_accessed=6 * 10**6, transcendentals=4 * 10**6
        ),
    )(
        tokens, cotangent, segment_ids, pad_mask, joint_weight, up_weight, down_weight,
        output_weight, *vectors,
    )
    ends = pl.pallas_call(
        finish_kernel,
        out_shape=[jax.ShapeDtypeStruct(shape, F32) for shape in out_shapes[:6]]
        + [jax.ShapeDtypeStruct((width,), F32) for width in TILE_WIDTHS],
        in_specs=[vmem] * 7,
        out_specs=[vmem] * 14,
    )(*made)
    result, grad_tokens, grad_j, grad_o, grad_u, grad_d = ends[:6]
    first_g, first_s, output_b, second_g, second_s, down_b, joint_b, up_b = ends[6:]
    return (
        result, grad_tokens, grad_j, joint_b, grad_o, output_b, first_g, first_s,
        grad_u, up_b, grad_d, down_b, second_g, second_s,
    )


def solution(mesh):
    placed = (
        P("dp", "blk", None),
        P("dp", "blk"),
        P("dp", "blk"),
        P(("dp", "blk"), None),
        P(("dp", "blk")),
        P(("dp", "blk"), None),
        P(("dp", "blk")),
        P(("dp", "blk")),
        P(("dp", "blk")),
        P(("dp", "blk"), None),
        P(("dp", "blk")),
        P(("dp", "blk"), None),
        P(("dp", "blk")),
        P(("dp", "blk")),
        P(("dp", "blk")),
        P("dp", "blk", None),
    )

    def spread(device_part):
        return jax.shard_map(
            device_part,
            mesh=mesh,
            in_specs=placed,
            out_specs=(
                P("dp", "blk", None),
                P("dp", "blk", None),
                P(("dp", "blk"), None),
                P(("dp", "blk")),
                P(("dp", "blk"), None),
                P(("dp", "blk")),
                P(("dp", "blk")),
                P(("dp", "blk")),
                P(("dp", "blk"), None),
                P(("dp", "blk")),
                P(("dp", "blk"), None),
                P(("dp", "blk")),
                P(("dp", "blk")),
                P(("dp", "blk")),
            ),
            check_vma=False,
        )

    def layer(*arrays):
        rows, length, features = arrays[0].shape
        shape = dict(mesh.shape)
        fits = (
            shape == {"dp": DP_SIZE, "blk": BLK_SIZE}
            and (rows, length, features) == (2 * shape["dp"], 512, 768)
            and arrays[9].shape[1] == 3072
        )
        return spread(fast_device if fits else per_device)(*arrays)

    return layer
```

```python
import jax
import jax.numpy as jnp
from jax import lax
from jax.experimental import pallas as pl
from jax.experimental.pallas import tpu as pltpu
from jax.sharding import PartitionSpec as P

HEADS = 12
SENDS, RECEIVES, LOCALS = 74, 92, 6
VMEM_MIB = 58


epsilon = 1e-05
masked_score = -1e30


def normalize(values_in, gain, shift):
    centered = values_in - jnp.mean(values_in, axis=-1, keepdims=True)
    inverse = lax.rsqrt(jnp.mean(centered * centered, axis=-1, keepdims=True) + epsilon)
    unit_rows = centered * inverse
    return (unit_rows * gain + shift, unit_rows, inverse)


def normalize_back(grad_normed, unit_rows, inverse, gain):
    scaled = grad_normed * gain
    grad_input = inverse * (
        scaled
        - jnp.mean(scaled, axis=-1, keepdims=True)
        - unit_rows * jnp.mean(scaled * unit_rows, axis=-1, keepdims=True)
    )
    return (
        grad_input,
        jnp.sum(grad_normed * unit_rows, axis=(0, 1)),
        jnp.sum(grad_normed, axis=(0, 1)),
    )


def project(activation, weight):
    return jnp.einsum("rcd,dn->rcn", activation, weight, preferred_element_type=jnp.float32)


def project_back(gradient, weight):
    return jnp.einsum("rcn,dn->rcd", gradient, weight, preferred_element_type=jnp.float32)


def outer_sum(activation, gradient):
    return jnp.einsum("rcd,rcn->dn", activation, gradient, preferred_element_type=jnp.float32)


def split_heads(matrix, head_count):
    return matrix.reshape(
        matrix.shape[0], matrix.shape[1], head_count, matrix.shape[2] // head_count
    )


def masked_scores(query_heads, key_heads, query_segment, key_segment, scaling):
    raw_scores = (
        jnp.einsum("rqhd,rkhd->rhqk", query_heads, key_heads, preferred_element_type=jnp.float32)
        * scaling
    )
    allowed = (query_segment[:, :, None] == key_segment[:, None, :])[:, None]
    return (jnp.where(allowed, raw_scores, masked_score), allowed)


def column_sums(gradient):
    return jnp.sum(gradient.astype(jnp.float32), axis=(0, 1))


def scatter_sum(gradient):
    summed = lax.psum_scatter(
        gradient.astype(jnp.bfloat16), ("dp", "blk"), scatter_dimension=0, tiled=True
    )
    return summed.astype(jnp.float32)


def per_device(
    tokens,
    segment_ids,
    pad_mask,
    joint_weight,
    joint_bias,
    output_weight,
    output_bias,
    first_gain,
    first_shift,
    up_weight,
    up_bias,
    down_weight,
    down_bias,
    second_gain,
    second_shift,
    cotangent,
):
    batch_rows, local_len, features = tokens.shape
    head_count = HEADS
    head_size = features // head_count
    scaling = head_size ** (-0.5)
    device_count = lax.axis_size("dp") * lax.axis_size("blk")
    small_parts = (
        joint_bias, output_bias, first_gain, first_shift, up_bias, down_bias, second_gain, second_shift
    )
    small_all = lax.all_gather(jnp.concatenate(small_parts), ("dp", "blk"), axis=0, tiled=True)
    small_all = small_all.reshape(device_count, -1)
    small_full = []
    small_at = 0
    for part in small_parts:
        small_full.append(small_all[:, small_at : small_at + part.shape[0]].reshape(-1))
        small_at += part.shape[0]
    full_joint_bias, full_output_bias, gain_one, shift_one = small_full[:4]
    full_up_bias, full_down_bias, gain_two, shift_two = small_full[4:]
    full_joint = lax.all_gather(joint_weight, ("dp", "blk"), axis=0, tiled=True)
    full_output = lax.all_gather(output_weight, ("dp", "blk"), axis=0, tiled=True)
    normed_one, unit_one, inverse_one = normalize(
        tokens, gain_one.astype(jnp.float32), shift_one.astype(jnp.float32)
    )
    normed_one_low = normed_one.astype(jnp.bfloat16)
    joint = project(normed_one_low, full_joint)
    bias_values = full_joint_bias.astype(jnp.float32)
    query = (joint[..., :features] + bias_values[:features]).astype(jnp.bfloat16)
    keys = joint[..., features : 2 * features].astype(jnp.bfloat16)
    values = (joint[..., 2 * features :] + bias_values[features:]).astype(jnp.bfloat16)
    key_segment = jnp.where(pad_mask == 1, segment_ids, -1)
    query_heads = split_heads(query, head_count)
    top_score = jnp.full((batch_rows, head_count, local_len), masked_score, jnp.float32)
    key_portion = lax.all_gather(keys, "blk", axis=1, tiled=True)
    value_portion = lax.all_gather(values, "blk", axis=1, tiled=True)
    segment_portion = lax.all_gather(key_segment, "blk", axis=1, tiled=True)
    scores, allowed = masked_scores(
        query_heads, split_heads(key_portion, head_count), segment_ids, segment_portion, scaling
    )
    new_top = jnp.maximum(top_score, jnp.max(scores, axis=-1))
    weights = jnp.where(allowed, jnp.exp(scores - new_top[..., None]), 0.0)
    total_weight = jnp.sum(weights, axis=-1)
    weighted = jnp.einsum(
        "rhqk,rkhd->rhqd",
        weights.astype(jnp.bfloat16),
        split_heads(value_portion, head_count),
        preferred_element_type=jnp.float32,
    )
    top_score, total_weight, weighted = (new_top, total_weight, weighted)
    log_total = top_score + jnp.log(total_weight)
    attended_heads = weighted / total_weight[..., None]
    attended = jnp.transpose(attended_heads, (0, 2, 1, 3)).reshape(batch_rows, local_len, features)
    attended_low = attended.astype(jnp.bfloat16)
    middle = tokens + project(attended_low, full_output) + full_output_bias.astype(jnp.float32)
    full_up = lax.all_gather(up_weight, ("dp", "blk"), axis=0, tiled=True)
    full_down = lax.all_gather(down_weight, ("dp", "blk"), axis=0, tiled=True)
    normed_two, unit_two, inverse_two = normalize(
        middle, gain_two.astype(jnp.float32), shift_two.astype(jnp.float32)
    )
    normed_two_low = normed_two.astype(jnp.bfloat16)
    hidden = project(normed_two_low, full_up) + full_up_bias.astype(jnp.float32)
    activated, gelu_pullback = jax.vjp(jax.nn.gelu, hidden)
    activated_low = activated.astype(jnp.bfloat16)
    result = middle + project(activated_low, full_down) + full_down_bias.astype(jnp.float32)
    later_up, later_down, later_gain_two = full_up, full_down, gain_two
    grad_result = cotangent.astype(jnp.bfloat16)
    grad_down_weight = outer_sum(activated_low, grad_result)
    grad_down_bias = column_sums(grad_result)
    grad_activated = project_back(grad_result, later_down)
    grad_hidden = gelu_pullback(grad_activated)[0].astype(jnp.bfloat16)
    grad_up_bias = column_sums(grad_hidden)
    grad_up_weight = outer_sum(normed_two_low, grad_hidden)
    grad_normed_two = project_back(grad_hidden, later_up)
    grad_from_second, grad_gain_two, grad_shift_two = normalize_back(
        grad_normed_two, unit_two, inverse_two, later_gain_two.astype(jnp.float32)
    )
    grad_middle = cotangent + grad_from_second
    grad_up_shard = scatter_sum(grad_up_weight)
    grad_down_shard = scatter_sum(grad_down_weight)
    later_joint, later_output, later_gain_one = full_joint, full_output, gain_one
    grad_branch = grad_middle.astype(jnp.bfloat16)
    grad_output_weight = outer_sum(attended_low, grad_branch)
    grad_output_bias = column_sums(grad_branch)
    grad_attended = project_back(grad_branch, later_output).astype(jnp.bfloat16)
    grad_heads = split_heads(grad_attended, head_count)
    delta = jnp.einsum("rqhd,rhqd->rhq", grad_heads.astype(jnp.float32), attended_heads)
    key_heads = split_heads(key_portion, head_count)
    scores, allowed = masked_scores(query_heads, key_heads, segment_ids, segment_portion, scaling)
    probs = jnp.where(allowed, jnp.exp(scores - log_total[..., None]), 0.0)
    grad_probs = jnp.einsum(
        "rqhd,rkhd->rhqk",
        grad_heads,
        split_heads(value_portion, head_count),
        preferred_element_type=jnp.float32,
    )
    grad_scores = (probs * (grad_probs - delta[..., None])).astype(jnp.bfloat16)
    grad_query = scaling * jnp.einsum(
        "rhqk,rkhd->rqhd", grad_scores, key_heads, preferred_element_type=jnp.float32
    )
    every_total, every_delta = (
        lax.all_gather(log_total, "blk", axis=2, tiled=True),
        lax.all_gather(delta, "blk", axis=2, tiled=True),
    )
    own_keys = split_heads(keys, head_count)
    own_values = split_heads(values, head_count)
    query_portion = lax.all_gather(query, "blk", axis=1, tiled=True)
    grad_portion = lax.all_gather(grad_attended, "blk", axis=1, tiled=True)
    segment_portion = lax.all_gather(segment_ids, "blk", axis=1, tiled=True)
    portion_queries = split_heads(query_portion, head_count)
    portion_grads = split_heads(grad_portion, head_count)
    scores, allowed = masked_scores(
        portion_queries, own_keys, segment_portion, key_segment, scaling
    )
    probs = jnp.where(allowed, jnp.exp(scores - every_total[..., None]), 0.0)
    grad_values = jnp.einsum(
        "rhqk,rqhd->rkhd",
        probs.astype(jnp.bfloat16),
        portion_grads,
        preferred_element_type=jnp.float32,
    )
    grad_probs = jnp.einsum(
        "rqhd,rkhd->rhqk", portion_grads, own_values, preferred_element_type=jnp.float32
    )
    grad_scores = (probs * (grad_probs - every_delta[..., None])).astype(jnp.bfloat16)
    grad_keys = scaling * jnp.einsum(
        "rhqk,rqhd->rkhd", grad_scores, portion_queries, preferred_element_type=jnp.float32
    )
    grad_keys, grad_values = (grad_keys, grad_values)
    grad_joint = jnp.concatenate(
        [
            grad_query.reshape(batch_rows, local_len, features),
            grad_keys.reshape(batch_rows, local_len, features),
            grad_values.reshape(batch_rows, local_len, features),
        ],
        axis=-1,
    ).astype(jnp.bfloat16)
    grad_joint_weight = outer_sum(normed_one_low, grad_joint)
    grad_joint_bias = jnp.concatenate(
        [column_sums(grad_joint[..., :features]), column_sums(grad_joint[..., 2 * features :])]
    )
    grad_normed_one = project_back(grad_joint, later_joint)
    grad_from_first, grad_gain_one, grad_shift_one = normalize_back(
        grad_normed_one, unit_one, inverse_one, later_gain_one.astype(jnp.float32)
    )
    grad_tokens = grad_middle + grad_from_first
    small_grads = (
        grad_joint_bias, grad_output_bias, grad_gain_one, grad_shift_one,
        grad_up_bias, grad_down_bias, grad_gain_two, grad_shift_two,
    )
    packed = jnp.concatenate([part.reshape(device_count, -1) for part in small_grads], axis=1)
    own = lax.psum_scatter(packed, ("dp", "blk"), scatter_dimension=0, tiled=True)[0]
    small_shards = []
    small_at = 0
    for part in small_parts:
        small_shards.append(own[small_at : small_at + part.shape[0]])
        small_at += part.shape[0]
    return (
        result,
        grad_tokens,
        scatter_sum(grad_joint_weight),
        small_shards[0],
        scatter_sum(grad_output_weight),
        small_shards[1],
        small_shards[2],
        small_shards[3],
        grad_up_shard,
        small_shards[4],
        grad_down_shard,
        small_shards[5],
        small_shards[6],
        small_shards[7],
    )


Z_SIZE, Y_SIZE, BLK_SIZE = 4, 2, 4
DP_SIZE = Z_SIZE * Y_SIZE
MESH = pl.DeviceIdType.MESH
BF = jnp.bfloat16
F32 = jnp.float32
WIDE, CHUNKS = 256, 3
TILE_WIDTHS = (24, 24, 24, 24, 24, 24, 48, 96)


def dot_nn(left, right):
    return lax.dot_general(left, right, (((1,), (0,)), ((), ())), preferred_element_type=F32)


def dot_nt(left, right):
    return lax.dot_general(left, right, (((1,), (1,)), ((), ())), preferred_element_type=F32)


def dot_tn(left, right):
    return lax.dot_general(left, right, (((0,), (0,)), ((), ())), preferred_element_type=F32)


def lane_pieces(lanes, width):
    lane = lax.broadcasted_iota(jnp.int32, (1, lanes), 1).astype(F32)
    piece = jnp.floor((lane + 0.5) * (1.0 / width))
    return piece, lane - width * piece


def piece_placer(lanes, width):
    place = lax.broadcasted_iota(jnp.int32, (128, lanes), 0).astype(F32)
    _, within = lane_pieces(lanes, width)
    return jnp.where(place == within, 1.0, 0.0).astype(BF)


def layer_kernel(*refs):
    ins, outs, scr = refs[:16], refs[16:23], refs[23:]
    (tok_in, cot_in, seg_in, pad_in, jw_in, uw_in, dw_in, ow_in), vectors = ins[:8], ins[8:]
    MID, GM, OJ, OO, OU, OD, OS = outs
    (
        TOK, COT, JW, UW, DW, JP0, JP1, UPW, UP, AP, TILE, SEGT, G, SEG, KSEG, QSEG, PV, QVB,
        N1, N2, GR, WJS0, WJS1, WUS, WDS, WOS, WJ0, WJ1, WU, WO,
        U1, I1, U2, I2, GB,
        Q, K, V, PB, OF, AT, AR, DA, DR, DOH, GJ0, GJ1,
        GP, ACT, GH, UBS, PT, RC, SX, RX,
        GD, GU, GA, GC, GO, GO2, RYd, RYu, RYa, RYc, RYo, Sd, Su, Sa, Sc, So,
        RZd, RZu, RZa, RZc, RZo, RZ0, S0, RY0, AUs, AUr, AAs, AAr, ACs, ACr, RCo, SXo, RXo,
        TS, TB, TL, TY, TV, VS, JBS, ssem, rsem, lsem,
    ) = scr
    dp = lax.axis_index("dp")
    blk = lax.axis_index("blk")
    z, y = dp // 2, dp % 2
    x, c = blk // 2, blk % 2
    count = [0, 0, 0]
    started = []

    def local(src, dst):
        n = count[1]
        count[1] += 1
        made = pltpu.make_async_copy(src, dst, lsem.at[n])
        made.start()
        return made

    def to_send():
        n = count[0]
        count[0] += 1
        return ssem.at[n]

    def to_receive():
        n = count[2]
        count[2] += 1
        return rsem.at[n]

    def group():
        return to_send(), to_receive()

    def send(src, dst, dev, sems):
        made = pltpu.make_async_remote_copy(
            src_ref=src, dst_ref=dst, send_sem=sems[0], recv_sem=sems[1],
            device_id=dev, device_id_type=MESH,
        )
        made.start()
        return made

    def wait_bytes(sem, ref):
        pltpu.make_async_copy(ref, ref, sem).wait()

    def received(copies):
        wait_bytes(copies[0][1], copies[1])

    def later_sent(copies):
        started.append(copies)

    def sent(copies):
        wait_bytes(copies[0][0], copies[1])

    started_over_z = []

    def later_sent_over_z(copies):
        started_over_z.append(copies)

    core_peer = (dp, 2 * x + 1 - c)
    x_peer = (dp, 2 * (1 - x) + c)
    far_peer = (dp, 2 * (1 - x) + 1 - c)
    blk_peers = (x_peer, far_peer, core_peer)
    y_peer = (2 * z + 1 - y, blk)
    inner = (z == 1) | (z == 2)
    z_left = (2 * ((z + Z_SIZE - 1) % Z_SIZE) + y, blk)
    z_right = (2 * ((z + 1) % Z_SIZE) + y, blk)
    z_side = (2 * ((z // 2) * 2 + 1 - z % 2) + y, blk)
    z_across = (2 * (Z_SIZE - 1 - z) + y, blk)

    def z_at(k):
        return (z + k) % Z_SIZE

    ow_copy = local(ow_in, WOS.at[blk, dp])
    jw_copy = local(jw_in, JW)
    tok_copy = local(tok_in, TOK)
    uw_copy = local(uw_in, UW)
    dw_copy = local(dw_in, DW)
    cot_copy = local(cot_in, COT)

    every = [
        ((dp + i) % DP_SIZE, (blk + j) % BLK_SIZE)
        for i in range(DP_SIZE) for j in range(BLK_SIZE) if i or j
    ]

    def entry_barrier():
        barrier = pltpu.get_barrier_semaphore()
        for dev in every:
            pl.semaphore_signal(barrier, inc=1, device_id=dev, device_id_type=MESH)
        pl.semaphore_wait(barrier, len(every))

    def swap_parts(parts, landing, chunked=False):
        sems = group()
        for dev in blk_peers:
            send(parts(dev[1]), landing.at[:, blk] if chunked else landing.at[blk], dev, sems)
        span = landing.at[:, pl.ds(c, 3)] if chunked else landing.at[pl.ds(c, 3)]
        later_sent((sems, span))
        return sems, span

    def small_tiles():
        TILE[...] = jnp.zeros_like(TILE)
        for row, (ref, width) in enumerate(zip(vectors, TILE_WIDTHS)):
            TILE[row : row + 1, 0:width] = ref[...].astype(F32).reshape(1, width)
        segment = seg_in[...].astype(F32)
        SEGT[...] = jnp.zeros_like(SEGT)
        SEGT[0:2] = segment
        SEGT[2:4] = jnp.where(pad_in[...] == 1, segment, -1.0)
        G[dp, blk] = TILE[...]
        SEG[blk] = SEGT[...]


    small_tiles()
    entry_barrier()

    def stats(values):
        mean = jnp.mean(values, axis=-1, keepdims=True)
        centered = values - mean
        inverse = lax.rsqrt(jnp.mean(centered * centered, axis=-1, keepdims=True) + epsilon)
        return centered * inverse, inverse

    def dp_part(slab, span):
        return slab, span, [group(), group()] + [(None, to_receive()) for _ in range(3)]

    def slabs_part(slabs):
        return dp_part(lambda i: slabs.at[i], lambda n: slabs.at[pl.ds(c, n)])

    def own_over_y(part):
        slab, span, sems = part
        send(slab(dp), slab(dp), y_peer, sems[0])
        later_sent((sems[0], span(4)))

    def own_over_z(part):
        slab, span, sems = part

        @pl.when(z < Z_SIZE - 1)
        def _():
            send(slab(dp), slab(dp), z_right, (sems[1][0], sems[1][1]))

        @pl.when(z > 0)
        def _():
            send(slab(dp), slab(dp), z_left, (sems[1][0], sems[2][1]))

        later_sent_over_z((sems[1], span(1), span(5)))

    def pass_on(part, there, arrived, onward, more, dev):
        slab, _, sems = part
        received((arrived, slab(there)))
        send(slab(there), slab(there), y_peer, sems[0])
        if onward is not None:

            @pl.when(more)
            def _():
                send(slab(there), slab(there), dev, (sems[1][0], onward[1]))

    def step_one(part):
        sems = part[2]

        @pl.when(z > 0)
        def _():
            pass_on(part, dp - 2, sems[1], sems[3], z < Z_SIZE - 1, z_right)

        @pl.when(z < Z_SIZE - 1)
        def _():
            pass_on(part, dp + 2, sems[2], sems[3], z > 0, z_left)

    def step_two(part):
        sems = part[2]

        @pl.when(z >= 2)
        def _():
            pass_on(part, dp - 4, sems[3], sems[4], z == 2, z_right)

        @pl.when(z < 2)
        def _():
            pass_on(part, dp + 4, sems[3], sems[4], z == 1, z_left)

    def step_three(part):
        sems = part[2]

        @pl.when(z == Z_SIZE - 1)
        def _():
            pass_on(part, dp - 6, sems[4], None, None, None)

        @pl.when(z == 0)
        def _():
            pass_on(part, dp + 6, sems[4], None, None, None)

    def dp_end(part):
        _, span, sems = part
        received((sems[0], span(4)))

    def gather_start(buf, r):
        over_x, to_core = group(), group()
        send(buf.at[r, blk], buf.at[r, blk], x_peer, over_x)
        send(buf.at[r, blk], buf.at[r, blk], core_peer, to_core)
        later_sent((over_x, buf.at[r, blk]))
        later_sent((to_core, buf.at[r, pl.ds(c, 2)]))
        return buf, r, over_x, to_core

    def gather_forward(part):
        buf, r, over_x, to_core = part
        received((over_x, buf.at[r, x_peer[1]]))
        send(buf.at[r, x_peer[1]], buf.at[r, x_peer[1]], core_peer, to_core)

    def gather_end(part):
        buf, r, _, to_core = part
        received((to_core, buf.at[r, pl.ds(c, 2)]))

    ow_copy.wait()
    o_part = dp_part(lambda i: WOS.at[blk, i], lambda n: WOS.at[blk, pl.ds(c, n)])
    a_part, c_part, g_part = slabs_part(WJS0), slabs_part(WJS1), slabs_part(G)

    def chunks_part(slabs):
        return dp_part(lambda i: slabs.at[:, i], lambda n: slabs.at[:, pl.ds(c, n)])

    u_part, d_part = chunks_part(WUS), chunks_part(WDS)
    own_over_z(o_part)
    own_over_y(o_part)

    def split_joint():
        jw_copy.wait()
        for b in range(BLK_SIZE):
            for s in range(3):
                at = 768 * s + 192 * b
                JP0[b, :, 64 * s : 64 * (s + 1)] = JW[:, at : at + 64]
                JP1[b, :, 128 * s : 128 * (s + 1)] = JW[:, at + 64 : at + 192]

    def swap_columns(parts, slabs):
        slabs[dp, blk] = parts[blk]
        return swap_parts(lambda b: parts.at[b], slabs.at[dp])

    split_joint()
    AP[blk] = JP0[blk]
    a_first = swap_parts(lambda b: JP0.at[b], AP)
    g_first = swap_parts(lambda b: TILE, G.at[dp])
    c_first = swap_columns(JP1, WJS1)
    seg_copies = swap_parts(lambda b: SEGT, SEG)

    def first_stats():
        tok_copy.wait()
        firsts = []
        for r in range(2):
            unit, inverse = stats(TOK[r])
            U1[r] = unit
            I1[r] = inverse
            N1[r, blk] = unit.astype(BF)
            firsts.append(gather_start(N1, r))
        return firsts

    n1_part = first_stats()
    n1_sent = (started[-4:-2], started[-2:])
    del started[-4:]

    def split_up():
        uw_copy.wait()
        for i in range(DP_SIZE):
            for b in range(BLK_SIZE):
                at = 96 * (BLK_SIZE * i + b)
                UPW[b, :, 96 * i : 96 * (i + 1)] = UW[:, at : at + 96]
        for n in range(CHUNKS):
            for b in range(BLK_SIZE):
                UP[n, b] = UPW[b, :, WIDE * n : WIDE * (n + 1)]

    def split_down():
        dw_copy.wait()
        for n in range(CHUNKS):
            WDS[n, dp] = DW[:, WIDE * n : WIDE * (n + 1)]

    def early_down():
        split_down()
        own_over_y(d_part)

    def low_cotangent():
        cot_copy.wait()
        for r in range(2):
            GR[r, blk] = COT[r].astype(BF)

    early_down()
    received(a_first)
    for p in range(2):
        WJS0[dp, p, :, 0:192] = AP[2 * p]
        WJS0[dp, p, :, 192:384] = AP[2 * p + 1]
    own_over_z(a_part)
    own_over_y(a_part)
    received(g_first)
    own_over_z(g_part)
    own_over_y(g_part)
    received(c_first)
    own_over_z(c_part)
    own_over_y(c_part)
    split_up()
    WUS[:, dp, blk] = UP[:, blk]
    u_first = swap_parts(lambda b: UP.at[:, b], WUS.at[:, dp], True)
    low_cotangent()
    gr_part = [gather_start(GR, r) for r in range(2)]
    step_one(a_part)
    step_one(g_part)
    step_one(o_part)
    step_two(a_part)
    step_two(g_part)
    step_two(o_part)
    gather_forward(n1_part[0])
    step_one(c_part)
    step_three(a_part)
    step_three(g_part)
    step_three(o_part)
    step_two(c_part)
    received(u_first)
    own_over_z(u_part)
    own_over_z(d_part)
    gather_forward(n1_part[1])
    dev_id = lax.broadcasted_iota(jnp.int32, (32, 1, 1), 0).astype(F32)
    blk_f = blk.astype(F32)
    piece24, _ = lane_pieces(768, 24)
    piece48, _ = lane_pieces(192, 48)
    piece96, _ = lane_pieces(768, 96)

    def mask24():
        return piece24[None] == dev_id

    def mask48(first_dev):
        return piece48[None] + (4.0 * blk_f + first_dev) == dev_id

    def mask96():
        return 4.0 * piece96[None] + blk_f == dev_id

    def place24():
        return piece_placer(768, 24)

    def place48():
        return piece_placer(192, 48)

    def place96():
        return piece_placer(768, 96)

    def small_end():
        dp_end(g_part)
        tiles = G[...].reshape(32 * 8, 128).astype(BF)

        def placed(placer, mask, lanes):
            spread = dot_nn(tiles, placer).reshape(32, 8, lanes)
            return jnp.sum(jnp.where(mask, spread, 0.0), axis=0)

        PV[0:8] = placed(place24(), mask24(), 768)
        PV[8:16] = placed(place96(), mask96(), 768)
        QVB[0:8] = placed(place48(), mask48(0.0), 192)
        QVB[8:16] = placed(place48(), mask48(16.0), 192)

    def segments_end():
        received(seg_copies)
        eye = jnp.where(
            lax.broadcasted_iota(jnp.int32, (128, 128), 0)
            == lax.broadcasted_iota(jnp.int32, (128, 128), 1), 1.0, 0.0,
        ).astype(BF)
        for b in range(BLK_SIZE):
            part = SEG[b]
            KSEG[:, 128 * b : 128 * (b + 1)] = part
            QSEG[128 * b : 128 * (b + 1)] = dot_nt(eye, part.astype(BF))


    segments_end()
    small_end()
    gain1, shift1, obias = PV[0:1], PV[1:2], PV[2:3]
    gain2, shift2, dbias = PV[3:4], PV[4:5], PV[5:6]

    def compact(slabs, whole):
        for i in range(DP_SIZE):
            rows = slabs(i).astype(F32)
            rows = rows.reshape(96, rows.shape[-1])
            whole[96 * i : 96 * (i + 1), :] = rows.astype(BF)

    def norm_rows(r):
        gather_end(n1_part[r])
        for copies in n1_sent[r]:
            sent(copies)
        for b in range(BLK_SIZE):
            N1[r, b] = (N1[r, b].astype(F32) * gain1 + shift1).astype(BF)

    def qkv_one(r):
        joint = dot_nn(N1[r].reshape(512, 768), WJ0[...])
        qbias, vbias = QVB[6:7, 0:64], QVB[14:15, 0:64]
        Q[r, 0] = ((joint[:, :64] + qbias).astype(BF).astype(F32) * 0.125).astype(BF)
        K[r, 0] = joint[:, 64:128].astype(BF)
        V[r, 0] = (joint[:, 128:] + vbias).astype(BF)

    def qkv_two(r):
        joint = dot_nn(N1[r].reshape(512, 768), WJ1[...])
        qbias, vbias = QVB[6:7, 64:192], QVB[14:15, 64:192]
        query = ((joint[:, :128] + qbias).astype(BF).astype(F32) * 0.125).astype(BF)
        keys = joint[:, 128:256].astype(BF)
        values = (joint[:, 256:] + vbias).astype(BF)
        for h in (1, 2):
            lanes = slice(64 * (h - 1), 64 * h)
            Q[r, h] = query[:, lanes]
            K[r, h] = keys[:, lanes]
            V[r, h] = values[:, lanes]

    def attend(r, h):
        scores = dot_nt(Q[r, h], K[r, h])
        scores = jnp.where(QSEG[:, r : r + 1] == KSEG[2 + r : 3 + r, :], scores, masked_score)
        top = jnp.max(scores, axis=-1, keepdims=True)
        expos = jnp.exp(scores - top)
        total = jnp.sum(expos, axis=-1, keepdims=True)
        probs = (expos * (1.0 / total)).astype(BF)
        PB[r, h] = probs
        out = dot_nn(probs, V[r, h])
        OF[r, h] = out
        if h:
            AT[r, :, 0:128, 64 * (h - 1) : 64 * h] = out.astype(BF).reshape(4, 128, 64)
        else:
            halves = out.astype(BF).reshape(4, 2, 64, 64)
            AT[r, :, 128:192, 0:64] = halves[:, 0]
            AT[r, :, 128:192, 64:128] = halves[:, 1]

    def swap_heads(src, dst, r):
        dst[r, blk] = src[r, blk]
        return swap_parts(lambda b: src.at[r, b], dst.at[r])

    dp_end(a_part)
    for i in range(DP_SIZE):
        pairs = WJS0[i].astype(F32)
        rows = [pairs[p][:, 192 * s : 192 * (s + 1)] for p in range(2) for s in range(2)]
        WJ0[96 * i : 96 * (i + 1), :] = jnp.concatenate(rows, axis=0).astype(BF)
    norm_rows(0)
    qkv_one(0)
    step_three(c_part)
    attend(0, 0)
    own_over_y(u_part)
    dp_end(o_part)
    wo_x, wo_core = group(), group()
    send(WOS.at[blk], WOS.at[blk], x_peer, wo_x)
    send(WOS.at[blk], WOS.at[blk], core_peer, wo_core)
    later_sent((wo_x, WOS.at[blk]))
    later_sent((wo_core, WOS.at[pl.ds(c, 2)]))
    norm_rows(1)
    qkv_one(1)
    attend(1, 0)
    step_one(u_part)
    dp_end(c_part)
    compact(lambda i: WJS1[i], WJ1)
    qkv_two(0)
    attend(0, 1)
    attend(0, 2)
    at_copies = [swap_heads(AT, AR, 0)]
    gather_forward(gr_part[0])
    qkv_two(1)
    step_two(u_part)
    attend(1, 1)
    step_one(d_part)
    attend(1, 2)
    at_copies.append(swap_heads(AT, AR, 1))
    received((wo_x, WOS.at[x_peer[1]]))
    send(WOS.at[x_peer[1]], WOS.at[x_peer[1]], core_peer, wo_core)
    received((wo_core, WOS.at[pl.ds(c, 2)]))
    compact(lambda i: WOS[:, i], WO)

    def head_zero(block):
        packed = block[128:192]
        return jnp.concatenate([packed[:, 0:64], packed[:, 64:128]], axis=0)

    def middle_rows(r):
        received(at_copies[r])
        total = TOK[r] + obias
        for b in range(BLK_SIZE):
            block = AR[r, b]
            total = total + dot_nn(head_zero(block), WO[192 * b : 192 * b + 64, :])
            total = total + dot_nn(block[0:128], WO[192 * b + 64 : 192 * (b + 1), :])
        MID[r] = total
        unit, inverse = stats(total)
        U2[r] = unit
        I2[r] = inverse
        N2[r, blk] = (unit * gain2 + shift2).astype(BF)
        return gather_start(N2, r)

    n2_part = [middle_rows(0)]
    step_three(u_part)
    n2_part.append(middle_rows(1))
    step_two(d_part)
    gather_forward(gr_part[1])
    dp_end(u_part)
    for n in range(CHUNKS):
        compact(lambda i: WUS[n, i], WU.at[n])
    gather_forward(n2_part[0])
    step_three(d_part)
    gather_end(n2_part[0])

    def rows_of(buf, r):
        return buf[r].reshape(512, 768)

    def up(r):
        for n in range(CHUNKS):
            cols = slice(WIDE * n, WIDE * (n + 1))
            hidden = dot_nn(rows_of(N2, r), WU[n]) + PV[15:16, cols]
            square = hidden * hidden
            bent = jnp.tanh(hidden * (0.7978845608028654 + 0.035677408136300125 * square))
            half = 0.5 * (1.0 + bent)
            ACT[r, :, cols] = (hidden * half).astype(BF)
            slope = 0.3989422804014327 + 0.05351611220445019 * square
            GP[r, :, cols] = (half + hidden * (1.0 - bent * bent) * slope).astype(BF)

    def hidden_back(r):
        for n in range(2):
            cols = slice(384 * n, 384 * (n + 1))
            rows = rows_of(GR, r)
            grad = 0.0
            for m in range(CHUNKS):
                weight = WDS[m, 4 * n : 4 * (n + 1)].reshape(384, WIDE)
                grad = grad + dot_nt(rows[:, WIDE * m : WIDE * (m + 1)], weight)
            grad = (grad * GP[r, :, cols].astype(F32)).astype(BF)
            GH[r, :, cols] = grad
            UBS[r, :, cols] = jnp.sum(grad.astype(F32), axis=0, keepdims=True)

    def sum_store(i, r, cols, values):
        PT[i, r, :, :, :, cols] = values.reshape(2, 2, 128, values.shape[-1]).astype(BF)

    def sum_start(i, r):
        sems = group()
        send(PT.at[i, r, :, 1 - c], RC.at[i, r], core_peer, sems)
        later_sent((sems, RC.at[i, r]))
        return sems, RC.at[i, r]

    def sum_middle(i, r, first):
        received(first)
        SX[i, r] = (PT[i, r, 1 - x, c].astype(F32) + RC[i, r, 1 - x].astype(F32)).astype(BF)
        sems = group()
        send(SX.at[i, r], RX.at[i, r], x_peer, sems)
        later_sent((sems, RX.at[i, r]))
        return sems, RX.at[i, r]

    def sum_end(i, r, second):
        received(second)
        return PT[i, r, x, c].astype(F32) + RC[i, r, x].astype(F32) + RX[i, r].astype(F32)

    def second_back(r):
        for n in range(3):
            cols = slice(256 * n, 256 * (n + 1))
            grad = 0.0
            for m in range(CHUNKS):
                grad = grad + dot_nt(GH[r, :, WIDE * m : WIDE * (m + 1)], WU[m, cols, :])
            sum_store(0, r, cols, grad)
        return sum_start(0, r)

    def first_back(r):
        for n in range(3):
            cols = slice(256 * n, 256 * (n + 1))
            sum_store(
                2, r, cols, dot_nt(GJ0[r], WJ0[cols, :]) + dot_nt(GJ1[r], WJ1[cols, :])
            )
        return sum_start(2, r)

    def down(r):
        for n in range(CHUNKS):
            cols = slice(WIDE * n, WIDE * (n + 1))
            sum_store(1, r, cols, dot_nn(ACT[r], WDS[n].reshape(768, WIDE)))
        return sum_start(1, r)

    def scatter_start(parts, recv):
        sems = group()
        send(parts.at[:, 1 - y], recv, y_peer, sems)
        later_sent((sems, recv))
        return sems, recv

    def scatter_middle(parts, recv, sums, landing, first):
        received(first)
        sums[...] = (parts[:, y].astype(F32) + recv[...].astype(F32)).astype(BF)
        sems = group()
        for k in range(1, Z_SIZE):
            send(sums.at[z_at(k)], landing.at[k - 1], (2 * z_at(k) + y, blk), sems)
        later_sent((sems, landing))
        return sums, landing, (sems, landing)

    def scatter_end(sums, landing, second):
        received(second)
        total = sums[z].astype(F32)
        for k in range(Z_SIZE - 1):
            total = total + landing[k].astype(F32)
        return total

    def return_columns(part, sends, recvs):
        sends[...] = scatter_end(*part).astype(BF)
        recvs[blk] = sends[blk]
        return swap_parts(lambda b: sends.at[b], recvs)

    def down_grad(n):
        grads = GR[:, :, :, WIDE * n : WIDE * (n + 1)].reshape(1024, WIDE)
        for m in range(2):
            cols = slice(384 * m, 384 * (m + 1))
            grad = dot_tn(ACT[:, :, cols].reshape(1024, 384), grads)
            GD[n, 2 * m : 2 * m + 2] = grad.reshape(2, 2, 96, WIDE).astype(BF)

    def row_grad(rows, grads, parts):
        for m in range(2):
            cols = slice(384 * m, 384 * (m + 1))
            grad = dot_tn(rows[:, :, :, cols].reshape(1024, 384), grads)
            parts[2 * m : 2 * m + 2] = grad.reshape(2, 2, 4, 24, grad.shape[-1]).astype(BF)

    def up_grad(n):
        row_grad(N2, GH[:, :, WIDE * n : WIDE * (n + 1)].reshape(1024, WIDE), GU.at[n])

    def joint_grad_one():
        for m in range(2):
            rows = N1[:, :, :, 384 * m : 384 * (m + 1)].reshape(1024, 384)
            grad = dot_tn(rows, GJ0[...].reshape(1024, 192)).reshape(2, 2, 4, 24, 192).astype(BF)
            for p in range(2):
                GA[2 * m : 2 * m + 2, :, p, :, 0:192] = grad[:, :, 2 * p]
                GA[2 * m : 2 * m + 2, :, p, :, 192:384] = grad[:, :, 2 * p + 1]
        return scatter_start(GA, RYa)

    def joint_grad_two():
        row_grad(N1, GJ1[...].reshape(1024, 384), GC)
        return scatter_start(GC, RYc)

    def output_grad():
        for b in range(BLK_SIZE):
            blocks = [AR[r, b] for r in range(2)]
            zero = jnp.concatenate([head_zero(block) for block in blocks], axis=0)
            rest = jnp.concatenate([block[0:128] for block in blocks], axis=0)
            grads = GB[...].reshape(256, 768)
            grad = jnp.concatenate([dot_tn(zero, grads), dot_tn(rest, grads)], axis=0)
            grad = grad.reshape(2, 4, 24, 768).astype(BF)
            for i in range(4):
                GO[i // 2, i % 2, 2 * b : 2 * b + 2] = grad[:, i]
        sems = group()
        send(GO.at[:, 1 - c], RCo, core_peer, sems)
        later_sent((sems, RCo))
        return sems, RCo

    def output_grad_middle(first):
        received(first)
        SXo[...] = (GO[1 - x, c].astype(F32) + RCo[1 - x].astype(F32)).astype(BF)
        sems = group()
        send(SXo, RXo, x_peer, sems)
        later_sent((sems, RXo))
        return sems, RXo

    def norm_back(e, unit, inverse, gain):
        f = e * gain
        grad = inverse * (
            f - jnp.mean(f, axis=-1, keepdims=True)
            - unit * jnp.mean(f * unit, axis=-1, keepdims=True)
        )
        return (
            grad, jnp.sum(e * unit, axis=0, keepdims=True), jnp.sum(e, axis=0, keepdims=True)
        )

    def second_norm_back(r, second):
        e = sum_end(0, r, second)
        grad, of_gain, of_shift = norm_back(e, U2[r], I2[r], gain2)
        grad = grad + COT[r]
        GM[r] = grad
        low = grad.astype(BF)
        GB[r] = low
        for b in range(BLK_SIZE):
            zero = dot_nt(low, WO[192 * b : 192 * b + 64, :]).astype(BF)
            DA[r, b, 128:192, 0:64] = zero[0:64]
            DA[r, b, 128:192, 64:128] = zero[64:128]
            DA[r, b, 0:128] = dot_nt(low, WO[192 * b + 64 : 192 * (b + 1), :]).astype(BF)
        copies = swap_heads(DA, DR, r)
        VS[3:4] += of_gain
        VS[4:5] += of_shift
        VS[2:3] += jnp.sum(low.astype(F32), axis=0, keepdims=True)
        VS[5:6] += jnp.sum(COT[r].astype(BF).astype(F32), axis=0, keepdims=True)
        return copies

    def attend_back(r, h):
        if h:
            DOH[...] = DR[r, :, 0:128, 64 * (h - 1) : 64 * h].reshape(512, 64)
        else:
            for t in range(4):
                DOH[128 * t : 128 * t + 64] = DR[r, t, 128:192, 0:64]
                DOH[128 * t + 64 : 128 * (t + 1)] = DR[r, t, 128:192, 64:128]
        grad_out = DOH[...]
        delta = jnp.sum(grad_out.astype(F32) * OF[r, h], axis=-1, keepdims=True)
        grad_probs = dot_nt(grad_out, V[r, h])
        grad_scores = (PB[r, h].astype(F32) * (grad_probs - delta)).astype(BF)
        grads = (
            (dot_nn(grad_scores, K[r, h]) * 0.125).astype(BF),
            dot_tn(grad_scores, Q[r, h]).astype(BF),
            dot_tn(PB[r, h], grad_out).astype(BF),
        )
        for s, grad in enumerate(grads):
            if h == 0:
                GJ0[r, :, 64 * s : 64 * (s + 1)] = grad
            else:
                at = 128 * s + 64 * (h - 1)
                GJ1[r, :, at : at + 64] = grad

    def z_first_start(parts, landing):
        sems = group()
        for k in range(1, Z_SIZE):
            send(parts.at[z_at(k)], landing.at[k - 1], (2 * z_at(k) + y, blk), sems)
        later_sent((sems, landing))
        return sems, landing

    def z_first_middle(parts, landing, sums, recv, first):
        received(first)
        total = parts[z].astype(F32)
        for k in range(Z_SIZE - 1):
            total = total + landing[k].astype(F32)
        sums[...] = total.astype(BF)
        sems = group()
        send(sums.at[1 - y], recv, y_peer, sems)
        later_sent((sems, recv))
        return sems, recv

    def z_first_end(sums, recv, second):
        received(second)
        return sums[y].astype(F32) + recv[...].astype(F32)

    def output_grad_over_dp(second):
        received(second)
        GO2[...] = (
            GO[x, c].astype(F32) + RCo[x].astype(F32) + RXo[...].astype(F32)
        ).astype(BF).reshape(4, 2, 24, 768)
        return scatter_start(GO2, RYo)

    def vector_sums():
        for r in range(2):
            JBS[r, :, 0:192] = jnp.sum(GJ0[r].astype(F32), axis=0, keepdims=True)
            JBS[r, :, 192:576] = jnp.sum(GJ1[r].astype(F32), axis=0, keepdims=True)

    def first_norm_back(r, second):
        e = sum_end(2, r, second)
        grad, of_gain, of_shift = norm_back(e, U1[r], I1[r], gain1)
        GM[r] = GM[r] + grad
        VS[0:1] += of_gain
        VS[1:2] += of_shift

    VS[...] = jnp.zeros_like(VS)
    d_first, d_second, u_grad_first, u_grad_second = [], [], [], []

    def d_over_y(n):
        d_first.append(scatter_start(GD.at[n], RYd.at[n]))

    def d_over_z(n):
        d_second.append(scatter_middle(GD.at[n], RYd.at[n], Sd.at[n], RZd.at[n], d_first[n]))

    def u_over_y(n):
        u_grad_first.append(scatter_start(GU.at[n], RYu.at[n]))

    def u_over_z(n):
        u_grad_second.append(
            scatter_middle(GU.at[n], RYu.at[n], Su.at[n], RZu.at[n], u_grad_first[n])
        )

    up(0)
    gather_forward(n2_part[1])
    gather_end(gr_part[0])
    gather_end(gr_part[1])
    gather_end(n2_part[1])
    up(1)
    down_grad(0)
    d_near_first = z_first_start(GD.at[0], RZ0)
    d_first.append(None)
    d_second.append(None)
    down_grad(1)
    d_over_y(1)
    dp_end(d_part)
    hidden_back(0)
    second_first = [second_back(0)]
    down_grad(2)
    d_over_y(2)
    hidden_back(1)
    second_second = [sum_middle(0, 0, second_first[0])]
    second_first.append(second_back(1))
    up_grad(0)
    u_over_y(0)
    second_second.append(sum_middle(0, 1, second_first[1]))
    up_grad(1)
    u_over_y(1)
    d_over_z(1)
    up_grad(2)
    u_over_y(2)
    da_copies = [second_norm_back(0, second_second[0])]
    d_over_z(2)
    result_first = [down(0), down(1)]
    da_copies.append(second_norm_back(1, second_second[1]))
    o_first = output_grad()
    received(da_copies[0])
    attend_back(0, 1)
    o_second = output_grad_middle(o_first)
    attend_back(0, 2)
    d_near_second = z_first_middle(GD.at[0], RZ0, S0, RY0, d_near_first)
    u_over_z(0)
    received(da_copies[1])
    attend_back(1, 1)
    attend_back(1, 2)
    c_grad_first = joint_grad_two()
    u_over_z(1)
    attend_back(0, 0)
    first_first = [first_back(0)]
    attend_back(1, 0)
    a_grad_first = joint_grad_one()
    first_second = [sum_middle(2, 0, first_first[0])]
    u_over_z(2)
    first_first.append(first_back(1))
    o_grad_first = output_grad_over_dp(o_second)
    first_second.append(sum_middle(2, 1, first_first[1]))
    result_second = [sum_middle(1, 0, result_first[0])]
    vector_sums()

    def down_out():
        OD[:, 0:WIDE] = z_first_end(S0, RY0, d_near_second)
        for n in range(1, CHUNKS):
            OD[:, WIDE * n : WIDE * (n + 1)] = scatter_end(*d_second[n])

    row = lax.broadcasted_iota(jnp.int32, (8, 1), 0)

    def picked(values, mask, placer):
        wide = jnp.where(mask, values[None], 0.0)
        wide = wide.reshape(256, wide.shape[-1])
        high = wide.astype(BF)
        rest = (wide - high.astype(F32)).astype(BF)
        return dot_nt(high, placer) + dot_nt(rest, placer)

    def vectors_early():
        joint = JBS[0] + JBS[1]
        queries = jnp.concatenate([joint[:, 0:64], joint[:, 192:320]], axis=1)
        values = jnp.concatenate([joint[:, 128:192], joint[:, 448:576]], axis=1)
        pieces = picked(jnp.where(row == 7, UBS[0] + UBS[1], 0.0), mask96(), place96())
        pieces += picked(jnp.where(row == 6, queries, 0.0), mask48(0.0), place48())
        pieces += picked(jnp.where(row == 6, values, 0.0), mask48(16.0), place48())
        TS[...] = pieces

    def vectors_over_blk():
        pieces = (TS[...] + picked(VS[...], mask24(), place24())).reshape(8, 4, 8, 128)
        for b in range(BLK_SIZE):
            TB[b] = pieces[:, b]
        TL[blk] = TB[blk]
        return swap_parts(lambda b: TB.at[b], TL)

    def vectors_over_dp(first):
        received(first)
        TY[...] = (TL[0] + TL[1]) + (TL[2] + TL[3])
        sems = group()
        for k in range(1, DP_SIZE):
            to = (dp + k) % DP_SIZE
            send(TY.at[to], TV.at[k - 1], (to, blk), sems)
        later_sent((sems, TV))
        return sems, TV

    def vectors_end(first):
        received(first)
        OS[...] = TY[dp] + jnp.sum(TV[...], axis=0)

    def return_head_zero():
        total = scatter_end(*a_grad_second).astype(BF)
        for p in range(2):
            AAs[2 * p] = total[p][:, 0:192]
            AAs[2 * p + 1] = total[p][:, 192:384]
        AAr[blk] = AAs[blk]
        return swap_parts(lambda b: AAs.at[b], AAr)

    def up_out():
        for part in u_back:
            received(part)
        for b in range(BLK_SIZE):
            whole = jnp.concatenate([AUr[n, b] for n in range(CHUNKS)], axis=1).astype(F32)
            for i in range(DP_SIZE):
                at = 96 * (BLK_SIZE * i + b)
                OU[:, at : at + 96] = whole[:, 96 * i : 96 * (i + 1)]

    def joint_out():
        received(c_back)
        received(a_back)
        for b in range(BLK_SIZE):
            one, two = AAr[b].astype(F32), ACr[b].astype(F32)
            for s in range(3):
                at = 768 * s + 192 * b
                OJ[:, at : at + 64] = one[:, 64 * s : 64 * (s + 1)]
                OJ[:, at + 64 : at + 192] = two[:, 128 * s : 128 * (s + 1)]

    def result_end():
        for r in range(2):
            MID[r] = MID[r] + sum_end(1, r, result_second[r]) + dbias

    vectors_early()
    c_grad_second = scatter_middle(GC, RYc, Sc, RZc, c_grad_first)
    first_norm_back(0, first_second[0])
    a_grad_second = scatter_middle(GA, RYa, Sa, RZa, a_grad_first)
    first_norm_back(1, first_second[1])
    o_grad_second = scatter_middle(GO2, RYo, So, RZo, o_grad_first)
    vector_part = vectors_over_blk()
    u_back = [return_columns(u_grad_second[n], AUs.at[n], AUr.at[n]) for n in range(CHUNKS)]
    result_second.append(sum_middle(1, 1, result_first[1]))
    c_back = return_columns(c_grad_second, ACs, ACr)
    vector_part = vectors_over_dp(vector_part)
    down_out()
    a_back = return_head_zero()
    up_out()
    vectors_end(vector_part)
    OO[...] = scatter_end(*o_grad_second)
    result_end()
    joint_out()
    assert (count[0], count[2], count[1]) == (SENDS, RECEIVES, LOCALS), count
    for copies in started:
        sent(copies)

    @pl.when(inner)
    def _():
        for sems, _, five in started_over_z:
            sent((sems, five))

    @pl.when(jnp.logical_not(inner))
    def _():
        for sems, one, _ in started_over_z:
            sent((sems, one))


def finish_kernel(*refs):
    big_in, sums, big_out, small_out, sems = refs[:6], refs[6], refs[7:13], refs[13:21], refs[21]
    copies = []
    for n, (source, target) in enumerate(zip(big_in, big_out)):
        made = pltpu.make_async_copy(source, target, sems.at[n])
        made.start()
        copies.append(made)
    for row, width in enumerate(TILE_WIDTHS):
        small_out[row][...] = sums[row, 0:width]
    for made in copies:
        made.wait()


def fast_device(
    tokens, segment_ids, pad_mask, joint_weight, joint_bias, output_weight, output_bias,
    first_gain, first_shift, up_weight, up_bias, down_weight, down_bias,
    second_gain, second_shift, cotangent,
):
    vectors = (
        first_gain, first_shift, output_bias, second_gain, second_shift, down_bias,
        joint_bias, up_bias,
    )

    def vm(*shape, dtype=BF):
        return pltpu.VMEM(shape, dtype)

    def fm(*shape):
        return pltpu.VMEM(shape, F32)

    scratch = [
        fm(2, 128, 768), fm(2, 128, 768), vm(24, 2304), vm(24, 3072), vm(96, 768),
        vm(4, 24, 192), vm(4, 24, 384), vm(4, 24, 768), vm(CHUNKS, 4, 24, WIDE), vm(4, 24, 192), fm(8, 128), fm(8, 128), fm(8, 4, 8, 128),
        fm(4, 8, 128), fm(8, 512), fm(512, 8), fm(16, 768), fm(16, 192),
        vm(2, 4, 128, 768), vm(2, 4, 128, 768), vm(2, 4, 128, 768),
        vm(8, 2, 24, 384), vm(8, 4, 24, 384), vm(CHUNKS, 8, 4, 24, WIDE), vm(CHUNKS, 8, 96, WIDE),
        vm(4, 8, 24, 768), vm(768, 192), vm(768, 384), vm(CHUNKS, 768, WIDE), vm(768, 768),
        fm(2, 128, 768), fm(2, 128, 1), fm(2, 128, 768), fm(2, 128, 1),
        vm(2, 128, 768),
        vm(2, 3, 512, 64), vm(2, 3, 512, 64), vm(2, 3, 512, 64), vm(2, 3, 512, 512),
        fm(2, 3, 512, 64), vm(2, 4, 192, 128), vm(2, 4, 192, 128),
        vm(2, 4, 192, 128), vm(2, 4, 192, 128), vm(512, 64), vm(2, 512, 192), vm(2, 512, 384),
        vm(2, 512, 768), vm(2, 512, 768), vm(2, 512, 768), fm(2, 1, 768),
        vm(3, 2, 2, 2, 128, 768), vm(3, 2, 2, 128, 768), vm(3, 2, 128, 768), vm(3, 2, 128, 768),
        vm(CHUNKS, 4, 2, 96, WIDE), vm(CHUNKS, 4, 2, 4, 24, WIDE), vm(4, 2, 2, 24, 384), vm(4, 2, 4, 24, 384),
        vm(2, 2, 8, 24, 768), vm(4, 2, 24, 768),
        vm(CHUNKS, 4, 96, WIDE), vm(CHUNKS, 4, 4, 24, WIDE), vm(4, 2, 24, 384), vm(4, 4, 24, 384), vm(4, 24, 768),
        vm(CHUNKS, 4, 96, WIDE), vm(CHUNKS, 4, 4, 24, WIDE), vm(4, 2, 24, 384), vm(4, 4, 24, 384), vm(4, 24, 768),
        vm(CHUNKS, 3, 96, WIDE), vm(CHUNKS, 3, 4, 24, WIDE), vm(3, 2, 24, 384), vm(3, 4, 24, 384), vm(3, 24, 768),
        vm(3, 2, 96, WIDE), vm(2, 96, WIDE), vm(96, WIDE),
        vm(CHUNKS, 4, 24, WIDE), vm(CHUNKS, 4, 24, WIDE), vm(4, 24, 192), vm(4, 24, 192),
        vm(4, 24, 384), vm(4, 24, 384), vm(2, 8, 24, 768), vm(8, 24, 768), vm(8, 24, 768),
        fm(256, 128), fm(4, 8, 8, 128), fm(4, 8, 8, 128), fm(8, 8, 128), fm(7, 8, 128),
        fm(8, 768), fm(2, 1, 576),
        pltpu.SemaphoreType.DMA((SENDS,)), pltpu.SemaphoreType.DMA((RECEIVES,)),
        pltpu.SemaphoreType.DMA((LOCALS,)),
    ]
    vmem = pl.BlockSpec(memory_space=pltpu.VMEM)
    anywhere = pl.BlockSpec(memory_space=pl.ANY)
    big = [(2, 128, 768), (2, 128, 768), (24, 2304), (24, 768), (24, 3072), (96, 768)]
    made = pl.pallas_call(
        layer_kernel,
        out_shape=[fm(*shape) for shape in big] + [fm(8, 128)],
        in_specs=[anywhere] * 2 + [vmem] * 2 + [anywhere] * 4 + [vmem] * 8,
        out_specs=[vmem] * 7,
        scratch_shapes=scratch,
        compiler_params=pltpu.CompilerParams(
            collective_id=0, has_side_effects=True, vmem_limit_bytes=VMEM_MIB * 2**20
        ),
        cost_estimate=pl.CostEstimate(
            flops=13 * 10**9, bytes_accessed=6 * 10**6, transcendentals=4 * 10**6
        ),
    )(
        tokens, cotangent, segment_ids, pad_mask, joint_weight, up_weight, down_weight,
        output_weight, *vectors,
    )
    ends = pl.pallas_call(
        finish_kernel,
        out_shape=[jax.ShapeDtypeStruct(shape, F32) for shape in big]
        + [jax.ShapeDtypeStruct((width,), F32) for width in TILE_WIDTHS],
        in_specs=[vmem] * 7,
        out_specs=[anywhere] * 6 + [vmem] * 8,
        scratch_shapes=[pltpu.SemaphoreType.DMA((6,))],
    )(*(pltpu.with_memory_space_constraint(array, pltpu.VMEM) for array in made))
    result, grad_tokens, grad_j, grad_o, grad_u, grad_d = ends[:6]
    first_g, first_s, output_b, second_g, second_s, down_b, joint_b, up_b = ends[6:]
    return (
        result, grad_tokens, grad_j, joint_b, grad_o, output_b, first_g, first_s,
        grad_u, up_b, grad_d, down_b, second_g, second_s,
    )


def solution(mesh):
    placed = (
        P("dp", "blk", None),
        P("dp", "blk"),
        P("dp", "blk"),
        P(("dp", "blk"), None),
        P(("dp", "blk")),
        P(("dp", "blk"), None),
        P(("dp", "blk")),
        P(("dp", "blk")),
        P(("dp", "blk")),
        P(("dp", "blk"), None),
        P(("dp", "blk")),
        P(("dp", "blk"), None),
        P(("dp", "blk")),
        P(("dp", "blk")),
        P(("dp", "blk")),
        P("dp", "blk", None),
    )

    def spread(device_part):
        return jax.shard_map(
            device_part,
            mesh=mesh,
            in_specs=placed,
            out_specs=(
                P("dp", "blk", None),
                P("dp", "blk", None),
                P(("dp", "blk"), None),
                P(("dp", "blk")),
                P(("dp", "blk"), None),
                P(("dp", "blk")),
                P(("dp", "blk")),
                P(("dp", "blk")),
                P(("dp", "blk"), None),
                P(("dp", "blk")),
                P(("dp", "blk"), None),
                P(("dp", "blk")),
                P(("dp", "blk")),
                P(("dp", "blk")),
            ),
            check_vma=False,
        )

    def layer(*arrays):
        rows, length, features = arrays[0].shape
        shape = dict(mesh.shape)
        fits = (
            shape == {"dp": DP_SIZE, "blk": BLK_SIZE}
            and (rows, length, features) == (2 * shape["dp"], 512, 768)
            and arrays[9].shape[1] == 3072
        )
        return spread(fast_device if fits else per_device)(*arrays)

    return layer
```

```python
import jax
import jax.numpy as jnp
from jax import lax
from jax.experimental import pallas as pl
from jax.experimental.pallas import tpu as pltpu
from jax.sharding import PartitionSpec as P

HEADS = 12
SENDS, RECEIVES, LOCALS = 74, 92, 6
VMEM_MIB = 58


epsilon = 1e-05
masked_score = -1e30


def normalize(values_in, gain, shift):
    centered = values_in - jnp.mean(values_in, axis=-1, keepdims=True)
    inverse = lax.rsqrt(jnp.mean(centered * centered, axis=-1, keepdims=True) + epsilon)
    unit_rows = centered * inverse
    return (unit_rows * gain + shift, unit_rows, inverse)


def normalize_back(grad_normed, unit_rows, inverse, gain):
    scaled = grad_normed * gain
    grad_input = inverse * (
        scaled
        - jnp.mean(scaled, axis=-1, keepdims=True)
        - unit_rows * jnp.mean(scaled * unit_rows, axis=-1, keepdims=True)
    )
    return (
        grad_input,
        jnp.sum(grad_normed * unit_rows, axis=(0, 1)),
        jnp.sum(grad_normed, axis=(0, 1)),
    )


def project(activation, weight):
    return jnp.einsum("rcd,dn->rcn", activation, weight, preferred_element_type=jnp.float32)


def project_back(gradient, weight):
    return jnp.einsum("rcn,dn->rcd", gradient, weight, preferred_element_type=jnp.float32)


def outer_sum(activation, gradient):
    return jnp.einsum("rcd,rcn->dn", activation, gradient, preferred_element_type=jnp.float32)


def split_heads(matrix, head_count):
    return matrix.reshape(
        matrix.shape[0], matrix.shape[1], head_count, matrix.shape[2] // head_count
    )


def masked_scores(query_heads, key_heads, query_segment, key_segment, scaling):
    raw_scores = (
        jnp.einsum("rqhd,rkhd->rhqk", query_heads, key_heads, preferred_element_type=jnp.float32)
        * scaling
    )
    allowed = (query_segment[:, :, None] == key_segment[:, None, :])[:, None]
    return (jnp.where(allowed, raw_scores, masked_score), allowed)


def column_sums(gradient):
    return jnp.sum(gradient.astype(jnp.float32), axis=(0, 1))


def scatter_sum(gradient):
    summed = lax.psum_scatter(
        gradient.astype(jnp.bfloat16), ("dp", "blk"), scatter_dimension=0, tiled=True
    )
    return summed.astype(jnp.float32)


def per_device(
    tokens,
    segment_ids,
    pad_mask,
    joint_weight,
    joint_bias,
    output_weight,
    output_bias,
    first_gain,
    first_shift,
    up_weight,
    up_bias,
    down_weight,
    down_bias,
    second_gain,
    second_shift,
    cotangent,
):
    batch_rows, local_len, features = tokens.shape
    head_count = HEADS
    head_size = features // head_count
    scaling = head_size ** (-0.5)
    device_count = lax.axis_size("dp") * lax.axis_size("blk")
    small_parts = (
        joint_bias, output_bias, first_gain, first_shift, up_bias, down_bias, second_gain, second_shift
    )
    small_all = lax.all_gather(jnp.concatenate(small_parts), ("dp", "blk"), axis=0, tiled=True)
    small_all = small_all.reshape(device_count, -1)
    small_full = []
    small_at = 0
    for part in small_parts:
        small_full.append(small_all[:, small_at : small_at + part.shape[0]].reshape(-1))
        small_at += part.shape[0]
    full_joint_bias, full_output_bias, gain_one, shift_one = small_full[:4]
    full_up_bias, full_down_bias, gain_two, shift_two = small_full[4:]
    full_joint = lax.all_gather(joint_weight, ("dp", "blk"), axis=0, tiled=True)
    full_output = lax.all_gather(output_weight, ("dp", "blk"), axis=0, tiled=True)
    normed_one, unit_one, inverse_one = normalize(
        tokens, gain_one.astype(jnp.float32), shift_one.astype(jnp.float32)
    )
    normed_one_low = normed_one.astype(jnp.bfloat16)
    joint = project(normed_one_low, full_joint)
    bias_values = full_joint_bias.astype(jnp.float32)
    query = (joint[..., :features] + bias_values[:features]).astype(jnp.bfloat16)
    keys = joint[..., features : 2 * features].astype(jnp.bfloat16)
    values = (joint[..., 2 * features :] + bias_values[features:]).astype(jnp.bfloat16)
    key_segment = jnp.where(pad_mask == 1, segment_ids, -1)
    query_heads = split_heads(query, head_count)
    top_score = jnp.full((batch_rows, head_count, local_len), masked_score, jnp.float32)
    key_portion = lax.all_gather(keys, "blk", axis=1, tiled=True)
    value_portion = lax.all_gather(values, "blk", axis=1, tiled=True)
    segment_portion = lax.all_gather(key_segment, "blk", axis=1, tiled=True)
    scores, allowed = masked_scores(
        query_heads, split_heads(key_portion, head_count), segment_ids, segment_portion, scaling
    )
    new_top = jnp.maximum(top_score, jnp.max(scores, axis=-1))
    weights = jnp.where(allowed, jnp.exp(scores - new_top[..., None]), 0.0)
    total_weight = jnp.sum(weights, axis=-1)
    weighted = jnp.einsum(
        "rhqk,rkhd->rhqd",
        weights.astype(jnp.bfloat16),
        split_heads(value_portion, head_count),
        preferred_element_type=jnp.float32,
    )
    top_score, total_weight, weighted = (new_top, total_weight, weighted)
    log_total = top_score + jnp.log(total_weight)
    attended_heads = weighted / total_weight[..., None]
    attended = jnp.transpose(attended_heads, (0, 2, 1, 3)).reshape(batch_rows, local_len, features)
    attended_low = attended.astype(jnp.bfloat16)
    middle = tokens + project(attended_low, full_output) + full_output_bias.astype(jnp.float32)
    full_up = lax.all_gather(up_weight, ("dp", "blk"), axis=0, tiled=True)
    full_down = lax.all_gather(down_weight, ("dp", "blk"), axis=0, tiled=True)
    normed_two, unit_two, inverse_two = normalize(
        middle, gain_two.astype(jnp.float32), shift_two.astype(jnp.float32)
    )
    normed_two_low = normed_two.astype(jnp.bfloat16)
    hidden = project(normed_two_low, full_up) + full_up_bias.astype(jnp.float32)
    activated, gelu_pullback = jax.vjp(jax.nn.gelu, hidden)
    activated_low = activated.astype(jnp.bfloat16)
    result = middle + project(activated_low, full_down) + full_down_bias.astype(jnp.float32)
    later_up, later_down, later_gain_two = full_up, full_down, gain_two
    grad_result = cotangent.astype(jnp.bfloat16)
    grad_down_weight = outer_sum(activated_low, grad_result)
    grad_down_bias = column_sums(grad_result)
    grad_activated = project_back(grad_result, later_down)
    grad_hidden = gelu_pullback(grad_activated)[0].astype(jnp.bfloat16)
    grad_up_bias = column_sums(grad_hidden)
    grad_up_weight = outer_sum(normed_two_low, grad_hidden)
    grad_normed_two = project_back(grad_hidden, later_up)
    grad_from_second, grad_gain_two, grad_shift_two = normalize_back(
        grad_normed_two, unit_two, inverse_two, later_gain_two.astype(jnp.float32)
    )
    grad_middle = cotangent + grad_from_second
    grad_up_shard = scatter_sum(grad_up_weight)
    grad_down_shard = scatter_sum(grad_down_weight)
    later_joint, later_output, later_gain_one = full_joint, full_output, gain_one
    grad_branch = grad_middle.astype(jnp.bfloat16)
    grad_output_weight = outer_sum(attended_low, grad_branch)
    grad_output_bias = column_sums(grad_branch)
    grad_attended = project_back(grad_branch, later_output).astype(jnp.bfloat16)
    grad_heads = split_heads(grad_attended, head_count)
    delta = jnp.einsum("rqhd,rhqd->rhq", grad_heads.astype(jnp.float32), attended_heads)
    key_heads = split_heads(key_portion, head_count)
    scores, allowed = masked_scores(query_heads, key_heads, segment_ids, segment_portion, scaling)
    probs = jnp.where(allowed, jnp.exp(scores - log_total[..., None]), 0.0)
    grad_probs = jnp.einsum(
        "rqhd,rkhd->rhqk",
        grad_heads,
        split_heads(value_portion, head_count),
        preferred_element_type=jnp.float32,
    )
    grad_scores = (probs * (grad_probs - delta[..., None])).astype(jnp.bfloat16)
    grad_query = scaling * jnp.einsum(
        "rhqk,rkhd->rqhd", grad_scores, key_heads, preferred_element_type=jnp.float32
    )
    every_total, every_delta = (
        lax.all_gather(log_total, "blk", axis=2, tiled=True),
        lax.all_gather(delta, "blk", axis=2, tiled=True),
    )
    own_keys = split_heads(keys, head_count)
    own_values = split_heads(values, head_count)
    query_portion = lax.all_gather(query, "blk", axis=1, tiled=True)
    grad_portion = lax.all_gather(grad_attended, "blk", axis=1, tiled=True)
    segment_portion = lax.all_gather(segment_ids, "blk", axis=1, tiled=True)
    portion_queries = split_heads(query_portion, head_count)
    portion_grads = split_heads(grad_portion, head_count)
    scores, allowed = masked_scores(
        portion_queries, own_keys, segment_portion, key_segment, scaling
    )
    probs = jnp.where(allowed, jnp.exp(scores - every_total[..., None]), 0.0)
    grad_values = jnp.einsum(
        "rhqk,rqhd->rkhd",
        probs.astype(jnp.bfloat16),
        portion_grads,
        preferred_element_type=jnp.float32,
    )
    grad_probs = jnp.einsum(
        "rqhd,rkhd->rhqk", portion_grads, own_values, preferred_element_type=jnp.float32
    )
    grad_scores = (probs * (grad_probs - every_delta[..., None])).astype(jnp.bfloat16)
    grad_keys = scaling * jnp.einsum(
        "rhqk,rqhd->rkhd", grad_scores, portion_queries, preferred_element_type=jnp.float32
    )
    grad_keys, grad_values = (grad_keys, grad_values)
    grad_joint = jnp.concatenate(
        [
            grad_query.reshape(batch_rows, local_len, features),
            grad_keys.reshape(batch_rows, local_len, features),
            grad_values.reshape(batch_rows, local_len, features),
        ],
        axis=-1,
    ).astype(jnp.bfloat16)
    grad_joint_weight = outer_sum(normed_one_low, grad_joint)
    grad_joint_bias = jnp.concatenate(
        [column_sums(grad_joint[..., :features]), column_sums(grad_joint[..., 2 * features :])]
    )
    grad_normed_one = project_back(grad_joint, later_joint)
    grad_from_first, grad_gain_one, grad_shift_one = normalize_back(
        grad_normed_one, unit_one, inverse_one, later_gain_one.astype(jnp.float32)
    )
    grad_tokens = grad_middle + grad_from_first
    small_grads = (
        grad_joint_bias, grad_output_bias, grad_gain_one, grad_shift_one,
        grad_up_bias, grad_down_bias, grad_gain_two, grad_shift_two,
    )
    packed = jnp.concatenate([part.reshape(device_count, -1) for part in small_grads], axis=1)
    own = lax.psum_scatter(packed, ("dp", "blk"), scatter_dimension=0, tiled=True)[0]
    small_shards = []
    small_at = 0
    for part in small_parts:
        small_shards.append(own[small_at : small_at + part.shape[0]])
        small_at += part.shape[0]
    return (
        result,
        grad_tokens,
        scatter_sum(grad_joint_weight),
        small_shards[0],
        scatter_sum(grad_output_weight),
        small_shards[1],
        small_shards[2],
        small_shards[3],
        grad_up_shard,
        small_shards[4],
        grad_down_shard,
        small_shards[5],
        small_shards[6],
        small_shards[7],
    )


Z_SIZE, Y_SIZE, BLK_SIZE = 4, 2, 4
DP_SIZE = Z_SIZE * Y_SIZE
MESH = pl.DeviceIdType.MESH
BF = jnp.bfloat16
F32 = jnp.float32
WIDE, CHUNKS = 256, 3
TILE_WIDTHS = (24, 24, 24, 24, 24, 24, 48, 96)


def dot_nn(left, right):
    return lax.dot_general(left, right, (((1,), (0,)), ((), ())), preferred_element_type=F32)


def dot_nt(left, right):
    return lax.dot_general(left, right, (((1,), (1,)), ((), ())), preferred_element_type=F32)


def dot_tn(left, right):
    return lax.dot_general(left, right, (((0,), (0,)), ((), ())), preferred_element_type=F32)


def lane_pieces(lanes, width):
    lane = lax.broadcasted_iota(jnp.int32, (1, lanes), 1).astype(F32)
    piece = jnp.floor((lane + 0.5) * (1.0 / width))
    return piece, lane - width * piece


def piece_placer(lanes, width):
    place = lax.broadcasted_iota(jnp.int32, (128, lanes), 0).astype(F32)
    _, within = lane_pieces(lanes, width)
    return jnp.where(place == within, 1.0, 0.0).astype(BF)


def layer_kernel(*refs):
    ins, outs, scr = refs[:16], refs[16:23], refs[23:]
    (tok_in, cot_in, seg_in, pad_in, jw_in, uw_in, dw_in, ow_in), vectors = ins[:8], ins[8:]
    MID, GM, OJ, OO, OU, OD, OS = outs
    (
        TOK, COT, JW, UW, DW, JP0, JP1, UPW, UP, AP, TILE, SEGT, G, SEG, KSEG, QSEG, PV, QVB,
        N1, N2, GR, WJS0, WJS1, WUS, WDS, WOS, WJ0, WJ1, WU, WO,
        U1, I1, U2, I2, GB,
        Q, K, V, PB, OF, AT, AR, DA, DR, DOH, GJ0, GJ1,
        GP, ACT, GH, UBS, PT, RC, SX, RX,
        GD, GU, GA, GC, GO, GO2, RYd, RYu, RYa, RYc, RYo, Sd, Su, Sa, Sc, So,
        RZd, RZu, RZa, RZc, RZo, RZ0, S0, RY0, AUs, AUr, AAs, AAr, ACs, ACr, RCo, SXo, RXo,
        TS, TB, TL, TY, TV, VS, JBS, ssem, rsem, lsem,
    ) = scr
    dp = lax.axis_index("dp")
    blk = lax.axis_index("blk")
    z, y = dp // 2, dp % 2
    x, c = blk // 2, blk % 2
    count = [0, 0, 0]
    started = []

    def local(src, dst):
        n = count[1]
        count[1] += 1
        made = pltpu.make_async_copy(src, dst, lsem.at[n])
        made.start()
        return made

    def to_send():
        n = count[0]
        count[0] += 1
        return ssem.at[n]

    def to_receive():
        n = count[2]
        count[2] += 1
        return rsem.at[n]

    def group():
        return to_send(), to_receive()

    def send(src, dst, dev, sems):
        made = pltpu.make_async_remote_copy(
            src_ref=src, dst_ref=dst, send_sem=sems[0], recv_sem=sems[1],
            device_id=dev, device_id_type=MESH,
        )
        made.start()
        return made

    def wait_bytes(sem, ref):
        pltpu.make_async_copy(ref, ref, sem).wait()

    def received(copies):
        wait_bytes(copies[0][1], copies[1])

    def later_sent(copies):
        started.append(copies)

    def sent(copies):
        wait_bytes(copies[0][0], copies[1])

    started_over_z = []

    def later_sent_over_z(copies):
        started_over_z.append(copies)

    core_peer = (dp, 2 * x + 1 - c)
    x_peer = (dp, 2 * (1 - x) + c)
    far_peer = (dp, 2 * (1 - x) + 1 - c)
    blk_peers = (x_peer, far_peer, core_peer)
    y_peer = (2 * z + 1 - y, blk)
    inner = (z == 1) | (z == 2)
    z_left = (2 * ((z + Z_SIZE - 1) % Z_SIZE) + y, blk)
    z_right = (2 * ((z + 1) % Z_SIZE) + y, blk)
    z_side = (2 * ((z // 2) * 2 + 1 - z % 2) + y, blk)
    z_across = (2 * (Z_SIZE - 1 - z) + y, blk)

    def z_at(k):
        return (z + k) % Z_SIZE

    ow_copy = local(ow_in, WOS.at[blk, dp])
    jw_copy = local(jw_in, JW)
    tok_copy = local(tok_in, TOK)
    uw_copy = local(uw_in, UW)
    dw_copy = local(dw_in, DW)
    cot_copy = local(cot_in, COT)

    partners = [(dp, (blk + j) % BLK_SIZE) for j in range(1, BLK_SIZE)]
    partners += [((dp + i) % DP_SIZE, blk) for i in range(1, DP_SIZE)]

    def entry_barrier():
        barrier = pltpu.get_barrier_semaphore()
        near = list(blk_peers) + [y_peer]
        for dev in near:
            pl.semaphore_signal(barrier, inc=1, device_id=dev, device_id_type=MESH)

        @pl.when(z > 0)
        def _():
            pl.semaphore_signal(barrier, inc=1, device_id=z_left, device_id_type=MESH)

        @pl.when(z < Z_SIZE - 1)
        def _():
            pl.semaphore_signal(barrier, inc=1, device_id=z_right, device_id_type=MESH)

        @pl.when(inner)
        def _():
            pl.semaphore_wait(barrier, 6)

        @pl.when(jnp.logical_not(inner))
        def _():
            pl.semaphore_wait(barrier, 5)

    def swap_parts(parts, landing, chunked=False):
        sems = group()
        for dev in blk_peers:
            send(parts(dev[1]), landing.at[:, blk] if chunked else landing.at[blk], dev, sems)
        span = landing.at[:, pl.ds(c, 3)] if chunked else landing.at[pl.ds(c, 3)]
        later_sent((sems, span))
        return sems, span

    def small_tiles():
        TILE[...] = jnp.zeros_like(TILE)
        for row, (ref, width) in enumerate(zip(vectors, TILE_WIDTHS)):
            TILE[row : row + 1, 0:width] = ref[...].astype(F32).reshape(1, width)
        segment = seg_in[...].astype(F32)
        SEGT[...] = jnp.zeros_like(SEGT)
        SEGT[0:2] = segment
        SEGT[2:4] = jnp.where(pad_in[...] == 1, segment, -1.0)
        G[dp, blk] = TILE[...]
        SEG[blk] = SEGT[...]


    small_tiles()
    entry_barrier()

    def stats(values):
        mean = jnp.mean(values, axis=-1, keepdims=True)
        centered = values - mean
        inverse = lax.rsqrt(jnp.mean(centered * centered, axis=-1, keepdims=True) + epsilon)
        return centered * inverse, inverse

    def dp_part(slab, span):
        return slab, span, [group(), group()] + [(None, to_receive()) for _ in range(3)]

    def slabs_part(slabs):
        return dp_part(lambda i: slabs.at[i], lambda n: slabs.at[pl.ds(c, n)])

    def own_over_y(part):
        slab, span, sems = part
        send(slab(dp), slab(dp), y_peer, sems[0])
        later_sent((sems[0], span(4)))

    def own_over_z(part):
        slab, span, sems = part

        @pl.when(z < Z_SIZE - 1)
        def _():
            send(slab(dp), slab(dp), z_right, (sems[1][0], sems[1][1]))

        @pl.when(z > 0)
        def _():
            send(slab(dp), slab(dp), z_left, (sems[1][0], sems[2][1]))

        later_sent_over_z((sems[1], span(1), span(5)))

    def pass_on(part, there, arrived, onward, more, dev):
        slab, _, sems = part
        received((arrived, slab(there)))
        send(slab(there), slab(there), y_peer, sems[0])
        if onward is not None:

            @pl.when(more)
            def _():
                send(slab(there), slab(there), dev, (sems[1][0], onward[1]))

    def step_one(part):
        sems = part[2]

        @pl.when(z > 0)
        def _():
            pass_on(part, dp - 2, sems[1], sems[3], z < Z_SIZE - 1, z_right)

        @pl.when(z < Z_SIZE - 1)
        def _():
            pass_on(part, dp + 2, sems[2], sems[3], z > 0, z_left)

    def step_two(part):
        sems = part[2]

        @pl.when(z >= 2)
        def _():
            pass_on(part, dp - 4, sems[3], sems[4], z == 2, z_right)

        @pl.when(z < 2)
        def _():
            pass_on(part, dp + 4, sems[3], sems[4], z == 1, z_left)

    def step_three(part):
        sems = part[2]

        @pl.when(z == Z_SIZE - 1)
        def _():
            pass_on(part, dp - 6, sems[4], None, None, None)

        @pl.when(z == 0)
        def _():
            pass_on(part, dp + 6, sems[4], None, None, None)

    def dp_end(part):
        _, span, sems = part
        received((sems[0], span(4)))

    def gather_start(buf, r):
        over_x, to_core = group(), group()
        send(buf.at[r, blk], buf.at[r, blk], x_peer, over_x)
        send(buf.at[r, blk], buf.at[r, blk], core_peer, to_core)
        later_sent((over_x, buf.at[r, blk]))
        later_sent((to_core, buf.at[r, pl.ds(c, 2)]))
        return buf, r, over_x, to_core

    def gather_forward(part):
        buf, r, over_x, to_core = part
        received((over_x, buf.at[r, x_peer[1]]))
        send(buf.at[r, x_peer[1]], buf.at[r, x_peer[1]], core_peer, to_core)

    def gather_end(part):
        buf, r, _, to_core = part
        received((to_core, buf.at[r, pl.ds(c, 2)]))

    ow_copy.wait()
    o_part = dp_part(lambda i: WOS.at[blk, i], lambda n: WOS.at[blk, pl.ds(c, n)])
    a_part, c_part, g_part = slabs_part(WJS0), slabs_part(WJS1), slabs_part(G)

    def chunks_part(slabs):
        return dp_part(lambda i: slabs.at[:, i], lambda n: slabs.at[:, pl.ds(c, n)])

    u_part, d_part = chunks_part(WUS), chunks_part(WDS)
    own_over_z(o_part)
    own_over_y(o_part)

    def split_joint():
        jw_copy.wait()
        for b in range(BLK_SIZE):
            for s in range(3):
                at = 768 * s + 192 * b
                JP0[b, :, 64 * s : 64 * (s + 1)] = JW[:, at : at + 64]
                JP1[b, :, 128 * s : 128 * (s + 1)] = JW[:, at + 64 : at + 192]

    def swap_columns(parts, slabs):
        slabs[dp, blk] = parts[blk]
        return swap_parts(lambda b: parts.at[b], slabs.at[dp])

    split_joint()
    AP[blk] = JP0[blk]
    a_first = swap_parts(lambda b: JP0.at[b], AP)
    g_first = swap_parts(lambda b: TILE, G.at[dp])
    c_first = swap_columns(JP1, WJS1)
    seg_copies = swap_parts(lambda b: SEGT, SEG)

    def first_stats():
        tok_copy.wait()
        firsts = []
        for r in range(2):
            unit, inverse = stats(TOK[r])
            U1[r] = unit
            I1[r] = inverse
            N1[r, blk] = unit.astype(BF)
            firsts.append(gather_start(N1, r))
        return firsts

    n1_part = first_stats()
    n1_sent = (started[-4:-2], started[-2:])
    del started[-4:]

    def split_up():
        uw_copy.wait()
        for i in range(DP_SIZE):
            for b in range(BLK_SIZE):
                at = 96 * (BLK_SIZE * i + b)
                UPW[b, :, 96 * i : 96 * (i + 1)] = UW[:, at : at + 96]
        for n in range(CHUNKS):
            for b in range(BLK_SIZE):
                UP[n, b] = UPW[b, :, WIDE * n : WIDE * (n + 1)]

    def split_down():
        dw_copy.wait()
        for n in range(CHUNKS):
            WDS[n, dp] = DW[:, WIDE * n : WIDE * (n + 1)]

    def early_down():
        split_down()
        own_over_y(d_part)

    def low_cotangent():
        cot_copy.wait()
        for r in range(2):
            GR[r, blk] = COT[r].astype(BF)

    early_down()
    received(a_first)
    for p in range(2):
        WJS0[dp, p, :, 0:192] = AP[2 * p]
        WJS0[dp, p, :, 192:384] = AP[2 * p + 1]
    own_over_z(a_part)
    own_over_y(a_part)
    received(g_first)
    own_over_z(g_part)
    own_over_y(g_part)
    received(c_first)
    own_over_z(c_part)
    own_over_y(c_part)
    split_up()
    WUS[:, dp, blk] = UP[:, blk]
    u_first = swap_parts(lambda b: UP.at[:, b], WUS.at[:, dp], True)
    low_cotangent()
    gr_part = [gather_start(GR, r) for r in range(2)]
    step_one(a_part)
    step_one(g_part)
    step_one(o_part)
    step_two(a_part)
    step_two(g_part)
    step_two(o_part)
    gather_forward(n1_part[0])
    step_one(c_part)
    step_three(a_part)
    step_three(g_part)
    step_three(o_part)
    step_two(c_part)
    received(u_first)
    own_over_z(u_part)
    own_over_z(d_part)
    gather_forward(n1_part[1])
    dev_id = lax.broadcasted_iota(jnp.int32, (32, 1, 1), 0).astype(F32)
    blk_f = blk.astype(F32)
    piece24, _ = lane_pieces(768, 24)
    piece48, _ = lane_pieces(192, 48)
    piece96, _ = lane_pieces(768, 96)

    def mask24():
        return piece24[None] == dev_id

    def mask48(first_dev):
        return piece48[None] + (4.0 * blk_f + first_dev) == dev_id

    def mask96():
        return 4.0 * piece96[None] + blk_f == dev_id

    def place24():
        return piece_placer(768, 24)

    def place48():
        return piece_placer(192, 48)

    def place96():
        return piece_placer(768, 96)

    def small_end():
        dp_end(g_part)
        tiles = G[...].reshape(32 * 8, 128).astype(BF)

        def placed(placer, mask, lanes):
            spread = dot_nn(tiles, placer).reshape(32, 8, lanes)
            return jnp.sum(jnp.where(mask, spread, 0.0), axis=0)

        PV[0:8] = placed(place24(), mask24(), 768)
        PV[8:16] = placed(place96(), mask96(), 768)
        QVB[0:8] = placed(place48(), mask48(0.0), 192)
        QVB[8:16] = placed(place48(), mask48(16.0), 192)

    def segments_end():
        received(seg_copies)
        eye = jnp.where(
            lax.broadcasted_iota(jnp.int32, (128, 128), 0)
            == lax.broadcasted_iota(jnp.int32, (128, 128), 1), 1.0, 0.0,
        ).astype(BF)
        for b in range(BLK_SIZE):
            part = SEG[b]
            KSEG[:, 128 * b : 128 * (b + 1)] = part
            QSEG[128 * b : 128 * (b + 1)] = dot_nt(eye, part.astype(BF))


    segments_end()
    small_end()
    gain1, shift1, obias = PV[0:1], PV[1:2], PV[2:3]
    gain2, shift2, dbias = PV[3:4], PV[4:5], PV[5:6]

    def compact(slabs, whole):
        for i in range(DP_SIZE):
            rows = slabs(i).astype(F32)
            rows = rows.reshape(96, rows.shape[-1])
            whole[96 * i : 96 * (i + 1), :] = rows.astype(BF)

    def norm_rows(r):
        gather_end(n1_part[r])
        for copies in n1_sent[r]:
            sent(copies)
        for b in range(BLK_SIZE):
            N1[r, b] = (N1[r, b].astype(F32) * gain1 + shift1).astype(BF)

    def qkv_one(r):
        joint = dot_nn(N1[r].reshape(512, 768), WJ0[...])
        qbias, vbias = QVB[6:7, 0:64], QVB[14:15, 0:64]
        Q[r, 0] = ((joint[:, :64] + qbias).astype(BF).astype(F32) * 0.125).astype(BF)
        K[r, 0] = joint[:, 64:128].astype(BF)
        V[r, 0] = (joint[:, 128:] + vbias).astype(BF)

    def qkv_two(r):
        joint = dot_nn(N1[r].reshape(512, 768), WJ1[...])
        qbias, vbias = QVB[6:7, 64:192], QVB[14:15, 64:192]
        query = ((joint[:, :128] + qbias).astype(BF).astype(F32) * 0.125).astype(BF)
        keys = joint[:, 128:256].astype(BF)
        values = (joint[:, 256:] + vbias).astype(BF)
        for h in (1, 2):
            lanes = slice(64 * (h - 1), 64 * h)
            Q[r, h] = query[:, lanes]
            K[r, h] = keys[:, lanes]
            V[r, h] = values[:, lanes]

    def attend(r, h):
        scores = dot_nt(Q[r, h], K[r, h])
        scores = jnp.where(QSEG[:, r : r + 1] == KSEG[2 + r : 3 + r, :], scores, masked_score)
        top = jnp.max(scores, axis=-1, keepdims=True)
        expos = jnp.exp(scores - top)
        total = jnp.sum(expos, axis=-1, keepdims=True)
        probs = (expos * (1.0 / total)).astype(BF)
        PB[r, h] = probs
        out = dot_nn(probs, V[r, h])
        OF[r, h] = out
        if h:
            AT[r, :, 0:128, 64 * (h - 1) : 64 * h] = out.astype(BF).reshape(4, 128, 64)
        else:
            halves = out.astype(BF).reshape(4, 2, 64, 64)
            AT[r, :, 128:192, 0:64] = halves[:, 0]
            AT[r, :, 128:192, 64:128] = halves[:, 1]

    def swap_heads(src, dst, r):
        dst[r, blk] = src[r, blk]
        return swap_parts(lambda b: src.at[r, b], dst.at[r])

    dp_end(a_part)
    for i in range(DP_SIZE):
        pairs = WJS0[i].astype(F32)
        rows = [pairs[p][:, 192 * s : 192 * (s + 1)] for p in range(2) for s in range(2)]
        WJ0[96 * i : 96 * (i + 1), :] = jnp.concatenate(rows, axis=0).astype(BF)
    dp_end(o_part)
    wo_x, wo_core = group(), group()
    send(WOS.at[blk], WOS.at[blk], x_peer, wo_x)
    send(WOS.at[blk], WOS.at[blk], core_peer, wo_core)
    later_sent((wo_x, WOS.at[blk]))
    later_sent((wo_core, WOS.at[pl.ds(c, 2)]))
    norm_rows(0)
    qkv_one(0)
    step_three(c_part)
    attend(0, 0)
    own_over_y(u_part)
    norm_rows(1)
    qkv_one(1)
    attend(1, 0)
    step_one(u_part)
    dp_end(c_part)
    compact(lambda i: WJS1[i], WJ1)
    qkv_two(0)
    attend(0, 1)
    attend(0, 2)
    at_copies = [swap_heads(AT, AR, 0)]
    gather_forward(gr_part[0])
    qkv_two(1)
    step_two(u_part)
    attend(1, 1)
    step_one(d_part)
    attend(1, 2)
    at_copies.append(swap_heads(AT, AR, 1))
    received((wo_x, WOS.at[x_peer[1]]))
    send(WOS.at[x_peer[1]], WOS.at[x_peer[1]], core_peer, wo_core)
    received((wo_core, WOS.at[pl.ds(c, 2)]))
    compact(lambda i: WOS[:, i], WO)

    def head_zero(block):
        packed = block[128:192]
        return jnp.concatenate([packed[:, 0:64], packed[:, 64:128]], axis=0)

    def middle_rows(r):
        received(at_copies[r])
        total = TOK[r] + obias
        for b in range(BLK_SIZE):
            block = AR[r, b]
            total = total + dot_nn(head_zero(block), WO[192 * b : 192 * b + 64, :])
            total = total + dot_nn(block[0:128], WO[192 * b + 64 : 192 * (b + 1), :])
        MID[r] = total
        unit, inverse = stats(total)
        U2[r] = unit
        I2[r] = inverse
        N2[r, blk] = (unit * gain2 + shift2).astype(BF)
        return gather_start(N2, r)

    n2_part = [middle_rows(0)]
    step_three(u_part)
    n2_part.append(middle_rows(1))
    step_two(d_part)
    gather_forward(gr_part[1])
    dp_end(u_part)
    for n in range(CHUNKS):
        compact(lambda i: WUS[n, i], WU.at[n])
    gather_forward(n2_part[0])
    step_three(d_part)
    gather_end(n2_part[0])

    def rows_of(buf, r):
        return buf[r].reshape(512, 768)

    def up(r):
        for n in range(CHUNKS):
            cols = slice(WIDE * n, WIDE * (n + 1))
            hidden = dot_nn(rows_of(N2, r), WU[n]) + PV[15:16, cols]
            square = hidden * hidden
            bent = jnp.tanh(hidden * (0.7978845608028654 + 0.035677408136300125 * square))
            half = 0.5 * (1.0 + bent)
            ACT[r, :, cols] = (hidden * half).astype(BF)
            slope = 0.3989422804014327 + 0.05351611220445019 * square
            GP[r, :, cols] = (half + hidden * (1.0 - bent * bent) * slope).astype(BF)

    def hidden_back(r):
        for n in range(2):
            cols = slice(384 * n, 384 * (n + 1))
            weight = jnp.concatenate(
                [WDS[m, 4 * n : 4 * (n + 1)].reshape(384, WIDE) for m in range(CHUNKS)], axis=1
            )
            grad = dot_nt(rows_of(GR, r), weight)
            grad = (grad * GP[r, :, cols].astype(F32)).astype(BF)
            GH[r, :, cols] = grad
            UBS[r, :, cols] = jnp.sum(grad.astype(F32), axis=0, keepdims=True)

    def sum_store(i, r, cols, values):
        PT[i, r, :, :, :, cols] = values.reshape(2, 2, 128, values.shape[-1]).astype(BF)

    def sum_start(i, r):
        sems = group()
        send(PT.at[i, r, :, 1 - c], RC.at[i, r], core_peer, sems)
        later_sent((sems, RC.at[i, r]))
        return sems, RC.at[i, r]

    def sum_middle(i, r, first):
        received(first)
        SX[i, r] = (PT[i, r, 1 - x, c].astype(F32) + RC[i, r, 1 - x].astype(F32)).astype(BF)
        sems = group()
        send(SX.at[i, r], RX.at[i, r], x_peer, sems)
        later_sent((sems, RX.at[i, r]))
        return sems, RX.at[i, r]

    def sum_end(i, r, second):
        received(second)
        return PT[i, r, x, c].astype(F32) + RC[i, r, x].astype(F32) + RX[i, r].astype(F32)

    def second_back(r):
        for n in range(3):
            cols = slice(256 * n, 256 * (n + 1))
            weight = jnp.concatenate([WU[m, cols, :] for m in range(CHUNKS)], axis=1)
            sum_store(0, r, cols, dot_nt(GH[r], weight))
        return sum_start(0, r)

    def first_back(r):
        for n in range(3):
            cols = slice(256 * n, 256 * (n + 1))
            sum_store(
                2, r, cols, dot_nt(GJ0[r], WJ0[cols, :]) + dot_nt(GJ1[r], WJ1[cols, :])
            )
        return sum_start(2, r)

    def down(r):
        for n in range(CHUNKS):
            cols = slice(WIDE * n, WIDE * (n + 1))
            sum_store(1, r, cols, dot_nn(ACT[r], WDS[n].reshape(768, WIDE)))
        return sum_start(1, r)

    def scatter_start(parts, recv):
        sems = group()
        send(parts.at[:, 1 - y], recv, y_peer, sems)
        later_sent((sems, recv))
        return sems, recv

    def scatter_middle(parts, recv, sums, landing, first):
        received(first)
        sums[...] = (parts[:, y].astype(F32) + recv[...].astype(F32)).astype(BF)
        sems = group()
        for k in range(1, Z_SIZE):
            send(sums.at[z_at(k)], landing.at[k - 1], (2 * z_at(k) + y, blk), sems)
        later_sent((sems, landing))
        return sums, landing, (sems, landing)

    def scatter_end(sums, landing, second):
        received(second)
        total = sums[z].astype(F32)
        for k in range(Z_SIZE - 1):
            total = total + landing[k].astype(F32)
        return total

    def return_columns(part, sends, recvs):
        sends[...] = scatter_end(*part).astype(BF)
        recvs[blk] = sends[blk]
        return swap_parts(lambda b: sends.at[b], recvs)

    def down_grad(n):
        grads = GR[:, :, :, WIDE * n : WIDE * (n + 1)].reshape(1024, WIDE)
        for m in range(2):
            cols = slice(384 * m, 384 * (m + 1))
            grad = dot_tn(ACT[:, :, cols].reshape(1024, 384), grads)
            GD[n, 2 * m : 2 * m + 2] = grad.reshape(2, 2, 96, WIDE).astype(BF)

    def row_grad(rows, grads, parts):
        for m in range(2):
            cols = slice(384 * m, 384 * (m + 1))
            grad = dot_tn(rows[:, :, :, cols].reshape(1024, 384), grads)
            parts[2 * m : 2 * m + 2] = grad.reshape(2, 2, 4, 24, grad.shape[-1]).astype(BF)

    def up_grad(n):
        row_grad(N2, GH[:, :, WIDE * n : WIDE * (n + 1)].reshape(1024, WIDE), GU.at[n])

    def joint_grad_one():
        for m in range(2):
            rows = N1[:, :, :, 384 * m : 384 * (m + 1)].reshape(1024, 384)
            grad = dot_tn(rows, GJ0[...].reshape(1024, 192)).reshape(2, 2, 4, 24, 192).astype(BF)
            for p in range(2):
                GA[2 * m : 2 * m + 2, :, p, :, 0:192] = grad[:, :, 2 * p]
                GA[2 * m : 2 * m + 2, :, p, :, 192:384] = grad[:, :, 2 * p + 1]
        return scatter_start(GA, RYa)

    def joint_grad_two():
        row_grad(N1, GJ1[...].reshape(1024, 384), GC)
        return scatter_start(GC, RYc)

    def output_grad():
        for b in range(BLK_SIZE):
            blocks = [AR[r, b] for r in range(2)]
            zero = jnp.concatenate([head_zero(block) for block in blocks], axis=0)
            rest = jnp.concatenate([block[0:128] for block in blocks], axis=0)
            grads = GB[...].reshape(256, 768)
            grad = jnp.concatenate([dot_tn(zero, grads), dot_tn(rest, grads)], axis=0)
            grad = grad.reshape(2, 4, 24, 768).astype(BF)
            for i in range(4):
                GO[i // 2, i % 2, 2 * b : 2 * b + 2] = grad[:, i]
        sems = group()
        send(GO.at[:, 1 - c], RCo, core_peer, sems)
        later_sent((sems, RCo))
        return sems, RCo

    def output_grad_middle(first):
        received(first)
        SXo[...] = (GO[1 - x, c].astype(F32) + RCo[1 - x].astype(F32)).astype(BF)
        sems = group()
        send(SXo, RXo, x_peer, sems)
        later_sent((sems, RXo))
        return sems, RXo

    def norm_back(e, unit, inverse, gain):
        f = e * gain
        grad = inverse * (
            f - jnp.mean(f, axis=-1, keepdims=True)
            - unit * jnp.mean(f * unit, axis=-1, keepdims=True)
        )
        return (
            grad, jnp.sum(e * unit, axis=0, keepdims=True), jnp.sum(e, axis=0, keepdims=True)
        )

    def second_norm_back(r, second):
        e = sum_end(0, r, second)
        grad, of_gain, of_shift = norm_back(e, U2[r], I2[r], gain2)
        grad = grad + COT[r]
        GM[r] = grad
        low = grad.astype(BF)
        GB[r] = low
        for b in range(BLK_SIZE):
            zero = dot_nt(low, WO[192 * b : 192 * b + 64, :]).astype(BF)
            DA[r, b, 128:192, 0:64] = zero[0:64]
            DA[r, b, 128:192, 64:128] = zero[64:128]
            DA[r, b, 0:128] = dot_nt(low, WO[192 * b + 64 : 192 * (b + 1), :]).astype(BF)
        copies = swap_heads(DA, DR, r)
        VS[3:4] += of_gain
        VS[4:5] += of_shift
        VS[2:3] += jnp.sum(low.astype(F32), axis=0, keepdims=True)
        VS[5:6] += jnp.sum(COT[r].astype(BF).astype(F32), axis=0, keepdims=True)
        return copies

    def attend_back(r, h):
        if h:
            DOH[...] = DR[r, :, 0:128, 64 * (h - 1) : 64 * h].reshape(512, 64)
        else:
            for t in range(4):
                DOH[128 * t : 128 * t + 64] = DR[r, t, 128:192, 0:64]
                DOH[128 * t + 64 : 128 * (t + 1)] = DR[r, t, 128:192, 64:128]
        grad_out = DOH[...]
        delta = jnp.sum(grad_out.astype(F32) * OF[r, h], axis=-1, keepdims=True)
        grad_probs = dot_nt(grad_out, V[r, h])
        grad_scores = (PB[r, h].astype(F32) * (grad_probs - delta)).astype(BF)
        grads = (
            (dot_nn(grad_scores, K[r, h]) * 0.125).astype(BF),
            dot_tn(grad_scores, Q[r, h]).astype(BF),
            dot_tn(PB[r, h], grad_out).astype(BF),
        )
        for s, grad in enumerate(grads):
            if h == 0:
                GJ0[r, :, 64 * s : 64 * (s + 1)] = grad
            else:
                at = 128 * s + 64 * (h - 1)
                GJ1[r, :, at : at + 64] = grad

    def z_first_start(parts, landing):
        sems = group()
        for k in range(1, Z_SIZE):
            send(parts.at[z_at(k)], landing.at[k - 1], (2 * z_at(k) + y, blk), sems)
        later_sent((sems, landing))
        return sems, landing

    def z_first_middle(parts, landing, sums, recv, first):
        received(first)
        total = parts[z].astype(F32)
        for k in range(Z_SIZE - 1):
            total = total + landing[k].astype(F32)
        sums[...] = total.astype(BF)
        sems = group()
        send(sums.at[1 - y], recv, y_peer, sems)
        later_sent((sems, recv))
        return sems, recv

    def z_first_end(sums, recv, second):
        received(second)
        return sums[y].astype(F32) + recv[...].astype(F32)

    def output_grad_over_dp(second):
        received(second)
        GO2[...] = (
            GO[x, c].astype(F32) + RCo[x].astype(F32) + RXo[...].astype(F32)
        ).astype(BF).reshape(4, 2, 24, 768)
        return scatter_start(GO2, RYo)

    def vector_sums():
        for r in range(2):
            JBS[r, :, 0:192] = jnp.sum(GJ0[r].astype(F32), axis=0, keepdims=True)
            JBS[r, :, 192:576] = jnp.sum(GJ1[r].astype(F32), axis=0, keepdims=True)

    def first_norm_back(r, second):
        e = sum_end(2, r, second)
        grad, of_gain, of_shift = norm_back(e, U1[r], I1[r], gain1)
        GM[r] = GM[r] + grad
        VS[0:1] += of_gain
        VS[1:2] += of_shift

    VS[...] = jnp.zeros_like(VS)
    d_first, d_second, u_grad_first, u_grad_second = [], [], [], []

    def d_over_y(n):
        d_first.append(scatter_start(GD.at[n], RYd.at[n]))

    def d_over_z(n):
        d_second.append(scatter_middle(GD.at[n], RYd.at[n], Sd.at[n], RZd.at[n], d_first[n]))

    def u_over_y(n):
        u_grad_first.append(scatter_start(GU.at[n], RYu.at[n]))

    def u_over_z(n):
        u_grad_second.append(
            scatter_middle(GU.at[n], RYu.at[n], Su.at[n], RZu.at[n], u_grad_first[n])
        )

    up(0)
    gather_forward(n2_part[1])
    gather_end(gr_part[0])
    gather_end(gr_part[1])
    gather_end(n2_part[1])
    up(1)
    down_grad(0)
    d_near_first = z_first_start(GD.at[0], RZ0)
    d_first.append(None)
    d_second.append(None)
    down_grad(1)
    d_over_y(1)
    dp_end(d_part)
    hidden_back(0)
    second_first = [second_back(0)]
    down_grad(2)
    d_over_y(2)
    hidden_back(1)
    second_second = [sum_middle(0, 0, second_first[0])]
    second_first.append(second_back(1))
    up_grad(0)
    u_over_y(0)
    second_second.append(sum_middle(0, 1, second_first[1]))
    up_grad(1)
    u_over_y(1)
    d_over_z(1)
    up_grad(2)
    u_over_y(2)
    da_copies = [second_norm_back(0, second_second[0])]
    d_over_z(2)
    result_first = [down(0), down(1)]
    da_copies.append(second_norm_back(1, second_second[1]))
    o_first = output_grad()
    received(da_copies[0])
    attend_back(0, 1)
    o_second = output_grad_middle(o_first)
    attend_back(0, 2)
    d_near_second = z_first_middle(GD.at[0], RZ0, S0, RY0, d_near_first)
    u_over_z(0)
    received(da_copies[1])
    attend_back(1, 1)
    attend_back(1, 2)
    c_grad_first = joint_grad_two()
    u_over_z(1)
    attend_back(0, 0)
    first_first = [first_back(0)]
    attend_back(1, 0)
    a_grad_first = joint_grad_one()
    first_second = [sum_middle(2, 0, first_first[0])]
    u_over_z(2)
    first_first.append(first_back(1))
    o_grad_first = output_grad_over_dp(o_second)
    first_second.append(sum_middle(2, 1, first_first[1]))
    result_second = [sum_middle(1, 0, result_first[0])]
    vector_sums()

    def down_out():
        OD[:, 0:WIDE] = z_first_end(S0, RY0, d_near_second)
        for n in range(1, CHUNKS):
            OD[:, WIDE * n : WIDE * (n + 1)] = scatter_end(*d_second[n])

    row = lax.broadcasted_iota(jnp.int32, (8, 1), 0)

    def picked(values, mask, placer):
        wide = jnp.where(mask, values[None], 0.0)
        wide = wide.reshape(256, wide.shape[-1])
        high = wide.astype(BF)
        rest = (wide - high.astype(F32)).astype(BF)
        return dot_nt(high, placer) + dot_nt(rest, placer)

    def vectors_early():
        joint = JBS[0] + JBS[1]
        queries = jnp.concatenate([joint[:, 0:64], joint[:, 192:320]], axis=1)
        values = jnp.concatenate([joint[:, 128:192], joint[:, 448:576]], axis=1)
        pieces = picked(jnp.where(row == 7, UBS[0] + UBS[1], 0.0), mask96(), place96())
        pieces += picked(jnp.where(row == 6, queries, 0.0), mask48(0.0), place48())
        pieces += picked(jnp.where(row == 6, values, 0.0), mask48(16.0), place48())
        TS[...] = pieces

    def vectors_over_blk():
        pieces = (TS[...] + picked(VS[...], mask24(), place24())).reshape(8, 4, 8, 128)
        for b in range(BLK_SIZE):
            TB[b] = pieces[:, b]
        TL[blk] = TB[blk]
        return swap_parts(lambda b: TB.at[b], TL)

    def vectors_over_dp(first):
        received(first)
        TY[...] = (TL[0] + TL[1]) + (TL[2] + TL[3])
        sems = group()
        for k in range(1, DP_SIZE):
            to = (dp + k) % DP_SIZE
            send(TY.at[to], TV.at[k - 1], (to, blk), sems)
        later_sent((sems, TV))
        return sems, TV

    def vectors_end(first):
        received(first)
        OS[...] = TY[dp] + jnp.sum(TV[...], axis=0)

    def return_head_zero():
        total = scatter_end(*a_grad_second).astype(BF)
        for p in range(2):
            AAs[2 * p] = total[p][:, 0:192]
            AAs[2 * p + 1] = total[p][:, 192:384]
        AAr[blk] = AAs[blk]
        return swap_parts(lambda b: AAs.at[b], AAr)

    def up_out():
        for part in u_back:
            received(part)
        for b in range(BLK_SIZE):
            whole = jnp.concatenate([AUr[n, b] for n in range(CHUNKS)], axis=1).astype(F32)
            for i in range(DP_SIZE):
                at = 96 * (BLK_SIZE * i + b)
                OU[:, at : at + 96] = whole[:, 96 * i : 96 * (i + 1)]

    def joint_out():
        received(c_back)
        received(a_back)
        for b in range(BLK_SIZE):
            one, two = AAr[b].astype(F32), ACr[b].astype(F32)
            for s in range(3):
                at = 768 * s + 192 * b
                OJ[:, at : at + 64] = one[:, 64 * s : 64 * (s + 1)]
                OJ[:, at + 64 : at + 192] = two[:, 128 * s : 128 * (s + 1)]

    def result_end():
        for r in range(2):
            MID[r] = MID[r] + sum_end(1, r, result_second[r]) + dbias

    vectors_early()
    c_grad_second = scatter_middle(GC, RYc, Sc, RZc, c_grad_first)
    first_norm_back(0, first_second[0])
    a_grad_second = scatter_middle(GA, RYa, Sa, RZa, a_grad_first)
    first_norm_back(1, first_second[1])
    o_grad_second = scatter_middle(GO2, RYo, So, RZo, o_grad_first)
    vector_part = vectors_over_blk()
    u_back = [return_columns(u_grad_second[n], AUs.at[n], AUr.at[n]) for n in range(CHUNKS)]
    result_second.append(sum_middle(1, 1, result_first[1]))
    vector_part = vectors_over_dp(vector_part)
    c_back = return_columns(c_grad_second, ACs, ACr)
    down_out()
    a_back = return_head_zero()
    up_out()
    vectors_end(vector_part)
    OO[...] = scatter_end(*o_grad_second)
    result_end()
    joint_out()
    assert (count[0], count[2], count[1]) == (SENDS, RECEIVES, LOCALS), count
    for copies in started:
        sent(copies)

    @pl.when(inner)
    def _():
        for sems, _, five in started_over_z:
            sent((sems, five))

    @pl.when(jnp.logical_not(inner))
    def _():
        for sems, one, _ in started_over_z:
            sent((sems, one))


def finish_kernel(*refs):
    big_in, sums, big_out, small_out, sems = refs[:6], refs[6], refs[7:13], refs[13:21], refs[21]
    copies = []
    for n, (source, target) in enumerate(zip(big_in, big_out)):
        made = pltpu.make_async_copy(source, target, sems.at[n])
        made.start()
        copies.append(made)
    for row, width in enumerate(TILE_WIDTHS):
        small_out[row][...] = sums[row, 0:width]
    for made in copies:
        made.wait()


def fast_device(
    tokens, segment_ids, pad_mask, joint_weight, joint_bias, output_weight, output_bias,
    first_gain, first_shift, up_weight, up_bias, down_weight, down_bias,
    second_gain, second_shift, cotangent,
):
    vectors = (
        first_gain, first_shift, output_bias, second_gain, second_shift, down_bias,
        joint_bias, up_bias,
    )

    def vm(*shape, dtype=BF):
        return pltpu.VMEM(shape, dtype)

    def fm(*shape):
        return pltpu.VMEM(shape, F32)

    scratch = [
        fm(2, 128, 768), fm(2, 128, 768), vm(24, 2304), vm(24, 3072), vm(96, 768),
        vm(4, 24, 192), vm(4, 24, 384), vm(4, 24, 768), vm(CHUNKS, 4, 24, WIDE), vm(4, 24, 192), fm(8, 128), fm(8, 128), fm(8, 4, 8, 128),
        fm(4, 8, 128), fm(8, 512), fm(512, 8), fm(16, 768), fm(16, 192),
        vm(2, 4, 128, 768), vm(2, 4, 128, 768), vm(2, 4, 128, 768),
        vm(8, 2, 24, 384), vm(8, 4, 24, 384), vm(CHUNKS, 8, 4, 24, WIDE), vm(CHUNKS, 8, 96, WIDE),
        vm(4, 8, 24, 768), vm(768, 192), vm(768, 384), vm(CHUNKS, 768, WIDE), vm(768, 768),
        fm(2, 128, 768), fm(2, 128, 1), fm(2, 128, 768), fm(2, 128, 1),
        vm(2, 128, 768),
        vm(2, 3, 512, 64), vm(2, 3, 512, 64), vm(2, 3, 512, 64), vm(2, 3, 512, 512),
        fm(2, 3, 512, 64), vm(2, 4, 192, 128), vm(2, 4, 192, 128),
        vm(2, 4, 192, 128), vm(2, 4, 192, 128), vm(512, 64), vm(2, 512, 192), vm(2, 512, 384),
        vm(2, 512, 768), vm(2, 512, 768), vm(2, 512, 768), fm(2, 1, 768),
        vm(3, 2, 2, 2, 128, 768), vm(3, 2, 2, 128, 768), vm(3, 2, 128, 768), vm(3, 2, 128, 768),
        vm(CHUNKS, 4, 2, 96, WIDE), vm(CHUNKS, 4, 2, 4, 24, WIDE), vm(4, 2, 2, 24, 384), vm(4, 2, 4, 24, 384),
        vm(2, 2, 8, 24, 768), vm(4, 2, 24, 768),
        vm(CHUNKS, 4, 96, WIDE), vm(CHUNKS, 4, 4, 24, WIDE), vm(4, 2, 24, 384), vm(4, 4, 24, 384), vm(4, 24, 768),
        vm(CHUNKS, 4, 96, WIDE), vm(CHUNKS, 4, 4, 24, WIDE), vm(4, 2, 24, 384), vm(4, 4, 24, 384), vm(4, 24, 768),
        vm(CHUNKS, 3, 96, WIDE), vm(CHUNKS, 3, 4, 24, WIDE), vm(3, 2, 24, 384), vm(3, 4, 24, 384), vm(3, 24, 768),
        vm(3, 2, 96, WIDE), vm(2, 96, WIDE), vm(96, WIDE),
        vm(CHUNKS, 4, 24, WIDE), vm(CHUNKS, 4, 24, WIDE), vm(4, 24, 192), vm(4, 24, 192),
        vm(4, 24, 384), vm(4, 24, 384), vm(2, 8, 24, 768), vm(8, 24, 768), vm(8, 24, 768),
        fm(256, 128), fm(4, 8, 8, 128), fm(4, 8, 8, 128), fm(8, 8, 128), fm(7, 8, 128),
        fm(8, 768), fm(2, 1, 576),
        pltpu.SemaphoreType.DMA((SENDS,)), pltpu.SemaphoreType.DMA((RECEIVES,)),
        pltpu.SemaphoreType.DMA((LOCALS,)),
    ]
    vmem = pl.BlockSpec(memory_space=pltpu.VMEM)
    anywhere = pl.BlockSpec(memory_space=pl.ANY)
    big = [(2, 128, 768), (2, 128, 768), (24, 2304), (24, 768), (24, 3072), (96, 768)]
    made = pl.pallas_call(
        layer_kernel,
        out_shape=[fm(*shape) for shape in big] + [fm(8, 128)],
        in_specs=[anywhere] * 2 + [vmem] * 2 + [anywhere] * 4 + [vmem] * 8,
        out_specs=[vmem] * 7,
        scratch_shapes=scratch,
        compiler_params=pltpu.CompilerParams(
            collective_id=0, has_side_effects=True, vmem_limit_bytes=VMEM_MIB * 2**20
        ),
        cost_estimate=pl.CostEstimate(
            flops=13 * 10**9, bytes_accessed=6 * 10**6, transcendentals=4 * 10**6
        ),
    )(
        tokens, cotangent, segment_ids, pad_mask, joint_weight, up_weight, down_weight,
        output_weight, *vectors,
    )
    ends = pl.pallas_call(
        finish_kernel,
        out_shape=[jax.ShapeDtypeStruct(shape, F32) for shape in big]
        + [jax.ShapeDtypeStruct((width,), F32) for width in TILE_WIDTHS],
        in_specs=[vmem] * 7,
        out_specs=[anywhere] * 6 + [vmem] * 8,
        scratch_shapes=[pltpu.SemaphoreType.DMA((6,))],
    )(*(pltpu.with_memory_space_constraint(array, pltpu.VMEM) for array in made))
    result, grad_tokens, grad_j, grad_o, grad_u, grad_d = ends[:6]
    first_g, first_s, output_b, second_g, second_s, down_b, joint_b, up_b = ends[6:]
    return (
        result, grad_tokens, grad_j, joint_b, grad_o, output_b, first_g, first_s,
        grad_u, up_b, grad_d, down_b, second_g, second_s,
    )


def solution(mesh):
    placed = (
        P("dp", "blk", None),
        P("dp", "blk"),
        P("dp", "blk"),
        P(("dp", "blk"), None),
        P(("dp", "blk")),
        P(("dp", "blk"), None),
        P(("dp", "blk")),
        P(("dp", "blk")),
        P(("dp", "blk")),
        P(("dp", "blk"), None),
        P(("dp", "blk")),
        P(("dp", "blk"), None),
        P(("dp", "blk")),
        P(("dp", "blk")),
        P(("dp", "blk")),
        P("dp", "blk", None),
    )

    def spread(device_part):
        return jax.shard_map(
            device_part,
            mesh=mesh,
            in_specs=placed,
            out_specs=(
                P("dp", "blk", None),
                P("dp", "blk", None),
                P(("dp", "blk"), None),
                P(("dp", "blk")),
                P(("dp", "blk"), None),
                P(("dp", "blk")),
                P(("dp", "blk")),
                P(("dp", "blk")),
                P(("dp", "blk"), None),
                P(("dp", "blk")),
                P(("dp", "blk"), None),
                P(("dp", "blk")),
                P(("dp", "blk")),
                P(("dp", "blk")),
            ),
            check_vma=False,
        )

    def layer(*arrays):
        rows, length, features = arrays[0].shape
        shape = dict(mesh.shape)
        fits = (
            shape == {"dp": DP_SIZE, "blk": BLK_SIZE}
            and (rows, length, features) == (2 * shape["dp"], 512, 768)
            and arrays[9].shape[1] == 3072
        )
        return spread(fast_device if fits else per_device)(*arrays)

    return layer
```

```python
import jax
import jax.numpy as jnp
from jax import lax
from jax.experimental import pallas as pl
from jax.experimental.pallas import tpu as pltpu
from jax.sharding import PartitionSpec as P

HEADS = 12
SENDS, RECEIVES, LOCALS = 74, 92, 6
VMEM_MIB = 58


epsilon = 1e-05
masked_score = -1e30


def normalize(values_in, gain, shift):
    centered = values_in - jnp.mean(values_in, axis=-1, keepdims=True)
    inverse = lax.rsqrt(jnp.mean(centered * centered, axis=-1, keepdims=True) + epsilon)
    unit_rows = centered * inverse
    return (unit_rows * gain + shift, unit_rows, inverse)


def normalize_back(grad_normed, unit_rows, inverse, gain):
    scaled = grad_normed * gain
    grad_input = inverse * (
        scaled
        - jnp.mean(scaled, axis=-1, keepdims=True)
        - unit_rows * jnp.mean(scaled * unit_rows, axis=-1, keepdims=True)
    )
    return (
        grad_input,
        jnp.sum(grad_normed * unit_rows, axis=(0, 1)),
        jnp.sum(grad_normed, axis=(0, 1)),
    )


def project(activation, weight):
    return jnp.einsum("rcd,dn->rcn", activation, weight, preferred_element_type=jnp.float32)


def project_back(gradient, weight):
    return jnp.einsum("rcn,dn->rcd", gradient, weight, preferred_element_type=jnp.float32)


def outer_sum(activation, gradient):
    return jnp.einsum("rcd,rcn->dn", activation, gradient, preferred_element_type=jnp.float32)


def split_heads(matrix, head_count):
    return matrix.reshape(
        matrix.shape[0], matrix.shape[1], head_count, matrix.shape[2] // head_count
    )


def masked_scores(query_heads, key_heads, query_segment, key_segment, scaling):
    raw_scores = (
        jnp.einsum("rqhd,rkhd->rhqk", query_heads, key_heads, preferred_element_type=jnp.float32)
        * scaling
    )
    allowed = (query_segment[:, :, None] == key_segment[:, None, :])[:, None]
    return (jnp.where(allowed, raw_scores, masked_score), allowed)


def column_sums(gradient):
    return jnp.sum(gradient.astype(jnp.float32), axis=(0, 1))


def scatter_sum(gradient):
    summed = lax.psum_scatter(
        gradient.astype(jnp.bfloat16), ("dp", "blk"), scatter_dimension=0, tiled=True
    )
    return summed.astype(jnp.float32)


def per_device(
    tokens,
    segment_ids,
    pad_mask,
    joint_weight,
    joint_bias,
    output_weight,
    output_bias,
    first_gain,
    first_shift,
    up_weight,
    up_bias,
    down_weight,
    down_bias,
    second_gain,
    second_shift,
    cotangent,
):
    batch_rows, local_len, features = tokens.shape
    head_count = HEADS
    head_size = features // head_count
    scaling = head_size ** (-0.5)
    device_count = lax.axis_size("dp") * lax.axis_size("blk")
    small_parts = (
        joint_bias, output_bias, first_gain, first_shift, up_bias, down_bias, second_gain, second_shift
    )
    small_all = lax.all_gather(jnp.concatenate(small_parts), ("dp", "blk"), axis=0, tiled=True)
    small_all = small_all.reshape(device_count, -1)
    small_full = []
    small_at = 0
    for part in small_parts:
        small_full.append(small_all[:, small_at : small_at + part.shape[0]].reshape(-1))
        small_at += part.shape[0]
    full_joint_bias, full_output_bias, gain_one, shift_one = small_full[:4]
    full_up_bias, full_down_bias, gain_two, shift_two = small_full[4:]
    full_joint = lax.all_gather(joint_weight, ("dp", "blk"), axis=0, tiled=True)
    full_output = lax.all_gather(output_weight, ("dp", "blk"), axis=0, tiled=True)
    normed_one, unit_one, inverse_one = normalize(
        tokens, gain_one.astype(jnp.float32), shift_one.astype(jnp.float32)
    )
    normed_one_low = normed_one.astype(jnp.bfloat16)
    joint = project(normed_one_low, full_joint)
    bias_values = full_joint_bias.astype(jnp.float32)
    query = (joint[..., :features] + bias_values[:features]).astype(jnp.bfloat16)
    keys = joint[..., features : 2 * features].astype(jnp.bfloat16)
    values = (joint[..., 2 * features :] + bias_values[features:]).astype(jnp.bfloat16)
    key_segment = jnp.where(pad_mask == 1, segment_ids, -1)
    query_heads = split_heads(query, head_count)
    top_score = jnp.full((batch_rows, head_count, local_len), masked_score, jnp.float32)
    key_portion = lax.all_gather(keys, "blk", axis=1, tiled=True)
    value_portion = lax.all_gather(values, "blk", axis=1, tiled=True)
    segment_portion = lax.all_gather(key_segment, "blk", axis=1, tiled=True)
    scores, allowed = masked_scores(
        query_heads, split_heads(key_portion, head_count), segment_ids, segment_portion, scaling
    )
    new_top = jnp.maximum(top_score, jnp.max(scores, axis=-1))
    weights = jnp.where(allowed, jnp.exp(scores - new_top[..., None]), 0.0)
    total_weight = jnp.sum(weights, axis=-1)
    weighted = jnp.einsum(
        "rhqk,rkhd->rhqd",
        weights.astype(jnp.bfloat16),
        split_heads(value_portion, head_count),
        preferred_element_type=jnp.float32,
    )
    top_score, total_weight, weighted = (new_top, total_weight, weighted)
    log_total = top_score + jnp.log(total_weight)
    attended_heads = weighted / total_weight[..., None]
    attended = jnp.transpose(attended_heads, (0, 2, 1, 3)).reshape(batch_rows, local_len, features)
    attended_low = attended.astype(jnp.bfloat16)
    middle = tokens + project(attended_low, full_output) + full_output_bias.astype(jnp.float32)
    full_up = lax.all_gather(up_weight, ("dp", "blk"), axis=0, tiled=True)
    full_down = lax.all_gather(down_weight, ("dp", "blk"), axis=0, tiled=True)
    normed_two, unit_two, inverse_two = normalize(
        middle, gain_two.astype(jnp.float32), shift_two.astype(jnp.float32)
    )
    normed_two_low = normed_two.astype(jnp.bfloat16)
    hidden = project(normed_two_low, full_up) + full_up_bias.astype(jnp.float32)
    activated, gelu_pullback = jax.vjp(jax.nn.gelu, hidden)
    activated_low = activated.astype(jnp.bfloat16)
    result = middle + project(activated_low, full_down) + full_down_bias.astype(jnp.float32)
    later_up, later_down, later_gain_two = full_up, full_down, gain_two
    grad_result = cotangent.astype(jnp.bfloat16)
    grad_down_weight = outer_sum(activated_low, grad_result)
    grad_down_bias = column_sums(grad_result)
    grad_activated = project_back(grad_result, later_down)
    grad_hidden = gelu_pullback(grad_activated)[0].astype(jnp.bfloat16)
    grad_up_bias = column_sums(grad_hidden)
    grad_up_weight = outer_sum(normed_two_low, grad_hidden)
    grad_normed_two = project_back(grad_hidden, later_up)
    grad_from_second, grad_gain_two, grad_shift_two = normalize_back(
        grad_normed_two, unit_two, inverse_two, later_gain_two.astype(jnp.float32)
    )
    grad_middle = cotangent + grad_from_second
    grad_up_shard = scatter_sum(grad_up_weight)
    grad_down_shard = scatter_sum(grad_down_weight)
    later_joint, later_output, later_gain_one = full_joint, full_output, gain_one
    grad_branch = grad_middle.astype(jnp.bfloat16)
    grad_output_weight = outer_sum(attended_low, grad_branch)
    grad_output_bias = column_sums(grad_branch)
    grad_attended = project_back(grad_branch, later_output).astype(jnp.bfloat16)
    grad_heads = split_heads(grad_attended, head_count)
    delta = jnp.einsum("rqhd,rhqd->rhq", grad_heads.astype(jnp.float32), attended_heads)
    key_heads = split_heads(key_portion, head_count)
    scores, allowed = masked_scores(query_heads, key_heads, segment_ids, segment_portion, scaling)
    probs = jnp.where(allowed, jnp.exp(scores - log_total[..., None]), 0.0)
    grad_probs = jnp.einsum(
        "rqhd,rkhd->rhqk",
        grad_heads,
        split_heads(value_portion, head_count),
        preferred_element_type=jnp.float32,
    )
    grad_scores = (probs * (grad_probs - delta[..., None])).astype(jnp.bfloat16)
    grad_query = scaling * jnp.einsum(
        "rhqk,rkhd->rqhd", grad_scores, key_heads, preferred_element_type=jnp.float32
    )
    every_total, every_delta = (
        lax.all_gather(log_total, "blk", axis=2, tiled=True),
        lax.all_gather(delta, "blk", axis=2, tiled=True),
    )
    own_keys = split_heads(keys, head_count)
    own_values = split_heads(values, head_count)
    query_portion = lax.all_gather(query, "blk", axis=1, tiled=True)
    grad_portion = lax.all_gather(grad_attended, "blk", axis=1, tiled=True)
    segment_portion = lax.all_gather(segment_ids, "blk", axis=1, tiled=True)
    portion_queries = split_heads(query_portion, head_count)
    portion_grads = split_heads(grad_portion, head_count)
    scores, allowed = masked_scores(
        portion_queries, own_keys, segment_portion, key_segment, scaling
    )
    probs = jnp.where(allowed, jnp.exp(scores - every_total[..., None]), 0.0)
    grad_values = jnp.einsum(
        "rhqk,rqhd->rkhd",
        probs.astype(jnp.bfloat16),
        portion_grads,
        preferred_element_type=jnp.float32,
    )
    grad_probs = jnp.einsum(
        "rqhd,rkhd->rhqk", portion_grads, own_values, preferred_element_type=jnp.float32
    )
    grad_scores = (probs * (grad_probs - every_delta[..., None])).astype(jnp.bfloat16)
    grad_keys = scaling * jnp.einsum(
        "rhqk,rqhd->rkhd", grad_scores, portion_queries, preferred_element_type=jnp.float32
    )
    grad_keys, grad_values = (grad_keys, grad_values)
    grad_joint = jnp.concatenate(
        [
            grad_query.reshape(batch_rows, local_len, features),
            grad_keys.reshape(batch_rows, local_len, features),
            grad_values.reshape(batch_rows, local_len, features),
        ],
        axis=-1,
    ).astype(jnp.bfloat16)
    grad_joint_weight = outer_sum(normed_one_low, grad_joint)
    grad_joint_bias = jnp.concatenate(
        [column_sums(grad_joint[..., :features]), column_sums(grad_joint[..., 2 * features :])]
    )
    grad_normed_one = project_back(grad_joint, later_joint)
    grad_from_first, grad_gain_one, grad_shift_one = normalize_back(
        grad_normed_one, unit_one, inverse_one, later_gain_one.astype(jnp.float32)
    )
    grad_tokens = grad_middle + grad_from_first
    small_grads = (
        grad_joint_bias, grad_output_bias, grad_gain_one, grad_shift_one,
        grad_up_bias, grad_down_bias, grad_gain_two, grad_shift_two,
    )
    packed = jnp.concatenate([part.reshape(device_count, -1) for part in small_grads], axis=1)
    own = lax.psum_scatter(packed, ("dp", "blk"), scatter_dimension=0, tiled=True)[0]
    small_shards = []
    small_at = 0
    for part in small_parts:
        small_shards.append(own[small_at : small_at + part.shape[0]])
        small_at += part.shape[0]
    return (
        result,
        grad_tokens,
        scatter_sum(grad_joint_weight),
        small_shards[0],
        scatter_sum(grad_output_weight),
        small_shards[1],
        small_shards[2],
        small_shards[3],
        grad_up_shard,
        small_shards[4],
        grad_down_shard,
        small_shards[5],
        small_shards[6],
        small_shards[7],
    )


Z_SIZE, Y_SIZE, BLK_SIZE = 4, 2, 4
DP_SIZE = Z_SIZE * Y_SIZE
MESH = pl.DeviceIdType.MESH
BF = jnp.bfloat16
F32 = jnp.float32
WIDE, CHUNKS = 256, 3
TILE_WIDTHS = (24, 24, 24, 24, 24, 24, 48, 96)


def dot_nn(left, right):
    return lax.dot_general(left, right, (((1,), (0,)), ((), ())), preferred_element_type=F32)


def dot_nt(left, right):
    return lax.dot_general(left, right, (((1,), (1,)), ((), ())), preferred_element_type=F32)


def dot_tn(left, right):
    return lax.dot_general(left, right, (((0,), (0,)), ((), ())), preferred_element_type=F32)


def lane_pieces(lanes, width):
    lane = lax.broadcasted_iota(jnp.int32, (1, lanes), 1).astype(F32)
    piece = jnp.floor((lane + 0.5) * (1.0 / width))
    return piece, lane - width * piece


def piece_placer(lanes, width):
    place = lax.broadcasted_iota(jnp.int32, (128, lanes), 0).astype(F32)
    _, within = lane_pieces(lanes, width)
    return jnp.where(place == within, 1.0, 0.0).astype(BF)


def layer_kernel(*refs):
    ins, outs, scr = refs[:16], refs[16:23], refs[23:]
    (tok_in, cot_in, seg_in, pad_in, jw_in, uw_in, dw_in, ow_in), vectors = ins[:8], ins[8:]
    MID, GM, OJ, OO, OU, OD, OS = outs
    (
        TOK, COT, JW, UW, DW, JP0, JP1, UPW, UP, AP, TILE, SEGT, G, SEG, KSEG, QSEG, PV, QVB,
        N1, N2, GR, WJS0, WJS1, WUS, WDS, WOS, WJ0, WJ1, WU, WO,
        U1, I1, U2, I2, GB,
        Q, K, V, PB, OF, AT, AR, DA, DR, DOH, GJ0, GJ1,
        GP, ACT, GH, UBS, PT, RC, SX, RX,
        GD, GU, GA, GC, GO, GO2, RYd, RYu, RYa, RYc, RYo, Sd, Su, Sa, Sc, So,
        RZd, RZu, RZa, RZc, RZo, RZ0, S0, RY0, AUs, AUr, AAs, AAr, ACs, ACr, RCo, SXo, RXo,
        TS, TB, TL, TY, TV, VS, JBS, ssem, rsem, lsem,
    ) = scr
    dp = lax.axis_index("dp")
    blk = lax.axis_index("blk")
    z, y = dp // 2, dp % 2
    x, c = blk // 2, blk % 2
    count = [0, 0, 0]
    started = []

    def local(src, dst):
        n = count[1]
        count[1] += 1
        made = pltpu.make_async_copy(src, dst, lsem.at[n])
        made.start()
        return made

    def to_send():
        n = count[0]
        count[0] += 1
        return ssem.at[n]

    def to_receive():
        n = count[2]
        count[2] += 1
        return rsem.at[n]

    def group():
        return to_send(), to_receive()

    def send(src, dst, dev, sems):
        made = pltpu.make_async_remote_copy(
            src_ref=src, dst_ref=dst, send_sem=sems[0], recv_sem=sems[1],
            device_id=dev, device_id_type=MESH,
        )
        made.start()
        return made

    def wait_bytes(sem, ref):
        pltpu.make_async_copy(ref, ref, sem).wait()

    def received(copies):
        wait_bytes(copies[0][1], copies[1])

    def later_sent(copies):
        started.append(copies)

    def sent(copies):
        wait_bytes(copies[0][0], copies[1])

    started_over_z = []

    def later_sent_over_z(copies):
        started_over_z.append(copies)

    core_peer = (dp, 2 * x + 1 - c)
    x_peer = (dp, 2 * (1 - x) + c)
    far_peer = (dp, 2 * (1 - x) + 1 - c)
    blk_peers = (x_peer, far_peer, core_peer)
    y_peer = (2 * z + 1 - y, blk)
    inner = (z == 1) | (z == 2)
    z_left = (2 * ((z + Z_SIZE - 1) % Z_SIZE) + y, blk)
    z_right = (2 * ((z + 1) % Z_SIZE) + y, blk)
    z_side = (2 * ((z // 2) * 2 + 1 - z % 2) + y, blk)
    z_across = (2 * (Z_SIZE - 1 - z) + y, blk)

    def z_at(k):
        return (z + k) % Z_SIZE

    ow_copy = local(ow_in, WOS.at[blk, dp])
    jw_copy = local(jw_in, JW)
    tok_copy = local(tok_in, TOK)
    uw_copy = local(uw_in, UW)
    dw_copy = local(dw_in, DW)
    cot_copy = local(cot_in, COT)

    partners = [(dp, (blk + j) % BLK_SIZE) for j in range(1, BLK_SIZE)]
    partners += [((dp + i) % DP_SIZE, blk) for i in range(1, DP_SIZE)]

    def entry_barrier():
        barrier = pltpu.get_barrier_semaphore()
        near = list(blk_peers) + [y_peer]
        for dev in near:
            pl.semaphore_signal(barrier, inc=1, device_id=dev, device_id_type=MESH)

        @pl.when(z > 0)
        def _():
            pl.semaphore_signal(barrier, inc=1, device_id=z_left, device_id_type=MESH)

        @pl.when(z < Z_SIZE - 1)
        def _():
            pl.semaphore_signal(barrier, inc=1, device_id=z_right, device_id_type=MESH)

        @pl.when(inner)
        def _():
            pl.semaphore_wait(barrier, 6)

        @pl.when(jnp.logical_not(inner))
        def _():
            pl.semaphore_wait(barrier, 5)

    def swap_parts(parts, landing, chunked=False):
        sems = group()
        for dev in blk_peers:
            send(parts(dev[1]), landing.at[:, blk] if chunked else landing.at[blk], dev, sems)
        span = landing.at[:, pl.ds(c, 3)] if chunked else landing.at[pl.ds(c, 3)]
        later_sent((sems, span))
        return sems, span

    def small_tiles():
        TILE[...] = jnp.zeros_like(TILE)
        for row, (ref, width) in enumerate(zip(vectors, TILE_WIDTHS)):
            TILE[row : row + 1, 0:width] = ref[...].astype(F32).reshape(1, width)
        segment = seg_in[...].astype(F32)
        SEGT[...] = jnp.zeros_like(SEGT)
        SEGT[0:2] = segment
        SEGT[2:4] = jnp.where(pad_in[...] == 1, segment, -1.0)
        G[dp, blk] = TILE[...]
        SEG[blk] = SEGT[...]


    small_tiles()
    entry_barrier()

    def stats(values):
        mean = jnp.mean(values, axis=-1, keepdims=True)
        centered = values - mean
        inverse = lax.rsqrt(jnp.mean(centered * centered, axis=-1, keepdims=True) + epsilon)
        return centered * inverse, inverse

    def dp_part(slab, span):
        return slab, span, [group(), group()] + [(None, to_receive()) for _ in range(3)]

    def slabs_part(slabs):
        return dp_part(lambda i: slabs.at[i], lambda n: slabs.at[pl.ds(c, n)])

    def own_over_y(part):
        slab, span, sems = part
        send(slab(dp), slab(dp), y_peer, sems[0])
        later_sent((sems[0], span(4)))

    def own_over_z(part):
        slab, span, sems = part

        @pl.when(z < Z_SIZE - 1)
        def _():
            send(slab(dp), slab(dp), z_right, (sems[1][0], sems[1][1]))

        @pl.when(z > 0)
        def _():
            send(slab(dp), slab(dp), z_left, (sems[1][0], sems[2][1]))

        later_sent_over_z((sems[1], span(1), span(5)))

    def pass_on(part, there, arrived, onward, more, dev):
        slab, _, sems = part
        received((arrived, slab(there)))
        send(slab(there), slab(there), y_peer, sems[0])
        if onward is not None:

            @pl.when(more)
            def _():
                send(slab(there), slab(there), dev, (sems[1][0], onward[1]))

    def step_one(part):
        sems = part[2]

        @pl.when(z > 0)
        def _():
            pass_on(part, dp - 2, sems[1], sems[3], z < Z_SIZE - 1, z_right)

        @pl.when(z < Z_SIZE - 1)
        def _():
            pass_on(part, dp + 2, sems[2], sems[3], z > 0, z_left)

    def step_two(part):
        sems = part[2]

        @pl.when(z >= 2)
        def _():
            pass_on(part, dp - 4, sems[3], sems[4], z == 2, z_right)

        @pl.when(z < 2)
        def _():
            pass_on(part, dp + 4, sems[3], sems[4], z == 1, z_left)

    def step_three(part):
        sems = part[2]

        @pl.when(z == Z_SIZE - 1)
        def _():
            pass_on(part, dp - 6, sems[4], None, None, None)

        @pl.when(z == 0)
        def _():
            pass_on(part, dp + 6, sems[4], None, None, None)

    def dp_end(part):
        _, span, sems = part
        received((sems[0], span(4)))

    def gather_start(buf, r):
        over_x, to_core = group(), group()
        send(buf.at[r, blk], buf.at[r, blk], x_peer, over_x)
        send(buf.at[r, blk], buf.at[r, blk], core_peer, to_core)
        later_sent((over_x, buf.at[r, blk]))
        later_sent((to_core, buf.at[r, pl.ds(c, 2)]))
        return buf, r, over_x, to_core

    def gather_forward(part):
        buf, r, over_x, to_core = part
        received((over_x, buf.at[r, x_peer[1]]))
        send(buf.at[r, x_peer[1]], buf.at[r, x_peer[1]], core_peer, to_core)

    def gather_end(part):
        buf, r, _, to_core = part
        received((to_core, buf.at[r, pl.ds(c, 2)]))

    ow_copy.wait()
    o_part = dp_part(lambda i: WOS.at[blk, i], lambda n: WOS.at[blk, pl.ds(c, n)])
    a_part, c_part, g_part = slabs_part(WJS0), slabs_part(WJS1), slabs_part(G)

    def chunks_part(slabs):
        return dp_part(lambda i: slabs.at[:, i], lambda n: slabs.at[:, pl.ds(c, n)])

    u_part, d_part = chunks_part(WUS), chunks_part(WDS)
    own_over_z(o_part)
    own_over_y(o_part)

    def split_joint():
        jw_copy.wait()
        for b in range(BLK_SIZE):
            for s in range(3):
                at = 768 * s + 192 * b
                JP0[b, :, 64 * s : 64 * (s + 1)] = JW[:, at : at + 64]
                JP1[b, :, 128 * s : 128 * (s + 1)] = JW[:, at + 64 : at + 192]

    def swap_columns(parts, slabs):
        slabs[dp, blk] = parts[blk]
        return swap_parts(lambda b: parts.at[b], slabs.at[dp])

    split_joint()
    AP[blk] = JP0[blk]
    a_first = swap_parts(lambda b: JP0.at[b], AP)
    g_first = swap_parts(lambda b: TILE, G.at[dp])
    c_first = swap_columns(JP1, WJS1)
    seg_copies = swap_parts(lambda b: SEGT, SEG)

    def first_stats():
        tok_copy.wait()
        firsts = []
        for r in range(2):
            unit, inverse = stats(TOK[r])
            U1[r] = unit
            I1[r] = inverse
            N1[r, blk] = unit.astype(BF)
            firsts.append(gather_start(N1, r))
        return firsts

    n1_part = first_stats()
    n1_sent = (started[-4:-2], started[-2:])
    del started[-4:]

    def split_up():
        uw_copy.wait()
        for i in range(DP_SIZE):
            for b in range(BLK_SIZE):
                at = 96 * (BLK_SIZE * i + b)
                UPW[b, :, 96 * i : 96 * (i + 1)] = UW[:, at : at + 96]
        for n in range(CHUNKS):
            for b in range(BLK_SIZE):
                UP[n, b] = UPW[b, :, WIDE * n : WIDE * (n + 1)]

    def split_down():
        dw_copy.wait()
        for n in range(CHUNKS):
            WDS[n, dp] = DW[:, WIDE * n : WIDE * (n + 1)]

    def early_down():
        split_down()
        own_over_y(d_part)

    def low_cotangent():
        cot_copy.wait()
        for r in range(2):
            GR[r, blk] = COT[r].astype(BF)

    early_down()
    received(a_first)
    for p in range(2):
        WJS0[dp, p, :, 0:192] = AP[2 * p]
        WJS0[dp, p, :, 192:384] = AP[2 * p + 1]
    own_over_z(a_part)
    own_over_y(a_part)
    received(g_first)
    own_over_z(g_part)
    own_over_y(g_part)
    received(c_first)
    own_over_z(c_part)
    own_over_y(c_part)
    split_up()
    WUS[:, dp, blk] = UP[:, blk]
    u_first = swap_parts(lambda b: UP.at[:, b], WUS.at[:, dp], True)
    low_cotangent()
    gr_part = [gather_start(GR, r) for r in range(2)]
    step_one(a_part)
    step_one(g_part)
    step_one(o_part)
    step_two(a_part)
    step_two(g_part)
    step_two(o_part)
    gather_forward(n1_part[0])
    step_one(c_part)
    step_three(a_part)
    step_three(g_part)
    step_three(o_part)
    step_two(c_part)
    received(u_first)
    own_over_z(u_part)
    own_over_z(d_part)
    gather_forward(n1_part[1])
    dev_id = lax.broadcasted_iota(jnp.int32, (32, 1, 1), 0).astype(F32)
    blk_f = blk.astype(F32)
    piece24, _ = lane_pieces(768, 24)
    piece48, _ = lane_pieces(192, 48)
    piece96, _ = lane_pieces(768, 96)

    def mask24():
        return piece24[None] == dev_id

    def mask48(first_dev):
        return piece48[None] + (4.0 * blk_f + first_dev) == dev_id

    def mask96():
        return 4.0 * piece96[None] + blk_f == dev_id

    def place24():
        return piece_placer(768, 24)

    def place48():
        return piece_placer(192, 48)

    def place96():
        return piece_placer(768, 96)

    def small_end():
        dp_end(g_part)
        tiles = G[...].reshape(32 * 8, 128).astype(BF)

        def placed(placer, mask, lanes):
            spread = dot_nn(tiles, placer).reshape(32, 8, lanes)
            return jnp.sum(jnp.where(mask, spread, 0.0), axis=0)

        PV[0:8] = placed(place24(), mask24(), 768)
        PV[8:16] = placed(place96(), mask96(), 768)
        QVB[0:8] = placed(place48(), mask48(0.0), 192)
        QVB[8:16] = placed(place48(), mask48(16.0), 192)

    def segments_end():
        received(seg_copies)
        eye = jnp.where(
            lax.broadcasted_iota(jnp.int32, (128, 128), 0)
            == lax.broadcasted_iota(jnp.int32, (128, 128), 1), 1.0, 0.0,
        ).astype(BF)
        for b in range(BLK_SIZE):
            part = SEG[b]
            KSEG[:, 128 * b : 128 * (b + 1)] = part
            QSEG[128 * b : 128 * (b + 1)] = dot_nt(eye, part.astype(BF))


    segments_end()
    small_end()
    gain1, shift1, obias = PV[0:1], PV[1:2], PV[2:3]
    gain2, shift2, dbias = PV[3:4], PV[4:5], PV[5:6]

    def compact(slabs, whole):
        for i in range(DP_SIZE):
            rows = slabs(i).astype(F32)
            rows = rows.reshape(96, rows.shape[-1])
            whole[96 * i : 96 * (i + 1), :] = rows.astype(BF)

    def norm_rows(r):
        gather_end(n1_part[r])
        for copies in n1_sent[r]:
            sent(copies)
        for b in range(BLK_SIZE):
            N1[r, b] = (N1[r, b].astype(F32) * gain1 + shift1).astype(BF)

    def qkv_one(r):
        joint = dot_nn(N1[r].reshape(512, 768), WJ0[...])
        qbias, vbias = QVB[6:7, 0:64], QVB[14:15, 0:64]
        Q[r, 0] = ((joint[:, :64] + qbias).astype(BF).astype(F32) * 0.125).astype(BF)
        K[r, 0] = joint[:, 64:128].astype(BF)
        V[r, 0] = (joint[:, 128:] + vbias).astype(BF)

    def qkv_two(r):
        joint = dot_nn(N1[r].reshape(512, 768), WJ1[...])
        qbias, vbias = QVB[6:7, 64:192], QVB[14:15, 64:192]
        query = ((joint[:, :128] + qbias).astype(BF).astype(F32) * 0.125).astype(BF)
        keys = joint[:, 128:256].astype(BF)
        values = (joint[:, 256:] + vbias).astype(BF)
        for h in (1, 2):
            lanes = slice(64 * (h - 1), 64 * h)
            Q[r, h] = query[:, lanes]
            K[r, h] = keys[:, lanes]
            V[r, h] = values[:, lanes]

    def attend(r, h):
        scores = dot_nt(Q[r, h], K[r, h])
        scores = jnp.where(QSEG[:, r : r + 1] == KSEG[2 + r : 3 + r, :], scores, masked_score)
        top = jnp.max(scores, axis=-1, keepdims=True)
        expos = jnp.exp(scores - top)
        total = jnp.sum(expos, axis=-1, keepdims=True)
        probs = (expos * (1.0 / total)).astype(BF)
        PB[r, h] = probs
        out = dot_nn(probs, V[r, h])
        OF[r, h] = out
        if h:
            AT[r, :, 0:128, 64 * (h - 1) : 64 * h] = out.astype(BF).reshape(4, 128, 64)
        else:
            halves = out.astype(BF).reshape(4, 2, 64, 64)
            AT[r, :, 128:192, 0:64] = halves[:, 0]
            AT[r, :, 128:192, 64:128] = halves[:, 1]

    def swap_heads(src, dst, r):
        dst[r, blk] = src[r, blk]
        return swap_parts(lambda b: src.at[r, b], dst.at[r])

    dp_end(a_part)
    for i in range(DP_SIZE):
        pairs = WJS0[i].astype(F32)
        rows = [pairs[p][:, 192 * s : 192 * (s + 1)] for p in range(2) for s in range(2)]
        WJ0[96 * i : 96 * (i + 1), :] = jnp.concatenate(rows, axis=0).astype(BF)
    dp_end(o_part)
    wo_x, wo_core = group(), group()
    send(WOS.at[blk], WOS.at[blk], x_peer, wo_x)
    send(WOS.at[blk], WOS.at[blk], core_peer, wo_core)
    later_sent((wo_x, WOS.at[blk]))
    later_sent((wo_core, WOS.at[pl.ds(c, 2)]))
    norm_rows(0)
    qkv_one(0)
    step_three(c_part)
    attend(0, 0)
    own_over_y(u_part)
    norm_rows(1)
    qkv_one(1)
    attend(1, 0)
    step_one(u_part)
    dp_end(c_part)
    compact(lambda i: WJS1[i], WJ1)
    qkv_two(0)
    attend(0, 1)
    attend(0, 2)
    at_copies = [swap_heads(AT, AR, 0)]
    gather_forward(gr_part[0])
    qkv_two(1)
    step_two(u_part)
    attend(1, 1)
    step_one(d_part)
    attend(1, 2)
    at_copies.append(swap_heads(AT, AR, 1))
    received((wo_x, WOS.at[x_peer[1]]))
    send(WOS.at[x_peer[1]], WOS.at[x_peer[1]], core_peer, wo_core)
    received((wo_core, WOS.at[pl.ds(c, 2)]))
    compact(lambda i: WOS[:, i], WO)

    def head_zero(block):
        packed = block[128:192]
        return jnp.concatenate([packed[:, 0:64], packed[:, 64:128]], axis=0)

    def middle_rows(r):
        received(at_copies[r])
        total = TOK[r] + obias
        for b in range(BLK_SIZE):
            block = AR[r, b]
            total = total + dot_nn(head_zero(block), WO[192 * b : 192 * b + 64, :])
            total = total + dot_nn(block[0:128], WO[192 * b + 64 : 192 * (b + 1), :])
        MID[r] = total
        unit, inverse = stats(total)
        U2[r] = unit
        I2[r] = inverse
        N2[r, blk] = (unit * gain2 + shift2).astype(BF)
        return gather_start(N2, r)

    n2_part = [middle_rows(0)]
    step_three(u_part)
    n2_part.append(middle_rows(1))
    step_two(d_part)
    gather_forward(gr_part[1])
    dp_end(u_part)
    for n in range(CHUNKS):
        compact(lambda i: WUS[n, i], WU.at[n])
    gather_forward(n2_part[0])
    step_three(d_part)
    gather_end(n2_part[0])

    def rows_of(buf, r):
        return buf[r].reshape(512, 768)

    def up(r):
        for n in range(CHUNKS):
            cols = slice(WIDE * n, WIDE * (n + 1))
            hidden = dot_nn(rows_of(N2, r), WU[n]) + PV[15:16, cols]
            square = hidden * hidden
            bent = jnp.tanh(hidden * (0.7978845608028654 + 0.035677408136300125 * square))
            half = 0.5 * (1.0 + bent)
            ACT[r, :, cols] = (hidden * half).astype(BF)
            slope = 0.3989422804014327 + 0.05351611220445019 * square
            GP[r, :, cols] = (half + hidden * (1.0 - bent * bent) * slope).astype(BF)

    def hidden_back(r):
        for n in range(2):
            cols = slice(384 * n, 384 * (n + 1))
            weight = jnp.concatenate(
                [WDS[m, 4 * n : 4 * (n + 1)].reshape(384, WIDE) for m in range(CHUNKS)], axis=1
            )
            grad = dot_nt(rows_of(GR, r), weight)
            grad = (grad * GP[r, :, cols].astype(F32)).astype(BF)
            GH[r, :, cols] = grad
            UBS[r, :, cols] = jnp.sum(grad.astype(F32), axis=0, keepdims=True)

    def sum_store(i, r, cols, values):
        PT[i, r, :, :, :, cols] = values.reshape(2, 2, 128, values.shape[-1]).astype(BF)

    def sum_start(i, r):
        sems = group()
        send(PT.at[i, r, :, 1 - c], RC.at[i, r], core_peer, sems)
        later_sent((sems, RC.at[i, r]))
        return sems, RC.at[i, r]

    def sum_middle(i, r, first):
        received(first)
        SX[i, r] = (PT[i, r, 1 - x, c].astype(F32) + RC[i, r, 1 - x].astype(F32)).astype(BF)
        sems = group()
        send(SX.at[i, r], RX.at[i, r], x_peer, sems)
        later_sent((sems, RX.at[i, r]))
        return sems, RX.at[i, r]

    def sum_end(i, r, second):
        received(second)
        return PT[i, r, x, c].astype(F32) + RC[i, r, x].astype(F32) + RX[i, r].astype(F32)

    def second_back(r):
        for n in range(3):
            cols = slice(256 * n, 256 * (n + 1))
            weight = jnp.concatenate([WU[m, cols, :] for m in range(CHUNKS)], axis=1)
            sum_store(0, r, cols, dot_nt(GH[r], weight))
        return sum_start(0, r)

    def first_back(r):
        for n in range(3):
            cols = slice(256 * n, 256 * (n + 1))
            sum_store(
                2, r, cols, dot_nt(GJ0[r], WJ0[cols, :]) + dot_nt(GJ1[r], WJ1[cols, :])
            )
        return sum_start(2, r)

    def down(r):
        for n in range(CHUNKS):
            cols = slice(WIDE * n, WIDE * (n + 1))
            sum_store(1, r, cols, dot_nn(ACT[r], WDS[n].reshape(768, WIDE)))
        return sum_start(1, r)

    def scatter_start(parts, recv):
        sems = group()
        send(parts.at[:, 1 - y], recv, y_peer, sems)
        later_sent((sems, recv))
        return sems, recv

    def scatter_middle(parts, recv, sums, landing, first):
        received(first)
        sums[...] = (parts[:, y].astype(F32) + recv[...].astype(F32)).astype(BF)
        sems = group()
        for k in range(1, Z_SIZE):
            send(sums.at[z_at(k)], landing.at[k - 1], (2 * z_at(k) + y, blk), sems)
        later_sent((sems, landing))
        return sums, landing, (sems, landing)

    def scatter_end(sums, landing, second):
        received(second)
        total = sums[z].astype(F32)
        for k in range(Z_SIZE - 1):
            total = total + landing[k].astype(F32)
        return total

    def return_columns(part, sends, recvs):
        sends[...] = scatter_end(*part).astype(BF)
        recvs[blk] = sends[blk]
        return swap_parts(lambda b: sends.at[b], recvs)

    def down_grad(n):
        grads = GR[:, :, :, WIDE * n : WIDE * (n + 1)].reshape(1024, WIDE)
        for m in range(2):
            cols = slice(384 * m, 384 * (m + 1))
            grad = dot_tn(ACT[:, :, cols].reshape(1024, 384), grads)
            GD[n, 2 * m : 2 * m + 2] = grad.reshape(2, 2, 96, WIDE).astype(BF)

    def row_grad(rows, grads, parts):
        for m in range(2):
            cols = slice(384 * m, 384 * (m + 1))
            grad = dot_tn(rows[:, :, :, cols].reshape(1024, 384), grads)
            parts[2 * m : 2 * m + 2] = grad.reshape(2, 2, 4, 24, grad.shape[-1]).astype(BF)

    def up_grad(n):
        row_grad(N2, GH[:, :, WIDE * n : WIDE * (n + 1)].reshape(1024, WIDE), GU.at[n])

    def joint_grad_one():
        for m in range(2):
            rows = N1[:, :, :, 384 * m : 384 * (m + 1)].reshape(1024, 384)
            grad = dot_tn(rows, GJ0[...].reshape(1024, 192)).reshape(2, 2, 4, 24, 192).astype(BF)
            for p in range(2):
                GA[2 * m : 2 * m + 2, :, p, :, 0:192] = grad[:, :, 2 * p]
                GA[2 * m : 2 * m + 2, :, p, :, 192:384] = grad[:, :, 2 * p + 1]
        return scatter_start(GA, RYa)

    def joint_grad_two():
        row_grad(N1, GJ1[...].reshape(1024, 384), GC)
        return scatter_start(GC, RYc)

    def output_grad():
        for b in range(BLK_SIZE):
            blocks = [AR[r, b] for r in range(2)]
            zero = jnp.concatenate([head_zero(block) for block in blocks], axis=0)
            rest = jnp.concatenate([block[0:128] for block in blocks], axis=0)
            grads = GB[...].reshape(256, 768)
            grad = jnp.concatenate([dot_tn(zero, grads), dot_tn(rest, grads)], axis=0)
            grad = grad.reshape(2, 4, 24, 768).astype(BF)
            for i in range(4):
                GO[i // 2, i % 2, 2 * b : 2 * b + 2] = grad[:, i]
        sems = group()
        send(GO.at[:, 1 - c], RCo, core_peer, sems)
        later_sent((sems, RCo))
        return sems, RCo

    def output_grad_middle(first):
        received(first)
        SXo[...] = (GO[1 - x, c].astype(F32) + RCo[1 - x].astype(F32)).astype(BF)
        sems = group()
        send(SXo, RXo, x_peer, sems)
        later_sent((sems, RXo))
        return sems, RXo

    def norm_back(e, unit, inverse, gain):
        f = e * gain
        grad = inverse * (
            f - jnp.mean(f, axis=-1, keepdims=True)
            - unit * jnp.mean(f * unit, axis=-1, keepdims=True)
        )
        return (
            grad, jnp.sum(e * unit, axis=0, keepdims=True), jnp.sum(e, axis=0, keepdims=True)
        )

    def second_norm_back(r, second):
        e = sum_end(0, r, second)
        grad, of_gain, of_shift = norm_back(e, U2[r], I2[r], gain2)
        grad = grad + COT[r]
        GM[r] = grad
        low = grad.astype(BF)
        GB[r] = low
        for b in range(BLK_SIZE):
            zero = dot_nt(low, WO[192 * b : 192 * b + 64, :]).astype(BF)
            DA[r, b, 128:192, 0:64] = zero[0:64]
            DA[r, b, 128:192, 64:128] = zero[64:128]
            DA[r, b, 0:128] = dot_nt(low, WO[192 * b + 64 : 192 * (b + 1), :]).astype(BF)
        copies = swap_heads(DA, DR, r)
        VS[3:4] += of_gain
        VS[4:5] += of_shift
        VS[2:3] += jnp.sum(low.astype(F32), axis=0, keepdims=True)
        VS[5:6] += jnp.sum(COT[r].astype(BF).astype(F32), axis=0, keepdims=True)
        return copies

    def attend_back(r, h):
        if h:
            DOH[...] = DR[r, :, 0:128, 64 * (h - 1) : 64 * h].reshape(512, 64)
        else:
            for t in range(4):
                DOH[128 * t : 128 * t + 64] = DR[r, t, 128:192, 0:64]
                DOH[128 * t + 64 : 128 * (t + 1)] = DR[r, t, 128:192, 64:128]
        grad_out = DOH[...]
        delta = jnp.sum(grad_out.astype(F32) * OF[r, h], axis=-1, keepdims=True)
        grad_probs = dot_nt(grad_out, V[r, h])
        grad_scores = (PB[r, h].astype(F32) * (grad_probs - delta)).astype(BF)
        grads = (
            (dot_nn(grad_scores, K[r, h]) * 0.125).astype(BF),
            dot_tn(grad_scores, Q[r, h]).astype(BF),
            dot_tn(PB[r, h], grad_out).astype(BF),
        )
        for s, grad in enumerate(grads):
            if h == 0:
                GJ0[r, :, 64 * s : 64 * (s + 1)] = grad
            else:
                at = 128 * s + 64 * (h - 1)
                GJ1[r, :, at : at + 64] = grad

    def z_first_start(parts, landing):
        sems = group()
        for k in range(1, Z_SIZE):
            send(parts.at[z_at(k)], landing.at[k - 1], (2 * z_at(k) + y, blk), sems)
        later_sent((sems, landing))
        return sems, landing

    def z_first_middle(parts, landing, sums, recv, first):
        received(first)
        total = parts[z].astype(F32)
        for k in range(Z_SIZE - 1):
            total = total + landing[k].astype(F32)
        sums[...] = total.astype(BF)
        sems = group()
        send(sums.at[1 - y], recv, y_peer, sems)
        later_sent((sems, recv))
        return sems, recv

    def z_first_end(sums, recv, second):
        received(second)
        return sums[y].astype(F32) + recv[...].astype(F32)

    def output_grad_over_dp(second):
        received(second)
        GO2[...] = (
            GO[x, c].astype(F32) + RCo[x].astype(F32) + RXo[...].astype(F32)
        ).astype(BF).reshape(4, 2, 24, 768)
        return scatter_start(GO2, RYo)

    def vector_sums():
        for r in range(2):
            JBS[r, :, 0:192] = jnp.sum(GJ0[r].astype(F32), axis=0, keepdims=True)
            JBS[r, :, 192:576] = jnp.sum(GJ1[r].astype(F32), axis=0, keepdims=True)

    def first_norm_back(r, second):
        e = sum_end(2, r, second)
        grad, of_gain, of_shift = norm_back(e, U1[r], I1[r], gain1)
        GM[r] = GM[r] + grad
        VS[0:1] += of_gain
        VS[1:2] += of_shift

    VS[...] = jnp.zeros_like(VS)
    d_first, d_second, u_grad_first, u_grad_second = [], [], [], []

    def d_over_y(n):
        d_first.append(scatter_start(GD.at[n], RYd.at[n]))

    def d_over_z(n):
        d_second.append(scatter_middle(GD.at[n], RYd.at[n], Sd.at[n], RZd.at[n], d_first[n]))

    def u_over_y(n):
        u_grad_first.append(scatter_start(GU.at[n], RYu.at[n]))

    def u_over_z(n):
        u_grad_second.append(
            scatter_middle(GU.at[n], RYu.at[n], Su.at[n], RZu.at[n], u_grad_first[n])
        )

    up(0)
    gather_forward(n2_part[1])
    gather_end(gr_part[0])
    gather_end(gr_part[1])
    gather_end(n2_part[1])
    up(1)
    down_grad(0)
    d_near_first = z_first_start(GD.at[0], RZ0)
    d_first.append(None)
    d_second.append(None)
    down_grad(1)
    d_over_y(1)
    dp_end(d_part)
    hidden_back(0)
    second_first = [second_back(0)]
    down_grad(2)
    d_over_y(2)
    hidden_back(1)
    second_second = [sum_middle(0, 0, second_first[0])]
    second_first.append(second_back(1))
    up_grad(0)
    u_over_y(0)
    second_second.append(sum_middle(0, 1, second_first[1]))
    up_grad(1)
    u_over_y(1)
    d_over_z(1)
    up_grad(2)
    u_over_y(2)
    da_copies = [second_norm_back(0, second_second[0])]
    d_over_z(2)
    result_first = [down(0), down(1)]
    da_copies.append(second_norm_back(1, second_second[1]))
    o_first = output_grad()
    received(da_copies[0])
    attend_back(0, 1)
    o_second = output_grad_middle(o_first)
    u_over_z(0)
    attend_back(0, 2)
    d_near_second = z_first_middle(GD.at[0], RZ0, S0, RY0, d_near_first)
    received(da_copies[1])
    attend_back(1, 1)
    attend_back(1, 2)
    c_grad_first = joint_grad_two()
    u_over_z(1)
    attend_back(0, 0)
    first_first = [first_back(0)]
    attend_back(1, 0)
    u_over_z(2)
    a_grad_first = joint_grad_one()
    first_second = [sum_middle(2, 0, first_first[0])]
    first_first.append(first_back(1))
    o_grad_first = output_grad_over_dp(o_second)
    first_second.append(sum_middle(2, 1, first_first[1]))
    result_second = [sum_middle(1, 0, result_first[0])]
    vector_sums()

    def down_out():
        OD[:, 0:WIDE] = z_first_end(S0, RY0, d_near_second)
        for n in range(1, CHUNKS):
            OD[:, WIDE * n : WIDE * (n + 1)] = scatter_end(*d_second[n])

    row = lax.broadcasted_iota(jnp.int32, (8, 1), 0)

    def picked(values, mask, placer):
        wide = jnp.where(mask, values[None], 0.0)
        wide = wide.reshape(256, wide.shape[-1])
        high = wide.astype(BF)
        rest = (wide - high.astype(F32)).astype(BF)
        return dot_nt(high, placer) + dot_nt(rest, placer)

    def vectors_early():
        joint = JBS[0] + JBS[1]
        queries = jnp.concatenate([joint[:, 0:64], joint[:, 192:320]], axis=1)
        values = jnp.concatenate([joint[:, 128:192], joint[:, 448:576]], axis=1)
        pieces = picked(jnp.where(row == 7, UBS[0] + UBS[1], 0.0), mask96(), place96())
        pieces += picked(jnp.where(row == 6, queries, 0.0), mask48(0.0), place48())
        pieces += picked(jnp.where(row == 6, values, 0.0), mask48(16.0), place48())
        TS[...] = pieces

    def vectors_over_blk():
        pieces = (TS[...] + picked(VS[...], mask24(), place24())).reshape(8, 4, 8, 128)
        for b in range(BLK_SIZE):
            TB[b] = pieces[:, b]
        TL[blk] = TB[blk]
        return swap_parts(lambda b: TB.at[b], TL)

    def vectors_over_dp(first):
        received(first)
        TY[...] = (TL[0] + TL[1]) + (TL[2] + TL[3])
        sems = group()
        for k in range(1, DP_SIZE):
            to = (dp + k) % DP_SIZE
            send(TY.at[to], TV.at[k - 1], (to, blk), sems)
        later_sent((sems, TV))
        return sems, TV

    def vectors_end(first):
        received(first)
        OS[...] = TY[dp] + jnp.sum(TV[...], axis=0)

    def return_head_zero():
        total = scatter_end(*a_grad_second).astype(BF)
        for p in range(2):
            AAs[2 * p] = total[p][:, 0:192]
            AAs[2 * p + 1] = total[p][:, 192:384]
        AAr[blk] = AAs[blk]
        return swap_parts(lambda b: AAs.at[b], AAr)

    def up_out():
        for part in u_back:
            received(part)
        for b in range(BLK_SIZE):
            whole = jnp.concatenate([AUr[n, b] for n in range(CHUNKS)], axis=1).astype(F32)
            for i in range(DP_SIZE):
                at = 96 * (BLK_SIZE * i + b)
                OU[:, at : at + 96] = whole[:, 96 * i : 96 * (i + 1)]

    def joint_out():
        received(c_back)
        received(a_back)
        for b in range(BLK_SIZE):
            one, two = AAr[b].astype(F32), ACr[b].astype(F32)
            for s in range(3):
                at = 768 * s + 192 * b
                OJ[:, at : at + 64] = one[:, 64 * s : 64 * (s + 1)]
                OJ[:, at + 64 : at + 192] = two[:, 128 * s : 128 * (s + 1)]

    def result_end():
        for r in range(2):
            MID[r] = MID[r] + sum_end(1, r, result_second[r]) + dbias

    vectors_early()
    c_grad_second = scatter_middle(GC, RYc, Sc, RZc, c_grad_first)
    first_norm_back(0, first_second[0])
    a_grad_second = scatter_middle(GA, RYa, Sa, RZa, a_grad_first)
    first_norm_back(1, first_second[1])
    o_grad_second = scatter_middle(GO2, RYo, So, RZo, o_grad_first)
    vector_part = vectors_over_blk()
    u_back = [return_columns(u_grad_second[n], AUs.at[n], AUr.at[n]) for n in range(CHUNKS)]
    result_second.append(sum_middle(1, 1, result_first[1]))
    vector_part = vectors_over_dp(vector_part)
    c_back = return_columns(c_grad_second, ACs, ACr)
    down_out()
    a_back = return_head_zero()
    up_out()
    vectors_end(vector_part)
    OO[...] = scatter_end(*o_grad_second)
    result_end()
    joint_out()
    assert (count[0], count[2], count[1]) == (SENDS, RECEIVES, LOCALS), count
    for copies in started:
        sent(copies)

    @pl.when(inner)
    def _():
        for sems, _, five in started_over_z:
            sent((sems, five))

    @pl.when(jnp.logical_not(inner))
    def _():
        for sems, one, _ in started_over_z:
            sent((sems, one))


def finish_kernel(*refs):
    big_in, sums, big_out, small_out, sems = refs[:6], refs[6], refs[7:13], refs[13:21], refs[21]
    copies = []
    for n, (source, target) in enumerate(zip(big_in, big_out)):
        made = pltpu.make_async_copy(source, target, sems.at[n])
        made.start()
        copies.append(made)
    for row, width in enumerate(TILE_WIDTHS):
        small_out[row][...] = sums[row, 0:width]
    for made in copies:
        made.wait()


def fast_device(
    tokens, segment_ids, pad_mask, joint_weight, joint_bias, output_weight, output_bias,
    first_gain, first_shift, up_weight, up_bias, down_weight, down_bias,
    second_gain, second_shift, cotangent,
):
    vectors = (
        first_gain, first_shift, output_bias, second_gain, second_shift, down_bias,
        joint_bias, up_bias,
    )

    def vm(*shape, dtype=BF):
        return pltpu.VMEM(shape, dtype)

    def fm(*shape):
        return pltpu.VMEM(shape, F32)

    scratch = [
        fm(2, 128, 768), fm(2, 128, 768), vm(24, 2304), vm(24, 3072), vm(96, 768),
        vm(4, 24, 192), vm(4, 24, 384), vm(4, 24, 768), vm(CHUNKS, 4, 24, WIDE), vm(4, 24, 192), fm(8, 128), fm(8, 128), fm(8, 4, 8, 128),
        fm(4, 8, 128), fm(8, 512), fm(512, 8), fm(16, 768), fm(16, 192),
        vm(2, 4, 128, 768), vm(2, 4, 128, 768), vm(2, 4, 128, 768),
        vm(8, 2, 24, 384), vm(8, 4, 24, 384), vm(CHUNKS, 8, 4, 24, WIDE), vm(CHUNKS, 8, 96, WIDE),
        vm(4, 8, 24, 768), vm(768, 192), vm(768, 384), vm(CHUNKS, 768, WIDE), vm(768, 768),
        fm(2, 128, 768), fm(2, 128, 1), fm(2, 128, 768), fm(2, 128, 1),
        vm(2, 128, 768),
        vm(2, 3, 512, 64), vm(2, 3, 512, 64), vm(2, 3, 512, 64), vm(2, 3, 512, 512),
        fm(2, 3, 512, 64), vm(2, 4, 192, 128), vm(2, 4, 192, 128),
        vm(2, 4, 192, 128), vm(2, 4, 192, 128), vm(512, 64), vm(2, 512, 192), vm(2, 512, 384),
        vm(2, 512, 768), vm(2, 512, 768), vm(2, 512, 768), fm(2, 1, 768),
        vm(3, 2, 2, 2, 128, 768), vm(3, 2, 2, 128, 768), vm(3, 2, 128, 768), vm(3, 2, 128, 768),
        vm(CHUNKS, 4, 2, 96, WIDE), vm(CHUNKS, 4, 2, 4, 24, WIDE), vm(4, 2, 2, 24, 384), vm(4, 2, 4, 24, 384),
        vm(2, 2, 8, 24, 768), vm(4, 2, 24, 768),
        vm(CHUNKS, 4, 96, WIDE), vm(CHUNKS, 4, 4, 24, WIDE), vm(4, 2, 24, 384), vm(4, 4, 24, 384), vm(4, 24, 768),
        vm(CHUNKS, 4, 96, WIDE), vm(CHUNKS, 4, 4, 24, WIDE), vm(4, 2, 24, 384), vm(4, 4, 24, 384), vm(4, 24, 768),
        vm(CHUNKS, 3, 96, WIDE), vm(CHUNKS, 3, 4, 24, WIDE), vm(3, 2, 24, 384), vm(3, 4, 24, 384), vm(3, 24, 768),
        vm(3, 2, 96, WIDE), vm(2, 96, WIDE), vm(96, WIDE),
        vm(CHUNKS, 4, 24, WIDE), vm(CHUNKS, 4, 24, WIDE), vm(4, 24, 192), vm(4, 24, 192),
        vm(4, 24, 384), vm(4, 24, 384), vm(2, 8, 24, 768), vm(8, 24, 768), vm(8, 24, 768),
        fm(256, 128), fm(4, 8, 8, 128), fm(4, 8, 8, 128), fm(8, 8, 128), fm(7, 8, 128),
        fm(8, 768), fm(2, 1, 576),
        pltpu.SemaphoreType.DMA((SENDS,)), pltpu.SemaphoreType.DMA((RECEIVES,)),
        pltpu.SemaphoreType.DMA((LOCALS,)),
    ]
    vmem = pl.BlockSpec(memory_space=pltpu.VMEM)
    anywhere = pl.BlockSpec(memory_space=pl.ANY)
    big = [(2, 128, 768), (2, 128, 768), (24, 2304), (24, 768), (24, 3072), (96, 768)]
    made = pl.pallas_call(
        layer_kernel,
        out_shape=[fm(*shape) for shape in big] + [fm(8, 128)],
        in_specs=[anywhere] * 2 + [vmem] * 2 + [anywhere] * 4 + [vmem] * 8,
        out_specs=[vmem] * 7,
        scratch_shapes=scratch,
        compiler_params=pltpu.CompilerParams(
            collective_id=0, has_side_effects=True, vmem_limit_bytes=VMEM_MIB * 2**20
        ),
        cost_estimate=pl.CostEstimate(
            flops=13 * 10**9, bytes_accessed=6 * 10**6, transcendentals=4 * 10**6
        ),
    )(
        tokens, cotangent, segment_ids, pad_mask, joint_weight, up_weight, down_weight,
        output_weight, *vectors,
    )
    ends = pl.pallas_call(
        finish_kernel,
        out_shape=[jax.ShapeDtypeStruct(shape, F32) for shape in big]
        + [jax.ShapeDtypeStruct((width,), F32) for width in TILE_WIDTHS],
        in_specs=[vmem] * 7,
        out_specs=[anywhere] * 6 + [vmem] * 8,
        scratch_shapes=[pltpu.SemaphoreType.DMA((6,))],
    )(*(pltpu.with_memory_space_constraint(array, pltpu.VMEM) for array in made))
    result, grad_tokens, grad_j, grad_o, grad_u, grad_d = ends[:6]
    first_g, first_s, output_b, second_g, second_s, down_b, joint_b, up_b = ends[6:]
    return (
        result, grad_tokens, grad_j, joint_b, grad_o, output_b, first_g, first_s,
        grad_u, up_b, grad_d, down_b, second_g, second_s,
    )


def solution(mesh):
    placed = (
        P("dp", "blk", None),
        P("dp", "blk"),
        P("dp", "blk"),
        P(("dp", "blk"), None),
        P(("dp", "blk")),
        P(("dp", "blk"), None),
        P(("dp", "blk")),
        P(("dp", "blk")),
        P(("dp", "blk")),
        P(("dp", "blk"), None),
        P(("dp", "blk")),
        P(("dp", "blk"), None),
        P(("dp", "blk")),
        P(("dp", "blk")),
        P(("dp", "blk")),
        P("dp", "blk", None),
    )

    def spread(device_part):
        return jax.shard_map(
            device_part,
            mesh=mesh,
            in_specs=placed,
            out_specs=(
                P("dp", "blk", None),
                P("dp", "blk", None),
                P(("dp", "blk"), None),
                P(("dp", "blk")),
                P(("dp", "blk"), None),
                P(("dp", "blk")),
                P(("dp", "blk")),
                P(("dp", "blk")),
                P(("dp", "blk"), None),
                P(("dp", "blk")),
                P(("dp", "blk"), None),
                P(("dp", "blk")),
                P(("dp", "blk")),
                P(("dp", "blk")),
            ),
            check_vma=False,
        )

    def layer(*arrays):
        rows, length, features = arrays[0].shape
        shape = dict(mesh.shape)
        fits = (
            shape == {"dp": DP_SIZE, "blk": BLK_SIZE}
            and (rows, length, features) == (2 * shape["dp"], 512, 768)
            and arrays[9].shape[1] == 3072
        )
        return spread(fast_device if fits else per_device)(*arrays)

    return layer
```
